256 devices in a mesh: date: 16 (over z, core), row: 4 (over x), col: 4 (over y).
Axes of the slice: x: 4, y: 4, z: 8, core: 2. Of those that a mesh axis runs over, the one named last changes fastest.
Arguments:
- stack: float32 [64, 2, 320, 2560], P('date', None, 'row', 'col'), may hold values from -20 to 20
- pair_list: int32 [64, 2], replicated, may hold values from 0 to 63, as said below
Outputs:
- filtered: float32 [64, 2, 64, 128], P('date', None, 'row', 'col')
- coherence: float32 [64, 64, 128], P('date', 'row', 'col')
The draws below stay inside these ranges and needn't reach their ends.
Inputs may be any that keep to these rules, and one draw needn't show every extreme that they name: `pair_list`: reference and secondary of each pair; the reference of rows d*4 to (d+1)*4 - 1 is one of acquisitions d*4 to (d+1)*4 - 1, and the secondary lies 1 to 3 acquisitions after it.
All inputs are finite; a program needn't handle non-finite values.
Results may differ from the reference program's by a relative error of at most 0.0003.
Values sent between devices are 32-bit elements; how exact they have to be, the bound alone decides.
No kernel may reach another device: no remote copies, remote signals or barrier semaphores. Data moves between devices by JAX's collectives and lax.ppermute only.
A program may use at most 64 MiB of HBM per device.

```python
import math
import jax
import jax.numpy as jnp
from jax import lax

A_DEV = 4
SPAN = 3
LOOK_R = 5
LOOK_C = 20
PATCH = 32
ACQ = 64
PAIRS = 64
ROWS = 320
COLS = 2560


def draw_stack(key, part):
    key = jax.random.fold_in(key, 3)
    key_common, key_noise, key_scale = jax.random.split(key, 3)
    common = jax.random.normal(key_common, (2, ROWS, COLS), jnp.float32)
    noise = jax.random.normal(key_noise, (ACQ, 2, ROWS, COLS), jnp.float32)
    scales = 1.0 + 0.0 * jax.random.uniform(key_scale, (ACQ, 1, 1, 1), jnp.float32)
    values = (0.8 * common[None] + 0.6 * noise) * scales
    return jnp.clip(values, -20.0, 20.0).astype(jnp.float32)


def draw_pair_list(key, part):
    key = jax.random.fold_in(key, 7)
    key_ref, key_step = jax.random.split(key)
    groups = ACQ // A_DEV
    rows_all = jnp.arange(PAIRS, dtype=jnp.int32)
    group_of = rows_all // A_DEV
    final_group = group_of == groups - 1
    upper = jnp.where(final_group, A_DEV - 1, A_DEV).astype(jnp.int32)
    offset_ref = jax.random.randint(key_ref, (PAIRS,), 0, upper, dtype=jnp.int32)
    reference_index = group_of * A_DEV + offset_ref
    step_size = jax.random.randint(key_step, (PAIRS,), 1, SPAN + 1, dtype=jnp.int32)
    secondary_index = jnp.minimum(reference_index + step_size, ACQ - 1)
    edge_rows = (rows_all % A_DEV == 0) & jnp.logical_not(final_group)
    reference_index = jnp.where(edge_rows, group_of * A_DEV + A_DEV - 1, reference_index)
    secondary_index = jnp.where(edge_rows, reference_index + SPAN, secondary_index)
    return jnp.stack([reference_index, secondary_index], axis=1).astype(jnp.int32)


def setup_inputs(seed: int = 0) -> dict:
    key_of = jax.random.split(jax.random.key(seed), 3)
    stack = draw_stack(jax.random.fold_in(key_of[2], 71), 0)
    pair_list = draw_pair_list(jax.random.fold_in(key_of[2], 71), 0)
    return {"stack": stack, "pair_list": pair_list}


def look_means(values):
    pair_total = values.shape[0]
    row_total = values.shape[1]
    col_total = values.shape[2]
    shaped = values.reshape(pair_total, row_total // LOOK_R, LOOK_R, col_total // LOOK_C, LOOK_C)
    return shaped.mean(axis=(2, 4))

def multilook(primary, secondary):
    cross_real = primary[:, 0] * secondary[:, 0] + primary[:, 1] * secondary[:, 1]
    cross_imag = primary[:, 1] * secondary[:, 0] - primary[:, 0] * secondary[:, 1]
    power_primary = primary[:, 0] * primary[:, 0] + primary[:, 1] * primary[:, 1]
    power_secondary = secondary[:, 0] * secondary[:, 0] + secondary[:, 1] * secondary[:, 1]
    look_real = look_means(cross_real)
    look_imag = look_means(cross_imag)
    mean_primary = look_means(power_primary)
    mean_secondary = look_means(power_secondary)
    magnitude = jnp.sqrt(look_real * look_real + look_imag * look_imag)
    coherence = magnitude / jnp.sqrt((mean_primary + 1e-06) * (mean_secondary + 1e-06))
    return (jnp.stack([look_real, look_imag], axis=1), coherence)

def transform_tables():
    indices = jnp.arange(PATCH, dtype=jnp.int32)
    phases = indices[:, None] * indices[None, :] % PATCH
    angles = phases.astype(jnp.float32) * (2.0 * math.pi / PATCH)
    return (jnp.cos(angles), jnp.sin(angles))

def along_first(matrix, values):
    return jnp.einsum('ku,niujv->nikjv', matrix, values, precision=lax.Precision.HIGHEST)

def along_second(matrix, values):
    return jnp.einsum('lv,niujv->niujl', matrix, values, precision=lax.Precision.HIGHEST)

def goldstein(extended):
    pair_total = extended.shape[0]
    half_patch = PATCH // 2
    blocks_down = extended.shape[2] // half_patch
    blocks_across = extended.shape[3] // half_patch
    blocks = extended.reshape(pair_total, 2, blocks_down, half_patch, blocks_across, half_patch)
    tall_pairs = jnp.concatenate([blocks[:, :, :-1], blocks[:, :, 1:]], axis=3)
    patches = jnp.concatenate([tall_pairs[:, :, :, :, :-1], tall_pairs[:, :, :, :, 1:]], axis=5)
    cosine, sine = transform_tables()
    real_in = patches[:, 0]
    imag_in = patches[:, 1]
    step_real = along_first(cosine, real_in) + along_first(sine, imag_in)
    step_imag = along_first(cosine, imag_in) - along_first(sine, real_in)
    spec_real = along_second(cosine, step_real) + along_second(sine, step_imag)
    spec_imag = along_second(cosine, step_imag) - along_second(sine, step_real)
    magnitude = jnp.sqrt(spec_real * spec_real + spec_imag * spec_imag)
    smooth = jnp.zeros_like(magnitude)
    for shift_down in (-1, 0, 1):
        for shift_across in (-1, 0, 1):
            smooth = smooth + jnp.roll(magnitude, (shift_down, shift_across), axis=(2, 4))
    response = jnp.sqrt(smooth / 9.0) / PATCH
    filt_real = spec_real * response
    filt_imag = spec_imag * response
    back_real = along_first(cosine, filt_real) - along_first(sine, filt_imag)
    back_imag = along_first(cosine, filt_imag) + along_first(sine, filt_real)
    out_real = along_second(cosine, back_real) - along_second(sine, back_imag)
    out_imag = along_second(cosine, back_imag) + along_second(sine, back_real)
    position = jnp.arange(PATCH, dtype=jnp.float32)
    taper_weights = jnp.where(position < half_patch, (position + 0.5) / half_patch, (PATCH - 0.5 - position) / half_patch)
    window = taper_weights[:, None, None] * taper_weights[None, None, :] / (PATCH * PATCH)

    def assemble(component):
        weighted = component * window
        down_sum = weighted[:, 1:, :half_patch] + weighted[:, :-1, half_patch:]
        assembled = down_sum[:, :, :, 1:, :half_patch] + down_sum[:, :, :, :-1, half_patch:]
        shape_now = assembled.shape
        return assembled.reshape(shape_now[0], shape_now[1] * shape_now[2], shape_now[3] * shape_now[4])
    return jnp.stack([assemble(out_real), assemble(out_imag)], axis=1)

def reference(stack, pair_list):

    def one_pair(indices):
        primary = lax.dynamic_slice_in_dim(stack, indices[0], 1, 0)
        secondary = lax.dynamic_slice_in_dim(stack, indices[1], 1, 0)
        look_pair, coherence = multilook(primary, secondary)
        return (look_pair[0], coherence[0])
    looked, coherence = lax.map(one_pair, pair_list)
    margin = PATCH // 2
    padded = jnp.pad(looked, ((0, 0), (0, 0), (margin, margin), (margin, margin)))

    def filter_one(single):
        return goldstein(single[None])[0]
    filtered = lax.map(filter_one, padded)
    return (filtered, coherence)
```

```python
import functools
import math

import jax
import jax.numpy as jnp
import numpy as np
from jax import lax
from jax.experimental import pallas as pl
from jax.experimental.pallas import tpu as pltpu
from jax.sharding import PartitionSpec as P

SPAN = 3
LOOK_R = 5
LOOK_C = 20
PATCH = 32
HALF = PATCH // 2
PAIRS_DEV = 4
F32 = jnp.float32
BF16 = jnp.bfloat16


def split_const(matrix):
    hi = matrix.astype(jnp.bfloat16)
    lo = (matrix - hi.astype(np.float64)).astype(jnp.bfloat16)
    return hi, lo


def taper(v):
    return np.where(v < HALF, (v + 0.5) / HALF, (PATCH - 0.5 - v) / HALF)


def look_table():
    x = np.arange(640)[:, None] // LOOK_C
    n = np.arange(256)[None, :]
    return (x == (n // 128) * HALF + n % HALF).astype(np.float64)


def row_forward():
    i, k, q, row = np.meshgrid(np.arange(2), np.arange(PATCH), np.arange(2), np.arange(48), indexing="ij")
    u = row - HALF * i
    angle = 2 * np.pi * k * u / PATCH
    value = np.where(q == 0, np.cos(angle), -np.sin(angle)) * ((u >= 0) & (u < PATCH))
    return value.reshape(64, 96)


def col_forward():
    h, c, p, v, c2, p2, l = np.meshgrid(
        np.arange(2), np.arange(2), np.arange(4), np.arange(HALF), np.arange(2), np.arange(4), np.arange(PATCH),
        indexing="ij",
    )
    angle = 2 * np.pi * l * (HALF * h + v) / PATCH
    value = np.where(c == c2, np.cos(angle), np.where(c == 1, np.sin(angle), -np.sin(angle)))
    return (value * (p == p2)).reshape(256, 256)


def neighbour_sum():
    a = np.arange(128)[:, None]
    b = np.arange(128)[None, :]
    d = (a - b) % PATCH
    return ((a // PATCH == b // PATCH) & ((d <= 1) | (d == PATCH - 1))).astype(np.float64)


def row_back():
    c2, r, c, i, k = np.meshgrid(
        np.arange(2), np.arange(HALF), np.arange(2), np.arange(2), np.arange(PATCH), indexing="ij"
    )
    u = r + HALF * (1 - i)
    angle = 2 * np.pi * k * u / PATCH
    value = np.where(c == c2, np.cos(angle), np.where(c2 == 0, -np.sin(angle), np.sin(angle))) * taper(u)
    return value.reshape(32, 128)


def col_back():
    j, p, l, q, p2, c = np.meshgrid(
        np.arange(3), np.arange(4), np.arange(PATCH), np.arange(2), np.arange(4), np.arange(PATCH), indexing="ij"
    )
    v = c + HALF - HALF * j
    angle = 2 * np.pi * l * v / PATCH
    value = np.where(q == 0, np.cos(angle), np.sin(angle)) * taper(v) * ((v >= 0) & (v < PATCH)) * (p == p2)
    return (value / (PATCH * PATCH)).reshape(384, 256)


def split(x):
    hi = x.astype(BF16)
    return hi, (x - hi.astype(F32)).astype(BF16)


def mm(a, b):
    return jnp.dot(a, b, preferred_element_type=F32)


def looks_kernel(idx_ref, stack_ref, recv_ref, table_ref, left_ref, right_ref, coh_ref, held, sem):
    copies = []
    for t in range(5):
        lanes = pl.ds(128 * t, 128)
        copies.append(pltpu.make_async_copy(stack_ref.at[:, :, :, lanes], held.at[0:4, :, t], sem.at[0, t]))
        copies.append(pltpu.make_async_copy(recv_ref.at[:, :, :, lanes], held.at[4:7, :, t], sem.at[1, t]))
    for copy in copies:
        copy.start()
    for copy in copies:
        copy.wait()

    def rows(acq, comp, k):
        tiles = [held[acq, comp, t, pl.ds(k, 16, stride=LOOK_R), :] for t in range(5)]
        return jnp.concatenate(tiles, axis=1)

    planes = []
    for p in range(PAIRS_DEV):
        a = idx_ref[2 * p]
        b = idx_ref[2 * p + 1]
        real = imag = power_a = power_b = None
        for k in range(LOOK_R):
            ar, ai, br, bi = rows(a, 0, k), rows(a, 1, k), rows(b, 0, k), rows(b, 1, k)
            terms = (ar * br + ai * bi, ai * br - ar * bi, ar * ar + ai * ai, br * br + bi * bi)
            if k == 0:
                real, imag, power_a, power_b = terms
            else:
                real, imag, power_a, power_b = (
                    real + terms[0], imag + terms[1], power_a + terms[2], power_b + terms[3],
                )
        planes += [real, imag, power_a, power_b]
    total = jnp.concatenate(planes, axis=0)
    hi, rest = total.astype(BF16), None
    rest = total - hi.astype(F32)
    mid = rest.astype(BF16)
    low = (rest - mid.astype(F32)).astype(BF16)
    table = table_ref[...]
    cells = (mm(hi, table) + (mm(mid, table) + mm(low, table))) * (1.0 / (LOOK_R * LOOK_C))
    cells = cells.reshape(PAIRS_DEV, 4, 16, 256)
    lane = lax.broadcasted_iota(jnp.int32, (16, 128), 1)
    group = lane // HALF
    left = jnp.zeros((16, 128), F32)
    right = jnp.zeros((16, 128), F32)
    for p in range(PAIRS_DEV):
        for comp in range(2):
            here = group == comp * PAIRS_DEV + p
            left = jnp.where(here, cells[p, comp, :, :128], left)
            right = jnp.where(here, cells[p, comp, :, 128:], right)
        whole = jnp.where((lane < HALF)[None], cells[p, :, :, :128], cells[p, :, :, 128:])
        magnitude = jnp.sqrt(whole[0] * whole[0] + whole[1] * whole[1])
        coherence = magnitude / jnp.sqrt((whole[2] + 1e-06) * (whole[3] + 1e-06))
        coh_ref[p] = coherence[:, :PATCH]
    left_ref[...] = left
    right_ref[...] = right


def looks(idx, stack, recv):
    table = jnp.asarray(look_table().astype(jnp.bfloat16))
    return pl.pallas_call(
        looks_kernel,
        out_shape=(
            jax.ShapeDtypeStruct((16, 128), F32),
            jax.ShapeDtypeStruct((16, 128), F32),
            jax.ShapeDtypeStruct((PAIRS_DEV, 16, 32), F32),
        ),
        in_specs=[
            pl.BlockSpec(memory_space=pltpu.SMEM),
            pl.BlockSpec(memory_space=pl.ANY),
            pl.BlockSpec(memory_space=pl.ANY),
            pl.BlockSpec(memory_space=pltpu.VMEM),
        ],
        out_specs=[pl.BlockSpec(memory_space=pltpu.VMEM)] * 3,
        scratch_shapes=[pltpu.VMEM((7, 2, 5, 80, 128), F32), pltpu.SemaphoreType.DMA((2, 5))],
        compiler_params=pltpu.CompilerParams(vmem_limit_bytes=24 * 2**20),
    )(idx, stack, recv, table)


def goldstein_kernel(
    edge_ref, up_ref, mid_ref, down_ref, rf_ref, cf_ref, ns_ref, rb_ref, cb_ref, out_ref
):
    up = jnp.where(edge_ref[0] == 0, 0.0, up_ref[...])
    down = jnp.where(edge_ref[1] == 0, 0.0, down_ref[...])
    x = jnp.concatenate([up, mid_ref[...], down], axis=0)
    lane = lax.broadcasted_iota(jnp.int32, (48, 128), 1)
    sign = jnp.where(lane < 64, -1.0, 1.0)
    turned = [pltpu.roll(x[:, 128 * b : 128 * b + 128], 64, 1) * sign for b in range(4)]
    xx = jnp.concatenate([x, jnp.concatenate(turned, axis=1)], axis=0)
    xh, xl = split(xx)
    rh, rl = rf_ref[0], rf_ref[1]
    y = mm(rh, xh) + (mm(rh, xl) + mm(rl, xh))
    ys = jnp.concatenate([y[:, 128 * j : 128 * j + 256] for j in range(3)], axis=0)
    yh, yl = split(ys)
    ch, cl = cf_ref[0], cf_ref[1]
    z = mm(yh, ch) + (mm(yl, ch) + mm(yh, cl))
    zr, zi = z[:, :128], z[:, 128:]
    magnitude = jnp.sqrt(zr * zr + zi * zi)
    mh, ml = split(magnitude)
    across = mm(mh, ns_ref[...]) + mm(ml, ns_ref[...])
    grouped = across.reshape(6, PATCH, 128)
    down_one = jnp.concatenate([grouped[:, PATCH - 1 :], grouped[:, : PATCH - 1]], axis=1)
    up_one = jnp.concatenate([grouped[:, 1:], grouped[:, :1]], axis=1)
    smooth = (grouped + (down_one + up_one)).reshape(192, 128)
    response = jnp.sqrt(smooth * (1.0 / 9.0)) * (1.0 / PATCH)
    fr, fi = zr * response, zi * response
    w = jnp.concatenate(
        [
            jnp.concatenate([fr[64 * j : 64 * j + 64] for j in range(3)], axis=1),
            jnp.concatenate([fi[64 * j : 64 * j + 64] for j in range(3)], axis=1),
        ],
        axis=0,
    )
    wh, wl = split(w)
    bh, bl = rb_ref[0], rb_ref[1]
    t = mm(bh, wh) + (mm(bh, wl) + mm(bl, wh))
    th, tl = split(t)
    gh, gl = cb_ref[0], cb_ref[1]
    o = mm(th, gh) + (mm(tl, gh) + mm(th, gl))
    real = o[:16, :128] - o[16:, 128:]
    imag = o[16:, :128] + o[:16, 128:]
    for p in range(PAIRS_DEV):
        out_ref[p, 0] = real[:, PATCH * p : PATCH * p + PATCH]
        out_ref[p, 1] = imag[:, PATCH * p : PATCH * p + PATCH]


def goldstein(edges, up, mid, down):
    def pair_of(matrix):
        return jnp.asarray(np.stack(split_const(matrix)))

    tables = (
        pair_of(row_forward()),
        pair_of(col_forward()),
        jnp.asarray(neighbour_sum().astype(jnp.bfloat16)),
        pair_of(row_back()),
        pair_of(col_back()),
    )
    vmem = pl.BlockSpec(memory_space=pltpu.VMEM)
    return pl.pallas_call(
        goldstein_kernel,
        out_shape=jax.ShapeDtypeStruct((PAIRS_DEV, 2, 16, 32), F32),
        in_specs=[pl.BlockSpec(memory_space=pltpu.SMEM)] + [vmem] * 8,
        out_specs=vmem,
        compiler_params=pltpu.CompilerParams(vmem_limit_bytes=24 * 2**20),
    )(edges, up, mid, down, *tables)


def fetch(x, axis, by):
    size = lax.axis_size(axis)
    return lax.ppermute(x, axis, [((i + by) % size, i) for i in range(size)])


def shards(stack, pair_list):
    date = lax.axis_index("date")
    row = lax.axis_index("row")
    col = lax.axis_index("col")
    following = fetch(stack[:SPAN], "date", 1)
    idx = lax.dynamic_slice_in_dim(pair_list, date * PAIRS_DEV, PAIRS_DEV, 0) - date * PAIRS_DEV
    left, right, coherence = looks(idx.reshape(-1), stack, following)
    before = jnp.where(col == 0, 0.0, fetch(right, "col", -1))
    after = jnp.where(col == lax.axis_size("col") - 1, 0.0, fetch(left, "col", 1))
    mid = jnp.concatenate([before, left, right, after], axis=1)
    up = fetch(mid, "row", -1)
    down = fetch(mid, "row", 1)
    edges = jnp.stack([row, lax.axis_size("row") - 1 - row]).astype(jnp.int32)
    return goldstein(edges, up, mid, down), coherence


def solution(mesh):
    in_specs = (P("date", None, "row", "col"), P())
    out_specs = (P("date", None, "row", "col"), P("date", "row", "col"))
    return jax.shard_map(shards, mesh=mesh, in_specs=in_specs, out_specs=out_specs, check_vma=False)
```

```python
import functools
import math

import jax
import jax.numpy as jnp
import numpy as np
from jax import lax
from jax.experimental import pallas as pl
from jax.experimental.pallas import tpu as pltpu
from jax.sharding import PartitionSpec as P

SPAN = 3
LOOK_R = 5
LOOK_C = 20
PATCH = 32
HALF = PATCH // 2
PAIRS_DEV = 4
F32 = jnp.float32
BF16 = jnp.bfloat16


def taper(v):
    return np.where(v < HALF, (v + 0.5) / HALF, (PATCH - 0.5 - v) / HALF)


def whole_part(x, divisor):
    return (x.astype(F32) * (1.0 / divisor) + 0.5 / divisor).astype(jnp.int32)


def look_table():
    lane = lax.broadcasted_iota(jnp.int32, (384, 256), 0)
    n = lax.broadcasted_iota(jnp.int32, (384, 256), 1)
    left = jnp.where(lane < 256, lane, 256 + lane % 64)
    right = jnp.where(lane < 256, 64 + lane, lane % 64)
    cell = whole_part(jnp.where(n < 128, left, right), LOOK_C)
    return (cell == n % HALF).astype(F32).astype(BF16)


def row_forward():
    i, k, q, row = np.meshgrid(np.arange(2), np.arange(PATCH), np.arange(2), np.arange(48), indexing="ij")
    u = row - HALF * i
    angle = 2 * np.pi * k * u / PATCH
    value = np.where(q == 0, np.cos(angle), -np.sin(angle)) * ((u >= 0) & (u < PATCH))
    return value.reshape(64, 96)


def col_forward():
    h, c, p, v, c2, p2, l = np.meshgrid(
        np.arange(2), np.arange(2), np.arange(4), np.arange(HALF), np.arange(2), np.arange(4), np.arange(PATCH),
        indexing="ij",
    )
    angle = 2 * np.pi * l * (HALF * h + v) / PATCH
    value = np.where(c == c2, np.cos(angle), np.where(c == 1, np.sin(angle), -np.sin(angle)))
    return (value * (p == p2)).reshape(256, 256)


def neighbour_sum():
    a = lax.broadcasted_iota(jnp.int32, (128, 128), 0)
    b = lax.broadcasted_iota(jnp.int32, (128, 128), 1)
    d = (a - b) & (PATCH - 1)
    near = (d <= 1) | (d == PATCH - 1)
    return (near & ((a & -PATCH) == (b & -PATCH))).astype(F32).astype(BF16)


def row_back():
    c2, r, c, i, k = np.meshgrid(
        np.arange(2), np.arange(HALF), np.arange(2), np.arange(2), np.arange(PATCH), indexing="ij"
    )
    u = r + HALF * (1 - i)
    angle = 2 * np.pi * k * u / PATCH
    value = np.where(c == c2, np.cos(angle), np.where(c2 == 0, -np.sin(angle), np.sin(angle))) * taper(u)
    return value.reshape(32, 128)


def col_back():
    j, p, l, q, p2, c = np.meshgrid(
        np.arange(3), np.arange(4), np.arange(PATCH), np.arange(2), np.arange(4), np.arange(PATCH), indexing="ij"
    )
    v = c + HALF - HALF * j
    angle = 2 * np.pi * l * v / PATCH
    value = np.where(q == 0, np.cos(angle), np.sin(angle)) * taper(v) * ((v >= 0) & (v < PATCH)) * (p == p2)
    return (value / (PATCH * PATCH)).reshape(384, 256)


def split(x):
    hi = x.astype(BF16)
    return hi, (x - hi.astype(F32)).astype(BF16)


def mm(a, b):
    return jnp.dot(a, b, preferred_element_type=F32)


def half_copies(stack_ref, first, out_ref, tile, sem, slot):
    count = out_ref.shape[0]
    return [
        pltpu.make_async_copy(
            stack_ref.at[first : first + count, comp, :, pl.ds(128 * (tile + t), 128)],
            out_ref.at[:, 2 * comp + t],
            sem.at[slot, 2 * comp + t],
        )
        for comp in range(2)
        for t in range(2)
    ]


def lower_lanes(shape):
    return lax.broadcasted_iota(jnp.int32, shape, len(shape) - 1) % 128 < 64


def fill_mixed(mid_ref, acq, left_ref, left_at, right_ref, right_at):
    real, imag = mid_ref[acq, 0], mid_ref[acq, 1]
    lower = lower_lanes(real.shape)
    if left_at is not None:
        left_ref[left_at, 4] = jnp.where(lower, real, pltpu.roll(imag, 64, 1))
    if right_at is not None:
        right_ref[right_at, 4] = jnp.where(lower, pltpu.roll(real, 64, 1), imag)


def pack_kernel(stack_ref, up_ref, down_ref, middle, sem):
    copies = [pltpu.make_async_copy(stack_ref.at[:, :, :, pl.ds(256, 128)], middle, sem.at[2, 0])]
    copies += half_copies(stack_ref, 0, up_ref, 0, sem, 0)
    copies += half_copies(stack_ref, 1, down_ref, 3, sem, 1)
    for copy in copies:
        copy.start()
    copies[0].wait()
    for acq in range(4):
        fill_mixed(middle, acq, up_ref, acq if acq < 3 else None, down_ref, acq - 1 if acq > 0 else None)
    for copy in copies[1:]:
        copy.wait()


def pack(stack):
    vmem = pl.BlockSpec(memory_space=pltpu.VMEM)
    half = jax.ShapeDtypeStruct((SPAN, 5, 80, 128), F32)
    return pl.pallas_call(
        pack_kernel,
        out_shape=(half, half),
        in_specs=[pl.BlockSpec(memory_space=pl.ANY)],
        out_specs=(vmem, vmem),
        scratch_shapes=[pltpu.VMEM((4, 2, 80, 128), F32), pltpu.SemaphoreType.DMA((3, 4))],
    )(stack)


def cross(a_ref, a, b_ref, b):
    real, imag = [0.0] * 3, [0.0] * 3
    for k in range(LOOK_R):
        rows = pl.ds(k, 16, stride=LOOK_R)
        x = [a_ref[a, t, rows, :] for t in range(5)]
        y = [b_ref[b, t, rows, :] for t in range(5)]
        for t in range(2):
            real[t] += x[t] * y[t] + x[t + 2] * y[t + 2]
            imag[t] += x[t + 2] * y[t] - x[t] * y[t + 2]
        real[2] += x[4] * y[4]
        imag[2] += x[4] * pltpu.roll(y[4], 64, 1)
    imag[2] = jnp.where(lower_lanes((16, 128)), -imag[2], imag[2])
    return jnp.concatenate(real, axis=1), jnp.concatenate(imag, axis=1)


def power(a_ref, a):
    total = [0.0] * 3
    for k in range(LOOK_R):
        x = [a_ref[a, t, pl.ds(k, 16, stride=LOOK_R), :] for t in range(5)]
        for t in range(2):
            total[t] += x[t] * x[t] + x[t + 2] * x[t + 2]
        total[2] += x[4] * x[4]
    return jnp.concatenate(total, axis=1)


def pooled(planes, table):
    high, low = split(jnp.concatenate(planes, axis=0))
    cells = (mm(high, table) + mm(low, table)) * (1.0 / (LOOK_R * LOOK_C))
    return cells.reshape(len(planes), 16, 256)


def pair_lanes():
    return lax.broadcasted_iota(jnp.int32, (16, 128), 1) // HALF


def message(cells, offset):
    group = pair_lanes()
    out = jnp.zeros((16, 128), F32)
    for p in range(PAIRS_DEV):
        for comp in range(2):
            value = cells[2 * p + comp, :, offset : offset + 128]
            out = jnp.where(group == comp * PAIRS_DEV + p, value, out)
    return out


def crossing_lanes(list_ref, date):
    group = pair_lanes() % PAIRS_DEV
    out = jnp.zeros((16, 128), jnp.int32)
    for p in range(PAIRS_DEV):
        second = list_ref[1, PAIRS_DEV * date + p] - 4 * date
        out = jnp.where(group == p, (second >= 4).astype(jnp.int32), out)
    return out == 1


def early_kernel(list_ref, stack_ref, trig_ref, *refs):
    left_ref, right_ref, power_ref, keep_l, keep_r, look_out, ns_out = refs[:7]
    rf_out, cf_out, rb_out, cb_out = refs[7:11]
    middle, sem = refs[11:]
    copies = [pltpu.make_async_copy(stack_ref.at[:, :, :, pl.ds(256, 128)], middle, sem.at[2, 0])]
    copies += half_copies(stack_ref, 0, keep_l, 0, sem, 0)
    copies += half_copies(stack_ref, 0, keep_r, 3, sem, 1)
    for copy in copies:
        copy.start()
    table = look_table()
    look_out[...] = table
    ns_out[...] = neighbour_sum()
    for source, target in (
        (trig_ref[:256], cf_out),
        (trig_ref[256:640], cb_out),
        (trig_ref[640:704, :96], rf_out),
        (trig_ref[640:672, 128:], rb_out),
    ):
        high, low = split(source)
        target[0] = high
        target[1] = low
    copies[0].wait()
    for acq in range(4):
        fill_mixed(middle, acq, keep_l, acq, keep_r, acq)
    for copy in copies[1:]:
        copy.wait()
    date = lax.axis_index("date")
    planes_l, planes_r = [], []
    for p in range(PAIRS_DEV):
        a = list_ref[0, PAIRS_DEV * date + p] - 4 * date
        b = jnp.minimum(list_ref[1, PAIRS_DEV * date + p] - 4 * date, 3)
        planes_l += cross(keep_l, a, keep_l, b)
        planes_r += cross(keep_r, a, keep_r, b)
    for acq in range(4):
        planes_l.append(power(keep_l, acq))
        planes_r.append(power(keep_r, acq))
    cells_l = pooled(planes_l, table)
    cells_r = pooled(planes_r, table)
    left_ref[...] = message(cells_l, 0)
    right_ref[...] = message(cells_r, 128)
    first = pair_lanes() % 2 == 0
    for acq in range(4):
        power_ref[acq] = jnp.where(first, cells_l[8 + acq, :, :128], cells_r[8 + acq, :, 128:])


def early(listed, stack):
    vmem = pl.BlockSpec(memory_space=pltpu.VMEM)
    smem = pl.BlockSpec(memory_space=pltpu.SMEM)
    trig = np.zeros((704, 256))
    trig[:256] = col_forward()
    trig[256:640] = col_back()
    trig[640:704, :96] = row_forward()
    trig[640:672, 128:] = row_back()
    message_shape = jax.ShapeDtypeStruct((16, 128), F32)
    half = jax.ShapeDtypeStruct((4, 5, 80, 128), F32)
    out_shape = (
        [message_shape, message_shape, jax.ShapeDtypeStruct((4, 16, 128), F32), half, half]
        + [jax.ShapeDtypeStruct(shape, BF16) for shape in ((384, 256), (128, 128))]
        + [
            jax.ShapeDtypeStruct((2,) + shape, BF16)
            for shape in ((64, 96), (256, 256), (32, 128), (384, 256))
        ]
    )
    return pl.pallas_call(
        early_kernel,
        out_shape=out_shape,
        in_specs=[smem, pl.BlockSpec(memory_space=pl.ANY), vmem],
        out_specs=[vmem] * len(out_shape),
        scratch_shapes=[pltpu.VMEM((4, 2, 80, 128), F32), pltpu.SemaphoreType.DMA((3, 4))],
        compiler_params=pltpu.CompilerParams(vmem_limit_bytes=24 * 2**20),
        cost_estimate=pl.CostEstimate(flops=10**9, bytes_accessed=10**7, transcendentals=0),
    )(listed, stack, jnp.asarray(trig, F32))


def late_kernel(
    list_ref, up_ref, down_ref, keep_l, keep_r, table_ref, left_in, left_ref, right_ref
):
    date = lax.axis_index("date")
    before = lax.rem(date + lax.axis_size("date") - 1, lax.axis_size("date"))
    planes_l, planes_r = [], []
    for p in range(PAIRS_DEV):
        own, other = PAIRS_DEV * date + p, PAIRS_DEV * before + p
        a = jnp.clip(list_ref[0, own] - 4 * date, 0, 3)
        b = jnp.clip(list_ref[1, own] - 4 * date - 4, 0, 2)
        planes_l += cross(keep_l, a, up_ref, b)
        a = jnp.clip(list_ref[0, other] - 4 * before - 1, 0, 2)
        b = jnp.clip(list_ref[1, other] - 4 * before - 4, 0, 3)
        planes_r += cross(down_ref, a, keep_r, b)
    cells = pooled(planes_l + planes_r, table_ref[...])
    crossing = crossing_lanes(list_ref, date)
    left_ref[...] = jnp.where(crossing, message(cells[:8], 0), left_in[...])
    right_ref[...] = message(cells[8:], 128)


def late(listed, up, down, keep_l, keep_r, table, left):
    vmem = pl.BlockSpec(memory_space=pltpu.VMEM)
    smem = pl.BlockSpec(memory_space=pltpu.SMEM)
    shape = jax.ShapeDtypeStruct((16, 128), F32)
    return pl.pallas_call(
        late_kernel,
        out_shape=(shape, shape),
        in_specs=[smem] + [vmem] * 6,
        out_specs=(vmem, vmem),
        compiler_params=pltpu.CompilerParams(vmem_limit_bytes=24 * 2**20),
    )(listed, up, down, keep_l, keep_r, table, left)


def merge_kernel(
    list_ref, before_late, before_early, left_ref, right_late, right_early, after_ref, mid_ref
):
    crossing = crossing_lanes(list_ref, lax.axis_index("date"))
    col = lax.axis_index("col")
    before = jnp.where(crossing, before_late[...], before_early[...])
    mid_ref[:, :128] = jnp.where(col == 0, 0.0, before)
    mid_ref[:, 128:256] = left_ref[...]
    mid_ref[:, 256:384] = jnp.where(crossing, right_late[...], right_early[...])
    mid_ref[:, 384:] = jnp.where(col == lax.axis_size("col") - 1, 0.0, after_ref[...])


def merge(listed, *parts):
    vmem = pl.BlockSpec(memory_space=pltpu.VMEM)
    smem = pl.BlockSpec(memory_space=pltpu.SMEM)
    return pl.pallas_call(
        merge_kernel,
        out_shape=jax.ShapeDtypeStruct((16, 512), F32),
        in_specs=[smem] + [vmem] * 6,
        out_specs=vmem,
        compiler_params=pltpu.CompilerParams(vmem_limit_bytes=8 * 2**20),
    )(listed, *parts)


def coherence_kernel(list_ref, mid_ref, own_ref, next_ref, out_ref):
    date = lax.axis_index("date")
    left, right = mid_ref[:, 128:256], mid_ref[:, 256:384]
    first = pair_lanes() % 2 == 0

    def whole(group):
        shift = 128 - HALF * group
        a = left if group == 0 else pltpu.roll(left, shift, 1)
        return jnp.where(first, a, pltpu.roll(right, (shift + HALF) % 128, 1))

    for p in range(PAIRS_DEV):
        a = list_ref[0, PAIRS_DEV * date + p] - 4 * date
        b = list_ref[1, PAIRS_DEV * date + p] - 4 * date
        real, imag = whole(p), whole(PAIRS_DEV + p)
        power_a = own_ref[a]
        power_b = jnp.where(b >= 4, next_ref[jnp.maximum(b - 4, 0)], own_ref[jnp.minimum(b, 3)])
        magnitude = jnp.sqrt(real * real + imag * imag)
        out_ref[p] = (magnitude / jnp.sqrt((power_a + 1e-06) * (power_b + 1e-06)))[:, :PATCH]


def coherences(listed, mid, own, following):
    vmem = pl.BlockSpec(memory_space=pltpu.VMEM)
    smem = pl.BlockSpec(memory_space=pltpu.SMEM)
    return pl.pallas_call(
        coherence_kernel,
        out_shape=jax.ShapeDtypeStruct((PAIRS_DEV, 16, 32), F32),
        in_specs=[smem] + [vmem] * 3,
        out_specs=vmem,
        compiler_params=pltpu.CompilerParams(vmem_limit_bytes=8 * 2**20),
        cost_estimate=pl.CostEstimate(flops=10**8, bytes_accessed=10**6, transcendentals=0),
    )(listed, mid, own, following)


def goldstein_kernel(
    up_ref, mid_ref, down_ref, rf_ref, cf_ref, ns_ref, rb_ref, cb_ref, out_ref
):
    row = lax.axis_index("row")
    up = jnp.where(row == 0, 0.0, up_ref[...])
    down = jnp.where(row == lax.axis_size("row") - 1, 0.0, down_ref[...])
    x = jnp.concatenate([up, mid_ref[...], down], axis=0)
    lane = lax.broadcasted_iota(jnp.int32, (48, 128), 1)
    sign = jnp.where(lane < 64, -1.0, 1.0)
    turned = [pltpu.roll(x[:, 128 * b : 128 * b + 128], 64, 1) * sign for b in range(4)]
    xx = jnp.concatenate([x, jnp.concatenate(turned, axis=1)], axis=0)
    xh, xl = split(xx)
    rh, rl = rf_ref[0], rf_ref[1]
    y = mm(rh, xh) + (mm(rh, xl) + mm(rl, xh))
    ys = jnp.concatenate([y[:, 128 * j : 128 * j + 256] for j in range(3)], axis=0)
    yh, yl = split(ys)
    ch, cl = cf_ref[0], cf_ref[1]
    z = mm(yh, ch) + (mm(yl, ch) + mm(yh, cl))
    zr, zi = z[:, :128], z[:, 128:]
    magnitude = jnp.sqrt(zr * zr + zi * zi)
    mh, ml = split(magnitude)
    across = mm(mh, ns_ref[...]) + mm(ml, ns_ref[...])
    grouped = across.reshape(6, PATCH, 128)
    down_one = jnp.concatenate([grouped[:, PATCH - 1 :], grouped[:, : PATCH - 1]], axis=1)
    up_one = jnp.concatenate([grouped[:, 1:], grouped[:, :1]], axis=1)
    smooth = (grouped + (down_one + up_one)).reshape(192, 128)
    response = jnp.sqrt(smooth * (1.0 / 9.0)) * (1.0 / PATCH)
    fr, fi = zr * response, zi * response
    w = jnp.concatenate(
        [
            jnp.concatenate([fr[64 * j : 64 * j + 64] for j in range(3)], axis=1),
            jnp.concatenate([fi[64 * j : 64 * j + 64] for j in range(3)], axis=1),
        ],
        axis=0,
    )
    wh, wl = split(w)
    bh, bl = rb_ref[0], rb_ref[1]
    t = mm(bh, wh) + (mm(bh, wl) + mm(bl, wh))
    th, tl = split(t)
    gh, gl = cb_ref[0], cb_ref[1]
    o = mm(th, gh) + (mm(tl, gh) + mm(th, gl))
    real = o[:16, :128] - o[16:, 128:]
    imag = o[16:, :128] + o[:16, 128:]
    for p in range(PAIRS_DEV):
        out_ref[p, 0] = real[:, PATCH * p : PATCH * p + PATCH]
        out_ref[p, 1] = imag[:, PATCH * p : PATCH * p + PATCH]


def goldstein(up, mid, down, *tables):
    vmem = pl.BlockSpec(memory_space=pltpu.VMEM)
    return pl.pallas_call(
        goldstein_kernel,
        out_shape=jax.ShapeDtypeStruct((PAIRS_DEV, 2, 16, 32), F32),
        in_specs=[vmem] * 8,
        out_specs=vmem,
        compiler_params=pltpu.CompilerParams(vmem_limit_bytes=24 * 2**20),
    )(up, mid, down, *tables)


def shards(stack, pair_list):
    names = ("date", "row", "col")
    sizes = tuple(lax.axis_size(name) for name in names)
    cells = [(d, r, c) for d in range(sizes[0]) for r in range(sizes[1]) for c in range(sizes[2])]

    def fetch(x, *by):
        def index(at):
            d, r, c = ((i + j) % n for i, j, n in zip(at, by, sizes))
            return (d * sizes[1] + r) * sizes[2] + c

        return lax.ppermute(x, names, [(index(at), i) for i, at in enumerate(cells)])

    listed = pair_list.T
    up, down = pack(stack)
    up = fetch(up, 1, 0, 0)
    down = fetch(down, -1, 0, 0)
    left_early, right_early, own_power, keep_l, keep_r, look, near, rf, cf, rb, cb = early(listed, stack)
    before_early = fetch(right_early, 0, 0, -1)
    next_power = fetch(own_power, 1, 0, 0)
    left, right_out = late(listed, up, down, keep_l, keep_r, look, left_early)
    after = fetch(left, 0, 0, 1)
    before_late = fetch(right_out, 1, 0, -1)
    right_late = fetch(right_out, 1, 0, 0)
    mid = merge(listed, before_late, before_early, left, right_late, right_early, after)
    above = fetch(mid, 0, -1, 0)
    below = fetch(mid, 0, 1, 0)
    coherence = coherences(listed, mid, own_power, next_power)
    return goldstein(above, mid, below, rf, cf, near, rb, cb), coherence


def solution(mesh):
    in_specs = (P("date", None, "row", "col"), P())
    out_specs = (P("date", None, "row", "col"), P("date", "row", "col"))
    return jax.shard_map(shards, mesh=mesh, in_specs=in_specs, out_specs=out_specs, check_vma=False)
```

```python
import functools
import math

import jax
import jax.numpy as jnp
import numpy as np
from jax import lax
from jax.experimental import pallas as pl
from jax.experimental.pallas import tpu as pltpu
from jax.sharding import PartitionSpec as P

SPAN = 3
LOOK_R = 5
LOOK_C = 20
PATCH = 32
HALF = PATCH // 2
PAIRS_DEV = 4
F32 = jnp.float32
BF16 = jnp.bfloat16
HBM = pltpu.MemorySpace.HBM


def taper(v):
    return np.where(v < HALF, (v + 0.5) / HALF, (PATCH - 0.5 - v) / HALF)


def whole_part(x, divisor):
    return (x.astype(F32) * (1.0 / divisor) + 0.5 / divisor).astype(jnp.int32)


def look_table():
    lane = lax.broadcasted_iota(jnp.int32, (384, 256), 0)
    n = lax.broadcasted_iota(jnp.int32, (384, 256), 1)
    left = jnp.where(lane < 256, lane, 256 + lane % 64)
    right = jnp.where(lane < 256, 64 + lane, lane % 64)
    cell = whole_part(jnp.where(n < 128, left, right), LOOK_C)
    return (cell == n % HALF).astype(F32).astype(BF16)


def row_forward():
    i, k, q, row = np.meshgrid(np.arange(2), np.arange(PATCH), np.arange(2), np.arange(48), indexing="ij")
    u = row - HALF * i
    angle = 2 * np.pi * k * u / PATCH
    value = np.where(q == 0, np.cos(angle), -np.sin(angle)) * ((u >= 0) & (u < PATCH))
    return value.reshape(64, 96)


def col_forward():
    h, c, p, v, c2, p2, l = np.meshgrid(
        np.arange(2), np.arange(2), np.arange(4), np.arange(HALF), np.arange(2), np.arange(4), np.arange(PATCH),
        indexing="ij",
    )
    angle = 2 * np.pi * l * (HALF * h + v) / PATCH
    value = np.where(c == c2, np.cos(angle), np.where(c == 1, np.sin(angle), -np.sin(angle)))
    return (value * (p == p2)).reshape(256, 256)


def neighbour_sum():
    a = lax.broadcasted_iota(jnp.int32, (128, 128), 0)
    b = lax.broadcasted_iota(jnp.int32, (128, 128), 1)
    d = (a - b) & (PATCH - 1)
    near = (d <= 1) | (d == PATCH - 1)
    return (near & ((a & -PATCH) == (b & -PATCH))).astype(F32).astype(BF16)


def row_back():
    c2, r, c, i, k = np.meshgrid(
        np.arange(2), np.arange(HALF), np.arange(2), np.arange(2), np.arange(PATCH), indexing="ij"
    )
    u = r + HALF * (1 - i)
    angle = 2 * np.pi * k * u / PATCH
    value = np.where(c == c2, np.cos(angle), np.where(c2 == 0, -np.sin(angle), np.sin(angle))) * taper(u)
    return value.reshape(32, 128)


def col_back():
    j, p, l, q, p2, c = np.meshgrid(
        np.arange(3), np.arange(4), np.arange(PATCH), np.arange(2), np.arange(4), np.arange(PATCH), indexing="ij"
    )
    v = c + HALF - HALF * j
    angle = 2 * np.pi * l * v / PATCH
    value = np.where(q == 0, np.cos(angle), np.sin(angle)) * taper(v) * ((v >= 0) & (v < PATCH)) * (p == p2)
    return (value / (PATCH * PATCH)).reshape(384, 256)


def split(x):
    hi = x.astype(BF16)
    return hi, (x - hi.astype(F32)).astype(BF16)


def mm(a, b):
    return jnp.dot(a, b, preferred_element_type=F32)


def half_copies(stack_ref, first, out_ref, tile, sem, slot):
    count = out_ref.shape[0]
    return [
        pltpu.make_async_copy(
            stack_ref.at[first : first + count, comp, :, pl.ds(128 * (tile + t), 128)],
            out_ref.at[:, 2 * comp + t],
            sem.at[slot, 2 * comp + t],
        )
        for comp in range(2)
        for t in range(2)
    ]


def lower_lanes(shape):
    return lax.broadcasted_iota(jnp.int32, shape, len(shape) - 1) % 128 < 64


def mixed_tile(real, imag, right):
    turned = pltpu.roll(jnp.where(right, real, imag), 64, 1)
    return jnp.where(lower_lanes(real.shape) == right, turned, jnp.where(right, imag, real))


def half_pair(stack_ref, count, left_ref, right_ref, middle, sem):
    lanes = pl.ds(256, 128)
    copies = [pltpu.make_async_copy(stack_ref.at[:count, :, :, lanes], middle, sem.at[2, 0])]
    copies += half_copies(stack_ref, 0, left_ref, 0, sem, 0)
    copies += half_copies(stack_ref, 0, right_ref, 3, sem, 1)
    for copy in copies:
        copy.start()
    return copies


def half_pair_end(copies, count, left_ref, right_ref, middle):
    copies[0].wait()
    for acq in range(count):
        left_ref[acq, 4] = mixed_tile(middle[acq, 0], middle[acq, 1], False)
        right_ref[acq, 4] = mixed_tile(middle[acq, 0], middle[acq, 1], True)
    for copy in copies[1:]:
        copy.wait()


def odd_date():
    return lax.axis_index("date") % 2


def pack_kernel(half_ref, out_ref):
    odd = odd_date() == 1
    for acq in range(SPAN):
        tiles = [[half_ref[acq, comp, :, pl.ds(128 * t, 128)] for t in range(3)] for comp in range(2)]
        for comp in range(2):
            out_ref[acq, 2 * comp] = jnp.where(odd, tiles[comp][1], tiles[comp][0])
            out_ref[acq, 2 * comp + 1] = jnp.where(odd, tiles[comp][2], tiles[comp][1])
        real, imag = (jnp.where(odd, tiles[comp][0], tiles[comp][2]) for comp in range(2))
        out_ref[acq, 4] = mixed_tile(real, imag, odd)


def pack(half):
    vmem = pl.BlockSpec(memory_space=pltpu.VMEM)
    return pl.pallas_call(
        pack_kernel,
        out_shape=jax.ShapeDtypeStruct((SPAN, 5, 80, 128), F32),
        in_specs=[vmem],
        out_specs=vmem,
        compiler_params=pltpu.CompilerParams(vmem_limit_bytes=16 * 2**20),
    )(half)


def cross(a_ref, a, b_ref, b):
    real, imag = [0.0] * 3, [0.0] * 3
    for k in range(LOOK_R):
        rows = pl.ds(k, 16, stride=LOOK_R)
        x = [a_ref[a, t, rows, :] for t in range(5)]
        y = [b_ref[b, t, rows, :] for t in range(5)]
        for t in range(2):
            real[t] += x[t] * y[t] + x[t + 2] * y[t + 2]
            imag[t] += x[t + 2] * y[t] - x[t] * y[t + 2]
        real[2] += x[4] * y[4]
        imag[2] += x[4] * pltpu.roll(y[4], 64, 1)
    imag[2] = jnp.where(lower_lanes((16, 128)), -imag[2], imag[2])
    return jnp.concatenate(real, axis=1), jnp.concatenate(imag, axis=1)


def power(a_ref, a):
    total = [0.0] * 3
    for k in range(LOOK_R):
        x = [a_ref[a, t, pl.ds(k, 16, stride=LOOK_R), :] for t in range(5)]
        for t in range(2):
            total[t] += x[t] * x[t] + x[t + 2] * x[t + 2]
        total[2] += x[4] * x[4]
    return jnp.concatenate(total, axis=1)


def pooled(planes, table):
    high, low = split(jnp.concatenate(planes, axis=0))
    cells = (mm(high, table) + mm(low, table)) * (1.0 / (LOOK_R * LOOK_C))
    return cells.reshape(len(planes), 16, 256)


def pair_lanes():
    return lax.broadcasted_iota(jnp.int32, (16, 128), 1) // HALF


def message(cells, offset):
    group = pair_lanes()
    out = jnp.zeros((16, 128), F32)
    for p in range(PAIRS_DEV):
        for comp in range(2):
            value = cells[2 * p + comp, :, offset : offset + 128]
            out = jnp.where(group == comp * PAIRS_DEV + p, value, out)
    return out


def power_cells(left_cells, right_cells):
    return jnp.where(lower_lanes((16, 128)), left_cells[:, :128], right_cells[:, 128:])


def by_pair(values):
    group = pair_lanes() % PAIRS_DEV
    out = values[0]
    for p in range(1, PAIRS_DEV):
        out = jnp.where(group == p, values[p], out)
    return out


def pair_of(list_ref, group, p):
    return tuple(list_ref[i, PAIRS_DEV * group + p] - 4 * group for i in range(2))


def early_kernel(
    list_ref, stack_ref, left_ref, right_ref, first_ref, second_ref, back_ref, crossing_ref, index_ref, keep, look_out,
    powers, middle, sem,
):
    keep_l, keep_r = keep.at[0], keep.at[1]
    copies = half_pair(stack_ref, 4, keep_l, keep_r, middle, sem)
    table = look_table()
    look_out[...] = table
    date = lax.axis_index("date")
    odd = odd_date() == 1
    before = jnp.maximum(date - 1, 0)
    own = [pair_of(list_ref, date, p) for p in range(PAIRS_DEV)]
    others = [pair_of(list_ref, before, p) for p in range(PAIRS_DEV)]
    crossing_ref[...] = by_pair([jnp.full((16, 128), (b >= 4).astype(jnp.int32)) for a, b in own])
    lane = lax.broadcasted_iota(jnp.int32, (8, 128), 1)
    index = jnp.zeros((8, 128), jnp.int32)
    for p in range(PAIRS_DEV):
        mine = jnp.where(odd, own[p][0], jnp.clip(others[p][1] - 4, 0, 3))
        theirs = jnp.where(odd, jnp.clip(own[p][1] - 4, 0, 2), jnp.clip(others[p][0] - 1, 0, 2))
        index = jnp.where(lane == p, mine, jnp.where(lane == PAIRS_DEV + p, theirs, index))
    index_ref[...] = index
    half_pair_end(copies, 4, keep_l, keep_r, middle)
    planes_l, planes_r = [], []
    for a, b in own:
        planes_l += cross(keep_l, a, keep_l, jnp.minimum(b, 3))
        planes_r += cross(keep_r, a, keep_r, jnp.minimum(b, 3))
    for acq in range(4):
        planes_l.append(power(keep_l, acq))
        planes_r.append(power(keep_r, acq))
    cells_l = pooled(planes_l, table)
    cells_r = pooled(planes_r, table)
    left_ref[...] = message(cells_l, 0)
    right_ref[...] = message(cells_r, 128)
    for acq in range(4):
        powers[acq] = power_cells(cells_l[8 + acq], cells_r[8 + acq])
    first_ref[...] = by_pair([powers[a] for a, b in own])
    second_ref[...] = by_pair([powers[jnp.minimum(b, 3)] for a, b in own])
    back_ref[...] = by_pair([powers[jnp.clip(b - 4, 0, 3)] for a, b in others])


def early(listed, stack):
    vmem = pl.BlockSpec(memory_space=pltpu.VMEM)
    smem = pl.BlockSpec(memory_space=pltpu.SMEM)
    out_shape = [jax.ShapeDtypeStruct((16, 128), F32)] * 5 + [
        jax.ShapeDtypeStruct((16, 128), jnp.int32),
        jax.ShapeDtypeStruct((8, 128), jnp.int32),
        jax.ShapeDtypeStruct((2, 4, 5, 80, 128), F32),
        jax.ShapeDtypeStruct((384, 256), BF16),
    ]
    return pl.pallas_call(
        early_kernel,
        out_shape=out_shape,
        in_specs=[smem, pl.BlockSpec(memory_space=HBM)],
        out_specs=[vmem] * len(out_shape),
        scratch_shapes=[
            pltpu.VMEM((4, 16, 128), F32), pltpu.VMEM((4, 2, 80, 128), F32), pltpu.SemaphoreType.DMA((3, 4)),
        ],
        compiler_params=pltpu.CompilerParams(vmem_limit_bytes=24 * 2**20),
        cost_estimate=pl.CostEstimate(flops=10**9, bytes_accessed=10**7, transcendentals=0),
    )(listed, stack)


def chip_kernel(
    list_ref, other_ref, keep, table_ref, crossing_ref, left_in, right_in, second_in, left_ref, right_ref, second_ref,
    first_swap, second_swap, *scratch,
):
    left_ref[...] = left_in[...]
    right_ref[...] = right_in[...]
    second_ref[...] = second_in[...]

    @pl.when(odd_date() == 0)
    def _():
        other_l, other_r, powers, middle, sem = scratch
        copies = half_pair(other_ref, SPAN, other_l, other_r, middle, sem)
        half_pair_end(copies, SPAN, other_l, other_r, middle)
        date = lax.axis_index("date")
        planes_l, planes_r, seconds = [], [], []
        for p in range(PAIRS_DEV):
            a, b = pair_of(list_ref, date, p)
            seconds.append(jnp.maximum(b - 4, 0))
            planes_l += cross(keep.at[0], a, other_l, seconds[p])
            planes_r += cross(keep.at[1], a, other_r, seconds[p])
        for acq in range(SPAN):
            planes_l.append(power(other_l, acq))
            planes_r.append(power(other_r, acq))
        cells_l = pooled(planes_l, table_ref[...])
        cells_r = pooled(planes_r, table_ref[...])
        crossing = crossing_ref[...] == 1
        left_ref[...] = jnp.where(crossing, message(cells_l, 0), left_in[...])
        right_ref[...] = jnp.where(crossing, message(cells_r, 128), right_in[...])
        for acq in range(SPAN):
            powers[acq] = power_cells(cells_l[8 + acq], cells_r[8 + acq])
        second_ref[...] = jnp.where(crossing, by_pair([powers[b] for b in seconds]), second_in[...])

    odd_col = lax.axis_index("col") % 2 == 1
    left, right = left_ref[...], right_ref[...]
    first_swap[...] = jnp.where(odd_col, left, right)
    second_swap[...] = jnp.where(odd_col, right, left)


def within_chip(listed, other, *arrays):
    vmem = pl.BlockSpec(memory_space=pltpu.VMEM)
    half = pltpu.VMEM((SPAN, 5, 80, 128), F32)
    return pl.pallas_call(
        chip_kernel,
        out_shape=[jax.ShapeDtypeStruct((16, 128), F32)] * 5,
        in_specs=[pl.BlockSpec(memory_space=pltpu.SMEM), pl.BlockSpec(memory_space=HBM)] + [vmem] * 6,
        out_specs=[vmem] * 5,
        scratch_shapes=[
            half, half, pltpu.VMEM((SPAN, 16, 128), F32), pltpu.VMEM((SPAN, 2, 80, 128), F32),
            pltpu.SemaphoreType.DMA((3, 4)),
        ],
        compiler_params=pltpu.CompilerParams(vmem_limit_bytes=24 * 2**20),
        cost_estimate=pl.CostEstimate(flops=10**9, bytes_accessed=10**7, transcendentals=0),
    )(listed, other, *arrays)


def table_kernel(after_ref, trig_ref, ns_out, rf_out, cf_out, rb_out, cb_out):
    ns_out[...] = neighbour_sum()
    for source, target in (
        (trig_ref[:256], cf_out),
        (trig_ref[256:640], cb_out),
        (trig_ref[640:704, :96], rf_out),
        (trig_ref[640:672, 128:], rb_out),
    ):
        high, low = split(source)
        target[0] = high
        target[1] = low


def filter_tables(after):
    vmem = pl.BlockSpec(memory_space=pltpu.VMEM)
    trig = np.zeros((704, 256))
    trig[:256] = col_forward()
    trig[256:640] = col_back()
    trig[640:704, :96] = row_forward()
    trig[640:672, 128:] = row_back()
    out_shape = [jax.ShapeDtypeStruct((128, 128), BF16)] + [
        jax.ShapeDtypeStruct((2,) + shape, BF16) for shape in ((64, 96), (256, 256), (32, 128), (384, 256))
    ]
    return pl.pallas_call(
        table_kernel,
        out_shape=out_shape,
        in_specs=[vmem] * 2,
        out_specs=[vmem] * 5,
        compiler_params=pltpu.CompilerParams(vmem_limit_bytes=16 * 2**20),
        cost_estimate=pl.CostEstimate(flops=10**8, bytes_accessed=10**6, transcendentals=0),
    )(after, jnp.asarray(trig, F32))


def late_kernel(index_ref, other_ref, keep, table_ref, back_in, out_ref):
    odd = odd_date() == 1
    side = jnp.where(odd, 0, 1)
    index = index_ref[...]
    planes = []
    for p in range(PAIRS_DEV):
        planes += cross(keep.at[side], index[0, p], other_ref, index[0, PAIRS_DEV + p])
    cells = pooled(planes, table_ref[...])
    cells = jnp.where(odd, cells[:, :, :128], cells[:, :, 128:])
    new = message(cells, 0)
    out_ref[:16] = jnp.where(odd | lower_lanes((16, 128)), new, -new)
    out_ref[16:] = back_in[...]


def late(*arrays):
    vmem = pl.BlockSpec(memory_space=pltpu.VMEM)
    return pl.pallas_call(
        late_kernel,
        out_shape=jax.ShapeDtypeStruct((32, 128), F32),
        in_specs=[vmem] * 5,
        out_specs=vmem,
        compiler_params=pltpu.CompilerParams(vmem_limit_bytes=24 * 2**20),
    )(*arrays)


def merge_kernel(
    crossing_ref, before_late, left_late, right_late, after_late, first_ref, second_ref, left_early, right_early, mid_ref
):
    crossing = (crossing_ref[...] == 1) & (odd_date() == 1)
    col = lax.axis_index("col")
    odd_col = col % 2 == 1
    before = jnp.where(crossing, before_late[:16], jnp.where(odd_col, first_ref[...], second_ref[...]))
    after = jnp.where(crossing, after_late[:16], jnp.where(odd_col, second_ref[...], first_ref[...]))
    mid_ref[:, :128] = jnp.where(col == 0, 0.0, before)
    mid_ref[:, 128:256] = jnp.where(crossing, left_late[:16], left_early[...])
    mid_ref[:, 256:384] = jnp.where(crossing, right_late[:16], right_early[...])
    mid_ref[:, 384:] = jnp.where(col == lax.axis_size("col") - 1, 0.0, after)


def merge(*arrays):
    vmem = pl.BlockSpec(memory_space=pltpu.VMEM)
    return pl.pallas_call(
        merge_kernel,
        out_shape=jax.ShapeDtypeStruct((16, 512), F32),
        in_specs=[vmem] * 9,
        out_specs=vmem,
        compiler_params=pltpu.CompilerParams(vmem_limit_bytes=8 * 2**20),
    )(*arrays)


def coherence_of(mid_ref, first, second, out_ref):
    lane = lax.broadcasted_iota(jnp.int32, (16, 128), 1)
    squares = []
    for at in (128, 256):
        x = mid_ref[:, at : at + 128]
        squares.append(x * x + pltpu.roll(x * x, 64, 1))
    magnitude = jnp.sqrt(jnp.where(lane < 64, squares[0], squares[1]))
    coherence = magnitude / jnp.sqrt((first + 1e-06) * (second + 1e-06))
    for p in range(PAIRS_DEV):
        left = coherence if p == 0 else pltpu.roll(coherence, 128 - HALF * p, 1)
        right = pltpu.roll(coherence, (HALF + 64 - HALF * p) % 128, 1)
        out_ref[p] = jnp.where(lane < HALF, left, right)[:, :PATCH]


def goldstein_kernel(
    first_swap, mid_ref, second_swap, ns_ref, rf_ref, cf_ref, rb_ref, cb_ref, crossing_ref, first_ref, second_ref, late_ref,
    out_ref, coh_ref,
):
    odd_crossing = (crossing_ref[...] == 1) & (odd_date() == 1)
    coherence_of(mid_ref, first_ref[...], jnp.where(odd_crossing, late_ref[16:], second_ref[...]), coh_ref)
    row = lax.axis_index("row")
    odd_row = row % 2 == 1
    up = jnp.where(odd_row, first_swap[...], second_swap[...])
    down = jnp.where(odd_row, second_swap[...], first_swap[...])
    up = jnp.where(row == 0, 0.0, up)
    down = jnp.where(row == lax.axis_size("row") - 1, 0.0, down)
    x = jnp.concatenate([up, mid_ref[...], down], axis=0)
    lane = lax.broadcasted_iota(jnp.int32, (48, 128), 1)
    sign = jnp.where(lane < 64, -1.0, 1.0)
    turned = [pltpu.roll(x[:, 128 * b : 128 * b + 128], 64, 1) * sign for b in range(4)]
    xx = jnp.concatenate([x, jnp.concatenate(turned, axis=1)], axis=0)
    xh, xl = split(xx)
    rh, rl = rf_ref[0], rf_ref[1]
    y = mm(rh, xh) + (mm(rh, xl) + mm(rl, xh))
    ys = jnp.concatenate([y[:, 128 * j : 128 * j + 256] for j in range(3)], axis=0)
    yh, yl = split(ys)
    ch, cl = cf_ref[0], cf_ref[1]
    z = mm(yh, ch) + (mm(yl, ch) + mm(yh, cl))
    zr, zi = z[:, :128], z[:, 128:]
    magnitude = jnp.sqrt(zr * zr + zi * zi)
    mh, ml = split(magnitude)
    across = mm(mh, ns_ref[...]) + mm(ml, ns_ref[...])
    grouped = across.reshape(6, PATCH, 128)
    down_one = jnp.concatenate([grouped[:, PATCH - 1 :], grouped[:, : PATCH - 1]], axis=1)
    up_one = jnp.concatenate([grouped[:, 1:], grouped[:, :1]], axis=1)
    smooth = (grouped + (down_one + up_one)).reshape(192, 128)
    response = jnp.sqrt(smooth * (1.0 / 9.0)) * (1.0 / PATCH)
    fr, fi = zr * response, zi * response
    w = jnp.concatenate(
        [
            jnp.concatenate([fr[64 * j : 64 * j + 64] for j in range(3)], axis=1),
            jnp.concatenate([fi[64 * j : 64 * j + 64] for j in range(3)], axis=1),
        ],
        axis=0,
    )
    wh, wl = split(w)
    bh, bl = rb_ref[0], rb_ref[1]
    t = mm(bh, wh) + (mm(bh, wl) + mm(bl, wh))
    th, tl = split(t)
    gh, gl = cb_ref[0], cb_ref[1]
    o = mm(th, gh) + (mm(tl, gh) + mm(th, gl))
    real = o[:16, :128] - o[16:, 128:]
    imag = o[16:, :128] + o[:16, 128:]
    for p in range(PAIRS_DEV):
        out_ref[p, 0] = real[:, PATCH * p : PATCH * p + PATCH]
        out_ref[p, 1] = imag[:, PATCH * p : PATCH * p + PATCH]


def goldstein(*arrays):
    vmem = pl.BlockSpec(memory_space=pltpu.VMEM)
    return pl.pallas_call(
        goldstein_kernel,
        out_shape=(
            jax.ShapeDtypeStruct((PAIRS_DEV, 2, 16, 32), F32), jax.ShapeDtypeStruct((PAIRS_DEV, 16, 32), F32),
        ),
        in_specs=[vmem] * 12,
        out_specs=(vmem, vmem),
        compiler_params=pltpu.CompilerParams(vmem_limit_bytes=24 * 2**20),
    )(*arrays)


def neighbour(i, n, first):
    if first:
        return i ^ 1
    return ((i - 1) ^ 1) + 1 if 0 < i < n - 1 else i


def shards(stack, pair_list):
    names = ("date", "row", "col")
    dates, rows, cols = (lax.axis_size(name) for name in names)

    def send(x, target):
        pairs = []
        for d in range(dates):
            for r in range(rows):
                for c in range(cols):
                    a, b, e = target(d, r, c)
                    pairs.append(((d * rows + r) * cols + c, (a * rows + b) * cols + e))
        return lax.ppermute(x, names, pairs)

    def swap_cols(first):
        def target(d, r, c):
            e = neighbour(c, cols, first)
            return (d, r, e) if e != c else (d, r ^ 1, c)

        return target

    def swap_rows(first):
        def target(d, r, c):
            b = neighbour(r, rows, first)
            return (d, b, c) if b != r else (d, r, c ^ 1)

        return target

    def between_dates(odd_target, even_target):
        def target(d, r, c):
            if d in (0, dates - 1):
                return d, r, c ^ 1
            if d % 2:
                up, e = odd_target(c)
                return d + up, r, e
            down, e = even_target(c)
            return d - down, r, e

        return target

    end = cols - 1
    straight = between_dates(lambda c: (1, c), lambda c: (1, c))
    from_right = between_dates(
        lambda c: (0, c - 1) if c > 0 else (1, 0),
        lambda c: (0, c + 1) if c < end else (1, end),
    )
    from_left = between_dates(
        lambda c: (1, 0) if c == 0 else (0, 0) if c == 1 else (1, c - 1) if c < end else (1, end),
        lambda c: (1, c + 1) if c < end else (0, end - 1),
    )

    odd = lax.axis_index("date") % 2 == 1
    half = jnp.where(odd, stack[1:, :, :, 256:], stack[:SPAN, :, :, :384])
    listed = pair_list.T
    other = send(pack(half), straight)
    chip = send(stack, lambda d, r, c: (d ^ 1, r, c))
    left, right, first, second, back, crossing, index, keep, look = early(listed, stack)
    left, right, second, one, two = within_chip(listed, chip, keep, look, crossing, left, right, second)
    one = send(one, swap_cols(True))
    two = send(two, swap_cols(False))
    tables = filter_tables(right)
    other, one, two = lax.optimization_barrier((other, one, two))
    new = late(index, other, keep, look, back)
    after = send(new, from_right)
    before = send(new, from_left)
    right_late = send(new, straight)
    mid = merge(crossing, before, new, right_late, after, one, two, left, right)
    one = send(mid, swap_rows(True))
    two = send(mid, swap_rows(False))
    return goldstein(one, mid, two, *tables, crossing, first, second, right_late)


def solution(mesh):
    in_specs = (P("date", None, "row", "col"), P())
    out_specs = (P("date", None, "row", "col"), P("date", "row", "col"))
    return jax.shard_map(shards, mesh=mesh, in_specs=in_specs, out_specs=out_specs, check_vma=False)
```

```python
import functools
import math

import jax
import jax.numpy as jnp
import numpy as np
from jax import lax
from jax.experimental import pallas as pl
from jax.experimental.pallas import tpu as pltpu
from jax.sharding import PartitionSpec as P

SPAN = 3
LOOK_R = 5
LOOK_C = 20
PATCH = 32
HALF = PATCH // 2
PAIRS_DEV = 4
F32 = jnp.float32
BF16 = jnp.bfloat16
HBM = pltpu.MemorySpace.HBM


def taper(v):
    return np.where(v < HALF, (v + 0.5) / HALF, (PATCH - 0.5 - v) / HALF)


def whole_part(x, divisor):
    return (x.astype(F32) * (1.0 / divisor) + 0.5 / divisor).astype(jnp.int32)


def look_table():
    lane = lax.broadcasted_iota(jnp.int32, (384, 256), 0)
    n = lax.broadcasted_iota(jnp.int32, (384, 256), 1)
    left = jnp.where(lane < 256, lane, 256 + lane % 64)
    right = jnp.where(lane < 256, 64 + lane, lane % 64)
    cell = whole_part(jnp.where(n < 128, left, right), LOOK_C)
    return (cell == n % HALF).astype(F32).astype(BF16)


def row_forward():
    i, k, q, row = np.meshgrid(np.arange(2), np.arange(PATCH), np.arange(2), np.arange(48), indexing="ij")
    u = row - HALF * i
    angle = 2 * np.pi * k * u / PATCH
    value = np.where(q == 0, np.cos(angle), -np.sin(angle)) * ((u >= 0) & (u < PATCH))
    return value.reshape(64, 96)


def col_forward():
    h, c, p, v, c2, p2, l = np.meshgrid(
        np.arange(2), np.arange(2), np.arange(4), np.arange(HALF), np.arange(2), np.arange(4), np.arange(PATCH),
        indexing="ij",
    )
    angle = 2 * np.pi * l * (HALF * h + v) / PATCH
    value = np.where(c == c2, np.cos(angle), np.where(c == 1, np.sin(angle), -np.sin(angle)))
    return (value * (p == p2)).reshape(256, 256)


def neighbour_sum():
    a = lax.broadcasted_iota(jnp.int32, (128, 128), 0)
    b = lax.broadcasted_iota(jnp.int32, (128, 128), 1)
    d = (a - b) & (PATCH - 1)
    near = (d <= 1) | (d == PATCH - 1)
    return (near & ((a & -PATCH) == (b & -PATCH))).astype(F32).astype(BF16)


def row_back():
    c2, r, c, i, k = np.meshgrid(
        np.arange(2), np.arange(HALF), np.arange(2), np.arange(2), np.arange(PATCH), indexing="ij"
    )
    u = r + HALF * (1 - i)
    angle = 2 * np.pi * k * u / PATCH
    value = np.where(c == c2, np.cos(angle), np.where(c2 == 0, -np.sin(angle), np.sin(angle))) * taper(u)
    return value.reshape(32, 128)


def col_back():
    j, p, l, q, p2, c = np.meshgrid(
        np.arange(3), np.arange(4), np.arange(PATCH), np.arange(2), np.arange(4), np.arange(PATCH), indexing="ij"
    )
    v = c + HALF - HALF * j
    angle = 2 * np.pi * l * v / PATCH
    value = np.where(q == 0, np.cos(angle), np.sin(angle)) * taper(v) * ((v >= 0) & (v < PATCH)) * (p == p2)
    return (value / (PATCH * PATCH)).reshape(384, 256)


def split(x):
    hi = x.astype(BF16)
    return hi, (x - hi.astype(F32)).astype(BF16)


def mm(a, b):
    return jnp.dot(a, b, preferred_element_type=F32)


def half_copies(stack_ref, first, out_ref, tile, sem, slot):
    count = out_ref.shape[0]
    return [
        pltpu.make_async_copy(
            stack_ref.at[first : first + count, comp, :, pl.ds(128 * (tile + t), 128)],
            out_ref.at[:, 2 * comp + t],
            sem.at[slot, 2 * comp + t],
        )
        for comp in range(2)
        for t in range(2)
    ]


def lower_lanes(shape):
    return lax.broadcasted_iota(jnp.int32, shape, len(shape) - 1) % 128 < 64


def mixed_tile(real, imag, right):
    turned = pltpu.roll(jnp.where(right, real, imag), 64, 1)
    return jnp.where(lower_lanes(real.shape) == right, turned, jnp.where(right, imag, real))


def half_pair(stack_ref, count, left_ref, right_ref, middle, sem):
    lanes = pl.ds(256, 128)
    copies = [pltpu.make_async_copy(stack_ref.at[:count, :, :, lanes], middle, sem.at[2, 0])]
    copies += half_copies(stack_ref, 0, left_ref, 0, sem, 0)
    copies += half_copies(stack_ref, 0, right_ref, 3, sem, 1)
    for copy in copies:
        copy.start()
    return copies


def half_pair_end(copies, count, left_ref, right_ref, middle):
    copies[0].wait()
    for acq in range(count):
        left_ref[acq, 4] = mixed_tile(middle[acq, 0], middle[acq, 1], False)
        right_ref[acq, 4] = mixed_tile(middle[acq, 0], middle[acq, 1], True)
    for copy in copies[1:]:
        copy.wait()


def odd_date():
    return lax.axis_index("date") % 2


def pack_kernel(stack_ref, out_ref, middle, sem):
    odd = odd_date()
    acqs = pl.ds(odd, SPAN)
    copies = [pltpu.make_async_copy(stack_ref.at[acqs, :, :, pl.ds(256, 128)], middle, sem.at[4])]
    for comp in range(2):
        for t in range(2):
            lanes = pl.ds(pl.multiple_of(128 * (3 * odd + t), 128), 128)
            at = 2 * comp + t
            copies.append(pltpu.make_async_copy(stack_ref.at[acqs, comp, :, lanes], out_ref.at[:, at], sem.at[at]))
    for copy in copies:
        copy.start()
    copies[0].wait()
    for acq in range(SPAN):
        out_ref[acq, 4] = mixed_tile(middle[acq, 0], middle[acq, 1], odd == 1)
    for copy in copies[1:]:
        copy.wait()


def pack(stack):
    return pl.pallas_call(
        pack_kernel,
        out_shape=pltpu.VMEM((SPAN, 5, 80, 128), F32),
        in_specs=[pl.BlockSpec(memory_space=pl.ANY)],
        out_specs=pl.BlockSpec(memory_space=pltpu.VMEM),
        scratch_shapes=[pltpu.VMEM((SPAN, 2, 80, 128), F32), pltpu.SemaphoreType.DMA((5,))],
        compiler_params=pltpu.CompilerParams(vmem_limit_bytes=60000000),
    )(stack)


def cross(a_ref, a, b_ref, b):
    real, imag = [0.0] * 3, [0.0] * 3
    for k in range(LOOK_R):
        rows = pl.ds(k, 16, stride=LOOK_R)
        x = [a_ref[a, t, rows, :] for t in range(5)]
        y = [b_ref[b, t, rows, :] for t in range(5)]
        for t in range(2):
            real[t] += x[t] * y[t] + x[t + 2] * y[t + 2]
            imag[t] += x[t + 2] * y[t] - x[t] * y[t + 2]
        real[2] += x[4] * y[4]
        imag[2] += x[4] * pltpu.roll(y[4], 64, 1)
    imag[2] = jnp.where(lower_lanes((16, 128)), -imag[2], imag[2])
    return jnp.concatenate(real, axis=1), jnp.concatenate(imag, axis=1)


def power(a_ref, a):
    total = [0.0] * 3
    for k in range(LOOK_R):
        x = [a_ref[a, t, pl.ds(k, 16, stride=LOOK_R), :] for t in range(5)]
        for t in range(2):
            total[t] += x[t] * x[t] + x[t + 2] * x[t + 2]
        total[2] += x[4] * x[4]
    return jnp.concatenate(total, axis=1)


def pooled(planes, table):
    high, low = split(jnp.concatenate(planes, axis=0))
    cells = (mm(high, table) + mm(low, table)) * (1.0 / (LOOK_R * LOOK_C))
    return cells.reshape(len(planes), 16, 256)


def pair_lanes():
    return lax.broadcasted_iota(jnp.int32, (16, 128), 1) // HALF


def message(cells, offset):
    group = pair_lanes()
    out = jnp.zeros((16, 128), F32)
    for p in range(PAIRS_DEV):
        for comp in range(2):
            value = cells[2 * p + comp, :, offset : offset + 128]
            out = jnp.where(group == comp * PAIRS_DEV + p, value, out)
    return out


def power_cells(left_cells, right_cells):
    return jnp.where(lower_lanes((16, 128)), left_cells[:, :128], right_cells[:, 128:])


def by_pair(values):
    group = pair_lanes() % PAIRS_DEV
    out = values[0]
    for p in range(1, PAIRS_DEV):
        out = jnp.where(group == p, values[p], out)
    return out


def pair_of(list_ref, group, p):
    return tuple(list_ref[i, PAIRS_DEV * group + p] - 4 * group for i in range(2))


def early_kernel(
    list_ref, stack_ref, left_ref, right_ref, first_ref, second_ref, back_ref, crossing_ref, index_ref, keep, look_out,
    powers, middle, sem,
):
    keep_l, keep_r = keep.at[0], keep.at[1]
    copies = half_pair(stack_ref, 4, keep_l, keep_r, middle, sem)
    table = look_table()
    look_out[...] = table
    date = lax.axis_index("date")
    odd = odd_date() == 1
    before = jnp.maximum(date - 1, 0)
    own = [pair_of(list_ref, date, p) for p in range(PAIRS_DEV)]
    others = [pair_of(list_ref, before, p) for p in range(PAIRS_DEV)]
    crossing_ref[...] = by_pair([jnp.full((16, 128), (b >= 4).astype(jnp.int32)) for a, b in own])
    lane = lax.broadcasted_iota(jnp.int32, (8, 128), 1)
    index = jnp.zeros((8, 128), jnp.int32)
    for p in range(PAIRS_DEV):
        mine = jnp.where(odd, own[p][0], jnp.clip(others[p][1] - 4, 0, 3))
        theirs = jnp.where(odd, jnp.clip(own[p][1] - 4, 0, 2), jnp.clip(others[p][0] - 1, 0, 2))
        index = jnp.where(lane == p, mine, jnp.where(lane == PAIRS_DEV + p, theirs, index))
    index_ref[...] = index
    half_pair_end(copies, 4, keep_l, keep_r, middle)
    planes_l, planes_r = [], []
    for a, b in own:
        planes_l += cross(keep_l, a, keep_l, jnp.minimum(b, 3))
        planes_r += cross(keep_r, a, keep_r, jnp.minimum(b, 3))
    for acq in range(4):
        planes_l.append(power(keep_l, acq))
        planes_r.append(power(keep_r, acq))
    cells_l = pooled(planes_l, table)
    cells_r = pooled(planes_r, table)
    left_ref[...] = message(cells_l, 0)
    right_ref[...] = message(cells_r, 128)
    for acq in range(4):
        powers[acq] = power_cells(cells_l[8 + acq], cells_r[8 + acq])
    first_ref[...] = by_pair([powers[a] for a, b in own])
    second_ref[...] = by_pair([powers[jnp.minimum(b, 3)] for a, b in own])
    back_ref[...] = by_pair([powers[jnp.clip(b - 4, 0, 3)] for a, b in others])


def early(listed, stack):
    vmem = pl.BlockSpec(memory_space=pltpu.VMEM)
    smem = pl.BlockSpec(memory_space=pltpu.SMEM)
    out_shape = [jax.ShapeDtypeStruct((16, 128), F32)] * 5 + [
        jax.ShapeDtypeStruct((16, 128), jnp.int32),
        jax.ShapeDtypeStruct((8, 128), jnp.int32),
        jax.ShapeDtypeStruct((2, 4, 5, 80, 128), F32),
        jax.ShapeDtypeStruct((384, 256), BF16),
    ]
    return pl.pallas_call(
        early_kernel,
        out_shape=out_shape,
        in_specs=[smem, pl.BlockSpec(memory_space=HBM)],
        out_specs=[vmem] * len(out_shape),
        scratch_shapes=[
            pltpu.VMEM((4, 16, 128), F32), pltpu.VMEM((4, 2, 80, 128), F32), pltpu.SemaphoreType.DMA((3, 4)),
        ],
        compiler_params=pltpu.CompilerParams(vmem_limit_bytes=24 * 2**20),
        cost_estimate=pl.CostEstimate(flops=10**9, bytes_accessed=10**7, transcendentals=0),
    )(listed, stack)


def chip_kernel(
    list_ref, other_ref, keep, table_ref, crossing_ref, left_in, right_in, second_in, left_ref, right_ref, second_ref,
    first_swap, second_swap, *scratch,
):
    left_ref[...] = left_in[...]
    right_ref[...] = right_in[...]
    second_ref[...] = second_in[...]

    @pl.when(odd_date() == 0)
    def _():
        other_l, other_r, powers, middle, sem = scratch
        copies = half_pair(other_ref, SPAN, other_l, other_r, middle, sem)
        half_pair_end(copies, SPAN, other_l, other_r, middle)
        date = lax.axis_index("date")
        planes_l, planes_r, seconds = [], [], []
        for p in range(PAIRS_DEV):
            a, b = pair_of(list_ref, date, p)
            seconds.append(jnp.maximum(b - 4, 0))
            planes_l += cross(keep.at[0], a, other_l, seconds[p])
            planes_r += cross(keep.at[1], a, other_r, seconds[p])
        for acq in range(SPAN):
            planes_l.append(power(other_l, acq))
            planes_r.append(power(other_r, acq))
        cells_l = pooled(planes_l, table_ref[...])
        cells_r = pooled(planes_r, table_ref[...])
        crossing = crossing_ref[...] == 1
        left_ref[...] = jnp.where(crossing, message(cells_l, 0), left_in[...])
        right_ref[...] = jnp.where(crossing, message(cells_r, 128), right_in[...])
        for acq in range(SPAN):
            powers[acq] = power_cells(cells_l[8 + acq], cells_r[8 + acq])
        second_ref[...] = jnp.where(crossing, by_pair([powers[b] for b in seconds]), second_in[...])

    odd_col = lax.axis_index("col") % 2 == 1
    left, right = left_ref[...], right_ref[...]
    first_swap[...] = jnp.where(odd_col, left, right)
    second_swap[...] = jnp.where(odd_col, right, left)


def within_chip(listed, other, *arrays):
    vmem = pl.BlockSpec(memory_space=pltpu.VMEM)
    half = pltpu.VMEM((SPAN, 5, 80, 128), F32)
    return pl.pallas_call(
        chip_kernel,
        out_shape=[jax.ShapeDtypeStruct((16, 128), F32)] * 5,
        in_specs=[pl.BlockSpec(memory_space=pltpu.SMEM), pl.BlockSpec(memory_space=HBM)] + [vmem] * 6,
        out_specs=[vmem] * 5,
        scratch_shapes=[
            half, half, pltpu.VMEM((SPAN, 16, 128), F32), pltpu.VMEM((SPAN, 2, 80, 128), F32),
            pltpu.SemaphoreType.DMA((3, 4)),
        ],
        compiler_params=pltpu.CompilerParams(vmem_limit_bytes=24 * 2**20),
        cost_estimate=pl.CostEstimate(flops=10**9, bytes_accessed=10**7, transcendentals=0),
    )(listed, other, *arrays)


def table_kernel(after_ref, trig_ref, ns_out, rf_out, cf_out, rb_out, cb_out):
    ns_out[...] = neighbour_sum()
    for source, target in (
        (trig_ref[:256], cf_out),
        (trig_ref[256:640], cb_out),
        (trig_ref[640:704, :96], rf_out),
        (trig_ref[640:672, 128:], rb_out),
    ):
        high, low = split(source)
        target[0] = high
        target[1] = low


def filter_tables(after):
    vmem = pl.BlockSpec(memory_space=pltpu.VMEM)
    trig = np.zeros((704, 256))
    trig[:256] = col_forward()
    trig[256:640] = col_back()
    trig[640:704, :96] = row_forward()
    trig[640:672, 128:] = row_back()
    out_shape = [jax.ShapeDtypeStruct((128, 128), BF16)] + [
        jax.ShapeDtypeStruct((2,) + shape, BF16) for shape in ((64, 96), (256, 256), (32, 128), (384, 256))
    ]
    return pl.pallas_call(
        table_kernel,
        out_shape=out_shape,
        in_specs=[vmem] * 2,
        out_specs=[vmem] * 5,
        compiler_params=pltpu.CompilerParams(vmem_limit_bytes=16 * 2**20),
        cost_estimate=pl.CostEstimate(flops=10**8, bytes_accessed=10**6, transcendentals=0),
    )(after, jnp.asarray(trig, F32))


def late_kernel(index_ref, other_ref, keep, table_ref, back_in, out_ref):
    odd = odd_date() == 1
    side = jnp.where(odd, 0, 1)
    index = index_ref[...]
    planes = []
    for p in range(PAIRS_DEV):
        planes += cross(keep.at[side], index[0, p], other_ref, index[0, PAIRS_DEV + p])
    cells = pooled(planes, table_ref[...])
    cells = jnp.where(odd, cells[:, :, :128], cells[:, :, 128:])
    new = message(cells, 0)
    out_ref[:16] = jnp.where(odd | lower_lanes((16, 128)), new, -new)
    out_ref[16:] = back_in[...]


def late(*arrays):
    vmem = pl.BlockSpec(memory_space=pltpu.VMEM)
    return pl.pallas_call(
        late_kernel,
        out_shape=jax.ShapeDtypeStruct((32, 128), F32),
        in_specs=[vmem] * 5,
        out_specs=vmem,
        compiler_params=pltpu.CompilerParams(vmem_limit_bytes=24 * 2**20),
    )(*arrays)


def merge_kernel(
    crossing_ref, before_late, right_late, after_late, left_late, first_ref, second_ref, left_early, right_early, mid_ref
):
    crossing = (crossing_ref[...] == 1) & (odd_date() == 1)
    col = lax.axis_index("col")
    odd_col = col % 2 == 1
    before = jnp.where(crossing, before_late[:16], jnp.where(odd_col, first_ref[...], second_ref[...]))
    after = jnp.where(crossing, after_late[:16], jnp.where(odd_col, second_ref[...], first_ref[...]))
    mid_ref[:, :128] = jnp.where(col == 0, 0.0, before)
    mid_ref[:, 128:256] = jnp.where(crossing, left_late[:16], left_early[...])
    mid_ref[:, 256:384] = jnp.where(crossing, right_late[:16], right_early[...])
    mid_ref[:, 384:] = jnp.where(col == lax.axis_size("col") - 1, 0.0, after)


def merge(*arrays):
    vmem = pl.BlockSpec(memory_space=pltpu.VMEM)
    return pl.pallas_call(
        merge_kernel,
        out_shape=jax.ShapeDtypeStruct((16, 512), F32),
        in_specs=[vmem] * 9,
        out_specs=vmem,
        compiler_params=pltpu.CompilerParams(vmem_limit_bytes=8 * 2**20),
    )(*arrays)


def coherence_of(mid_ref, first, second, out_ref):
    lane = lax.broadcasted_iota(jnp.int32, (16, 128), 1)
    squares = []
    for at in (128, 256):
        x = mid_ref[:, at : at + 128]
        squares.append(x * x + pltpu.roll(x * x, 64, 1))
    magnitude = jnp.sqrt(jnp.where(lane < 64, squares[0], squares[1]))
    coherence = magnitude / jnp.sqrt((first + 1e-06) * (second + 1e-06))
    for p in range(PAIRS_DEV):
        left = coherence if p == 0 else pltpu.roll(coherence, 128 - HALF * p, 1)
        right = pltpu.roll(coherence, (HALF + 64 - HALF * p) % 128, 1)
        out_ref[p] = jnp.where(lane < HALF, left, right)[:, :PATCH]


def goldstein_kernel(
    first_swap, mid_ref, second_swap, ns_ref, rf_ref, cf_ref, rb_ref, cb_ref, crossing_ref, first_ref, second_ref, late_ref,
    out_ref, coh_ref,
):
    odd_crossing = (crossing_ref[...] == 1) & (odd_date() == 1)
    coherence_of(mid_ref, first_ref[...], jnp.where(odd_crossing, late_ref[16:], second_ref[...]), coh_ref)
    row = lax.axis_index("row")
    odd_row = row % 2 == 1
    up = jnp.where(odd_row, first_swap[...], second_swap[...])
    down = jnp.where(odd_row, second_swap[...], first_swap[...])
    up = jnp.where(row == 0, 0.0, up)
    down = jnp.where(row == lax.axis_size("row") - 1, 0.0, down)
    x = jnp.concatenate([up, mid_ref[...], down], axis=0)
    lane = lax.broadcasted_iota(jnp.int32, (48, 128), 1)
    sign = jnp.where(lane < 64, -1.0, 1.0)
    turned = [pltpu.roll(x[:, 128 * b : 128 * b + 128], 64, 1) * sign for b in range(4)]
    xx = jnp.concatenate([x, jnp.concatenate(turned, axis=1)], axis=0)
    xh, xl = split(xx)
    rh, rl = rf_ref[0], rf_ref[1]
    y = mm(jnp.concatenate([rh, rh], axis=1), jnp.concatenate([xh, xl], axis=0)) + mm(rl, xh)
    ys = jnp.concatenate([y[:, 128 * j : 128 * j + 256] for j in range(3)], axis=0)
    yh, yl = split(ys)
    ch, cl = cf_ref[0], cf_ref[1]
    z = mm(yh, ch) + (mm(yl, ch) + mm(yh, cl))
    zr, zi = z[:, :128], z[:, 128:]
    magnitude = jnp.sqrt(zr * zr + zi * zi)
    mh, ml = split(magnitude)
    across = mm(jnp.concatenate([mh, ml], axis=1), jnp.concatenate([ns_ref[...], ns_ref[...]], axis=0))
    grouped = across.reshape(6, PATCH, 128)
    down_one = jnp.concatenate([grouped[:, PATCH - 1 :], grouped[:, : PATCH - 1]], axis=1)
    up_one = jnp.concatenate([grouped[:, 1:], grouped[:, :1]], axis=1)
    smooth = (grouped + (down_one + up_one)).reshape(192, 128)
    response = jnp.sqrt(smooth * (1.0 / 9.0)) * (1.0 / PATCH)
    fr, fi = zr * response, zi * response
    w = jnp.concatenate(
        [
            jnp.concatenate([fr[64 * j : 64 * j + 64] for j in range(3)], axis=1),
            jnp.concatenate([fi[64 * j : 64 * j + 64] for j in range(3)], axis=1),
        ],
        axis=0,
    )
    wh, wl = split(w)
    bh, bl = rb_ref[0], rb_ref[1]
    t = mm(jnp.concatenate([bh, bh], axis=1), jnp.concatenate([wh, wl], axis=0)) + mm(bl, wh)
    th, tl = split(t)
    gh, gl = cb_ref[0], cb_ref[1]
    oo = mm(jnp.concatenate([th, tl], axis=0), gh)
    o = oo[:32] + (oo[32:] + mm(th, gl))
    real = o[:16, :128] - o[16:, 128:]
    imag = o[16:, :128] + o[:16, 128:]
    for p in range(PAIRS_DEV):
        out_ref[p, 0] = real[:, PATCH * p : PATCH * p + PATCH]
        out_ref[p, 1] = imag[:, PATCH * p : PATCH * p + PATCH]


def goldstein(*arrays):
    vmem = pl.BlockSpec(memory_space=pltpu.VMEM)
    return pl.pallas_call(
        goldstein_kernel,
        out_shape=(
            jax.ShapeDtypeStruct((PAIRS_DEV, 2, 16, 32), F32), jax.ShapeDtypeStruct((PAIRS_DEV, 16, 32), F32),
        ),
        in_specs=[vmem] * 12,
        out_specs=(vmem, vmem),
        compiler_params=pltpu.CompilerParams(vmem_limit_bytes=24 * 2**20),
    )(*arrays)


def neighbour(i, n, first):
    if first:
        return i ^ 1
    return ((i - 1) ^ 1) + 1 if 0 < i < n - 1 else i


def shards(stack, pair_list):
    names = ("date", "row", "col")
    dates, rows, cols = (lax.axis_size(name) for name in names)

    def send(x, target):
        pairs = []
        for d in range(dates):
            for r in range(rows):
                for c in range(cols):
                    a, b, e = target(d, r, c)
                    pairs.append(((d * rows + r) * cols + c, (a * rows + b) * cols + e))
        return lax.ppermute(x, names, pairs)

    def swap_cols(first):
        def target(d, r, c):
            e = neighbour(c, cols, first)
            return (d, r, e) if e != c else (d, r ^ 1, c)

        return target

    def swap_rows(first):
        def target(d, r, c):
            b = neighbour(r, rows, first)
            return (d, b, c) if b != r else (d, r, c ^ 1)

        return target

    def between_dates(odd_target, even_target):
        def target(d, r, c):
            if d in (0, dates - 1):
                return d, r, c ^ 1
            if d % 2:
                up, e = odd_target(c)
                return d + up, r, e
            down, e = even_target(c)
            return d - down, r, e

        return target

    end = cols - 1
    straight = between_dates(lambda c: (1, c), lambda c: (1, c))
    def ring(d, r, c):
        if d % 2:
            return (d, r, c - 1) if c > 0 else (d - 1, r, c)
        return (d, r, c + 1) if c < end else (d + 1, r, c)

    from_left = between_dates(
        lambda c: (1, 0) if c == 0 else (0, 0) if c == 1 else (1, c - 1) if c < end else (1, end),
        lambda c: (1, c + 1) if c < end else (0, end - 1),
    )

    listed = pair_list.T
    other = send(pack(stack), straight)
    chip = send(stack, lambda d, r, c: (d ^ 1, r, c))
    left, right, first, second, back, crossing, index, keep, look = early(listed, stack)
    left, right, second, one, two = within_chip(listed, chip, keep, look, crossing, left, right, second)
    one = send(one, swap_cols(True))
    two = send(two, swap_cols(False))
    tables = filter_tables(right)
    other, one, two = lax.optimization_barrier((other, one, two))
    new = late(index, other, keep, look, back)
    after = send(new, ring)
    before = send(new, from_left)
    right_late = send(new, straight)
    mid = merge(crossing, before, right_late, after, new, one, two, left, right)
    one = send(mid, swap_rows(True))
    two = send(mid, swap_rows(False))
    return goldstein(one, mid, two, *tables, crossing, first, second, right_late)


def solution(mesh):
    in_specs = (P("date", None, "row", "col"), P())
    out_specs = (P("date", None, "row", "col"), P("date", "row", "col"))
    return jax.shard_map(shards, mesh=mesh, in_specs=in_specs, out_specs=out_specs, check_vma=False)
```

```python
import functools
import math

import jax
import jax.numpy as jnp
import numpy as np
from jax import lax
from jax.experimental import pallas as pl
from jax.experimental.pallas import tpu as pltpu
from jax.sharding import PartitionSpec as P

SPAN = 3
LOOK_R = 5
LOOK_C = 20
PATCH = 32
HALF = PATCH // 2
PAIRS_DEV = 4
F32 = jnp.float32
BF16 = jnp.bfloat16
HBM = pltpu.MemorySpace.HBM


def taper(v):
    return np.where(v < HALF, (v + 0.5) / HALF, (PATCH - 0.5 - v) / HALF)


def whole_part(x, divisor):
    return (x.astype(F32) * (1.0 / divisor) + 0.5 / divisor).astype(jnp.int32)


def look_table():
    lane = lax.broadcasted_iota(jnp.int32, (384, 256), 0)
    n = lax.broadcasted_iota(jnp.int32, (384, 256), 1)
    left = jnp.where(lane < 256, lane, 256 + lane % 64)
    right = jnp.where(lane < 256, 64 + lane, lane % 64)
    cell = whole_part(jnp.where(n < 128, left, right), LOOK_C)
    return (cell == n % HALF).astype(F32).astype(BF16)


def row_forward():
    i, k, q, row = np.meshgrid(np.arange(2), np.arange(PATCH), np.arange(2), np.arange(48), indexing="ij")
    u = row - HALF * i
    angle = 2 * np.pi * k * u / PATCH
    value = np.where(q == 0, np.cos(angle), -np.sin(angle)) * ((u >= 0) & (u < PATCH))
    return value.reshape(64, 96)


def col_forward():
    h, c, p, v, c2, p2, l = np.meshgrid(
        np.arange(2), np.arange(2), np.arange(4), np.arange(HALF), np.arange(2), np.arange(4), np.arange(PATCH),
        indexing="ij",
    )
    angle = 2 * np.pi * l * (HALF * h + v) / PATCH
    value = np.where(c == c2, np.cos(angle), np.where(c == 1, np.sin(angle), -np.sin(angle)))
    return (value * (p == p2)).reshape(256, 256)


def neighbour_sum():
    a = lax.broadcasted_iota(jnp.int32, (128, 128), 0)
    b = lax.broadcasted_iota(jnp.int32, (128, 128), 1)
    d = (a - b) & (PATCH - 1)
    near = (d <= 1) | (d == PATCH - 1)
    return (near & ((a & -PATCH) == (b & -PATCH))).astype(F32).astype(BF16)


def row_back():
    c2, r, c, i, k = np.meshgrid(
        np.arange(2), np.arange(HALF), np.arange(2), np.arange(2), np.arange(PATCH), indexing="ij"
    )
    u = r + HALF * (1 - i)
    angle = 2 * np.pi * k * u / PATCH
    value = np.where(c == c2, np.cos(angle), np.where(c2 == 0, -np.sin(angle), np.sin(angle))) * taper(u)
    return value.reshape(32, 128)


def col_back():
    j, p, l, q, p2, c = np.meshgrid(
        np.arange(3), np.arange(4), np.arange(PATCH), np.arange(2), np.arange(4), np.arange(PATCH), indexing="ij"
    )
    v = c + HALF - HALF * j
    angle = 2 * np.pi * l * v / PATCH
    value = np.where(q == 0, np.cos(angle), np.sin(angle)) * taper(v) * ((v >= 0) & (v < PATCH)) * (p == p2)
    return (value / (PATCH * PATCH)).reshape(384, 256)


def split(x):
    hi = x.astype(BF16)
    return hi, (x - hi.astype(F32)).astype(BF16)


def mm(a, b):
    return jnp.dot(a, b, preferred_element_type=F32)


def half_copies(stack_ref, first, out_ref, tile, sem, slot):
    count = out_ref.shape[0]
    return [
        pltpu.make_async_copy(
            stack_ref.at[first : first + count, comp, :, pl.ds(128 * (tile + t), 128)],
            out_ref.at[:, 2 * comp + t],
            sem.at[slot, 2 * comp + t],
        )
        for comp in range(2)
        for t in range(2)
    ]


def lower_lanes(shape):
    return lax.broadcasted_iota(jnp.int32, shape, len(shape) - 1) % 128 < 64


def mixed_tile(real, imag, right):
    turned = pltpu.roll(jnp.where(right, real, imag), 64, 1)
    return jnp.where(lower_lanes(real.shape) == right, turned, jnp.where(right, imag, real))


def half_pair(stack_ref, count, left_ref, right_ref, middle, sem):
    lanes = pl.ds(256, 128)
    copies = [pltpu.make_async_copy(stack_ref.at[:count, :, :, lanes], middle, sem.at[2, 0])]
    copies += half_copies(stack_ref, 0, left_ref, 0, sem, 0)
    copies += half_copies(stack_ref, 0, right_ref, 3, sem, 1)
    for copy in copies:
        copy.start()
    return copies


def half_pair_end(copies, count, left_ref, right_ref, middle):
    copies[0].wait()
    for acq in range(count):
        left_ref[acq, 4] = mixed_tile(middle[acq, 0], middle[acq, 1], False)
        right_ref[acq, 4] = mixed_tile(middle[acq, 0], middle[acq, 1], True)
    for copy in copies[1:]:
        copy.wait()


def odd_date():
    return lax.axis_index("date") % 2


def pack_kernel(stack_ref, out_ref, middle, sem):
    odd = odd_date()
    acqs = pl.ds(odd, SPAN)
    copies = [pltpu.make_async_copy(stack_ref.at[acqs, :, :, pl.ds(256, 128)], middle, sem.at[4])]
    for comp in range(2):
        for t in range(2):
            lanes = pl.ds(pl.multiple_of(128 * (3 * odd + t), 128), 128)
            at = 2 * comp + t
            copies.append(pltpu.make_async_copy(stack_ref.at[acqs, comp, :, lanes], out_ref.at[:, at], sem.at[at]))
    for copy in copies:
        copy.start()
    copies[0].wait()
    for acq in range(SPAN):
        out_ref[acq, 4] = mixed_tile(middle[acq, 0], middle[acq, 1], odd == 1)
    for copy in copies[1:]:
        copy.wait()


def pack(stack):
    return pl.pallas_call(
        pack_kernel,
        out_shape=pltpu.VMEM((SPAN, 5, 80, 128), F32),
        in_specs=[pl.BlockSpec(memory_space=pl.ANY)],
        out_specs=pl.BlockSpec(memory_space=pltpu.VMEM),
        scratch_shapes=[pltpu.VMEM((SPAN, 2, 80, 128), F32), pltpu.SemaphoreType.DMA((5,))],
        compiler_params=pltpu.CompilerParams(vmem_limit_bytes=60000000),
    )(stack)


def cross(a_ref, a, b_ref, b):
    real, imag = [0.0] * 3, [0.0] * 3
    for k in range(LOOK_R):
        rows = pl.ds(k, 16, stride=LOOK_R)
        x = [a_ref[a, t, rows, :] for t in range(5)]
        y = [b_ref[b, t, rows, :] for t in range(5)]
        for t in range(2):
            real[t] += x[t] * y[t] + x[t + 2] * y[t + 2]
            imag[t] += x[t + 2] * y[t] - x[t] * y[t + 2]
        real[2] += x[4] * y[4]
        imag[2] += x[4] * pltpu.roll(y[4], 64, 1)
    imag[2] = jnp.where(lower_lanes((16, 128)), -imag[2], imag[2])
    return jnp.concatenate(real, axis=1), jnp.concatenate(imag, axis=1)


def power(a_ref, a):
    total = [0.0] * 3
    for k in range(LOOK_R):
        x = [a_ref[a, t, pl.ds(k, 16, stride=LOOK_R), :] for t in range(5)]
        for t in range(2):
            total[t] += x[t] * x[t] + x[t + 2] * x[t + 2]
        total[2] += x[4] * x[4]
    return jnp.concatenate(total, axis=1)


def pooled(planes, table):
    high, low = split(jnp.concatenate(planes, axis=0))
    cells = (mm(high, table) + mm(low, table)) * (1.0 / (LOOK_R * LOOK_C))
    return cells.reshape(len(planes), 16, 256)


def pair_lanes():
    return lax.broadcasted_iota(jnp.int32, (16, 128), 1) // HALF


def message(cells, offset):
    group = pair_lanes()
    out = jnp.zeros((16, 128), F32)
    for p in range(PAIRS_DEV):
        for comp in range(2):
            value = cells[2 * p + comp, :, offset : offset + 128]
            out = jnp.where(group == comp * PAIRS_DEV + p, value, out)
    return out


def power_cells(left_cells, right_cells):
    return jnp.where(lower_lanes((16, 128)), left_cells[:, :128], right_cells[:, 128:])


def by_pair(values):
    group = pair_lanes() % PAIRS_DEV
    out = values[0]
    for p in range(1, PAIRS_DEV):
        out = jnp.where(group == p, values[p], out)
    return out


def pair_of(list_ref, group, p):
    return tuple(list_ref[i, PAIRS_DEV * group + p] - 4 * group for i in range(2))


def early_kernel(
    list_ref, stack_ref, left_ref, right_ref, first_ref, second_ref, back_ref, crossing_ref, index_ref, keep, look_out,
    powers, middle, sem,
):
    keep_l, keep_r = keep.at[0], keep.at[1]
    copies = half_pair(stack_ref, 4, keep_l, keep_r, middle, sem)
    table = look_table()
    look_out[...] = table
    date = lax.axis_index("date")
    odd = odd_date() == 1
    before = jnp.maximum(date - 1, 0)
    own = [pair_of(list_ref, date, p) for p in range(PAIRS_DEV)]
    others = [pair_of(list_ref, before, p) for p in range(PAIRS_DEV)]
    crossing_ref[...] = by_pair([jnp.full((16, 128), (b >= 4).astype(jnp.int32)) for a, b in own])
    lane = lax.broadcasted_iota(jnp.int32, (8, 128), 1)
    index = jnp.zeros((8, 128), jnp.int32)
    for p in range(PAIRS_DEV):
        mine = jnp.where(odd, own[p][0], jnp.clip(others[p][1] - 4, 0, 3))
        theirs = jnp.where(odd, jnp.clip(own[p][1] - 4, 0, 2), jnp.clip(others[p][0] - 1, 0, 2))
        index = jnp.where(lane == p, mine, jnp.where(lane == PAIRS_DEV + p, theirs, index))
    index_ref[...] = index
    half_pair_end(copies, 4, keep_l, keep_r, middle)
    planes_l, planes_r = [], []
    for a, b in own:
        planes_l += cross(keep_l, a, keep_l, jnp.minimum(b, 3))
        planes_r += cross(keep_r, a, keep_r, jnp.minimum(b, 3))
    for acq in range(4):
        planes_l.append(power(keep_l, acq))
        planes_r.append(power(keep_r, acq))
    cells_l = pooled(planes_l, table)
    cells_r = pooled(planes_r, table)
    left_ref[...] = message(cells_l, 0)
    right_ref[...] = message(cells_r, 128)
    for acq in range(4):
        powers[acq] = power_cells(cells_l[8 + acq], cells_r[8 + acq])
    first_ref[...] = by_pair([powers[a] for a, b in own])
    second_ref[...] = by_pair([powers[jnp.minimum(b, 3)] for a, b in own])
    back_ref[...] = by_pair([powers[jnp.clip(b - 4, 0, 3)] for a, b in others])


def early(listed, stack):
    vmem = pl.BlockSpec(memory_space=pltpu.VMEM)
    smem = pl.BlockSpec(memory_space=pltpu.SMEM)
    out_shape = [jax.ShapeDtypeStruct((16, 128), F32)] * 5 + [
        jax.ShapeDtypeStruct((16, 128), jnp.int32),
        jax.ShapeDtypeStruct((8, 128), jnp.int32),
        jax.ShapeDtypeStruct((2, 4, 5, 80, 128), F32),
        jax.ShapeDtypeStruct((384, 256), BF16),
    ]
    return pl.pallas_call(
        early_kernel,
        out_shape=out_shape,
        in_specs=[smem, pl.BlockSpec(memory_space=HBM)],
        out_specs=[vmem] * len(out_shape),
        scratch_shapes=[
            pltpu.VMEM((4, 16, 128), F32), pltpu.VMEM((4, 2, 80, 128), F32), pltpu.SemaphoreType.DMA((3, 4)),
        ],
        compiler_params=pltpu.CompilerParams(vmem_limit_bytes=24 * 2**20),
        cost_estimate=pl.CostEstimate(flops=10**9, bytes_accessed=10**7, transcendentals=0),
    )(listed, stack)


def chip_kernel(
    list_ref, other_ref, keep, table_ref, crossing_ref, left_in, right_in, second_in, left_ref, right_ref, second_ref,
    first_swap, second_swap, *scratch,
):
    left_ref[...] = left_in[...]
    right_ref[...] = right_in[...]
    second_ref[...] = second_in[...]

    @pl.when(odd_date() == 0)
    def _():
        other_l, other_r, powers, middle, sem = scratch
        copies = half_pair(other_ref, SPAN, other_l, other_r, middle, sem)
        half_pair_end(copies, SPAN, other_l, other_r, middle)
        date = lax.axis_index("date")
        planes_l, planes_r, seconds = [], [], []
        for p in range(PAIRS_DEV):
            a, b = pair_of(list_ref, date, p)
            seconds.append(jnp.maximum(b - 4, 0))
            planes_l += cross(keep.at[0], a, other_l, seconds[p])
            planes_r += cross(keep.at[1], a, other_r, seconds[p])
        for acq in range(SPAN):
            planes_l.append(power(other_l, acq))
            planes_r.append(power(other_r, acq))
        cells_l = pooled(planes_l, table_ref[...])
        cells_r = pooled(planes_r, table_ref[...])
        crossing = crossing_ref[...] == 1
        left_ref[...] = jnp.where(crossing, message(cells_l, 0), left_in[...])
        right_ref[...] = jnp.where(crossing, message(cells_r, 128), right_in[...])
        for acq in range(SPAN):
            powers[acq] = power_cells(cells_l[8 + acq], cells_r[8 + acq])
        second_ref[...] = jnp.where(crossing, by_pair([powers[b] for b in seconds]), second_in[...])

    odd_col = lax.axis_index("col") % 2 == 1
    left, right = left_ref[...], right_ref[...]
    first_swap[...] = jnp.where(odd_col, left, right)
    second_swap[...] = jnp.where(odd_col, right, left)


def within_chip(listed, other, *arrays):
    vmem = pl.BlockSpec(memory_space=pltpu.VMEM)
    half = pltpu.VMEM((SPAN, 5, 80, 128), F32)
    return pl.pallas_call(
        chip_kernel,
        out_shape=[jax.ShapeDtypeStruct((16, 128), F32)] * 5,
        in_specs=[pl.BlockSpec(memory_space=pltpu.SMEM), pl.BlockSpec(memory_space=HBM)] + [vmem] * 6,
        out_specs=[vmem] * 5,
        scratch_shapes=[
            half, half, pltpu.VMEM((SPAN, 16, 128), F32), pltpu.VMEM((SPAN, 2, 80, 128), F32),
            pltpu.SemaphoreType.DMA((3, 4)),
        ],
        compiler_params=pltpu.CompilerParams(vmem_limit_bytes=24 * 2**20),
        cost_estimate=pl.CostEstimate(flops=10**9, bytes_accessed=10**7, transcendentals=0),
    )(listed, other, *arrays)


def table_kernel(after_ref, trig_ref, ns_out, rf_out, cf_out, rb_out, cb_out):
    ns_out[...] = neighbour_sum()
    for source, target in (
        (trig_ref[:256], cf_out),
        (trig_ref[256:640], cb_out),
        (trig_ref[640:704, :96], rf_out),
        (trig_ref[640:672, 128:], rb_out),
    ):
        high, low = split(source)
        target[0] = high
        target[1] = low


def filter_tables(after):
    vmem = pl.BlockSpec(memory_space=pltpu.VMEM)
    trig = np.zeros((704, 256))
    trig[:256] = col_forward()
    trig[256:640] = col_back()
    trig[640:704, :96] = row_forward()
    trig[640:672, 128:] = row_back()
    out_shape = [jax.ShapeDtypeStruct((128, 128), BF16)] + [
        jax.ShapeDtypeStruct((2,) + shape, BF16) for shape in ((64, 96), (256, 256), (32, 128), (384, 256))
    ]
    return pl.pallas_call(
        table_kernel,
        out_shape=out_shape,
        in_specs=[vmem] * 2,
        out_specs=[vmem] * 5,
        compiler_params=pltpu.CompilerParams(vmem_limit_bytes=16 * 2**20),
        cost_estimate=pl.CostEstimate(flops=10**8, bytes_accessed=10**6, transcendentals=0),
    )(after, jnp.asarray(trig, F32))


def late_kernel(index_ref, other_ref, keep, table_ref, back_in, new_ref, out_ref):
    odd = odd_date() == 1
    side = jnp.where(odd, 0, 1)
    index = index_ref[...]
    planes = []
    for p in range(PAIRS_DEV):
        planes += cross(keep.at[side], index[0, p], other_ref, index[0, PAIRS_DEV + p])
    table = table_ref[:, pl.ds(pl.multiple_of(128 * side, 128), 128)]
    high, low = split(jnp.concatenate(planes, axis=0))
    cells = mm(high, table) + mm(low, table)
    new = message(cells.reshape(len(planes), 16, 128), 0) * (1.0 / (LOOK_R * LOOK_C))
    new = jnp.where(odd | lower_lanes((16, 128)), new, -new)
    new_ref[...] = new
    out_ref[:16] = new
    out_ref[16:] = back_in[...]


def late(*arrays):
    vmem = pl.BlockSpec(memory_space=pltpu.VMEM)
    return pl.pallas_call(
        late_kernel,
        out_shape=(jax.ShapeDtypeStruct((16, 128), F32), jax.ShapeDtypeStruct((32, 128), F32)),
        in_specs=[vmem] * 5,
        out_specs=(vmem, vmem),
        compiler_params=pltpu.CompilerParams(vmem_limit_bytes=24 * 2**20),
    )(*arrays)


def merge_kernel(
    crossing_ref, before_late, right_late, after_late, left_late, first_ref, second_ref, left_early, right_early, mid_ref
):
    crossing = (crossing_ref[...] == 1) & (odd_date() == 1)
    col = lax.axis_index("col")
    odd_col = col % 2 == 1
    before = jnp.where(crossing, before_late[:16], jnp.where(odd_col, first_ref[...], second_ref[...]))
    after = jnp.where(crossing, after_late[...], jnp.where(odd_col, second_ref[...], first_ref[...]))
    mid_ref[:, :128] = jnp.where(col == 0, 0.0, before)
    mid_ref[:, 128:256] = jnp.where(crossing, left_late[...], left_early[...])
    mid_ref[:, 256:384] = jnp.where(crossing, right_late[:16], right_early[...])
    mid_ref[:, 384:] = jnp.where(col == lax.axis_size("col") - 1, 0.0, after)


def merge(*arrays):
    vmem = pl.BlockSpec(memory_space=pltpu.VMEM)
    return pl.pallas_call(
        merge_kernel,
        out_shape=jax.ShapeDtypeStruct((16, 512), F32),
        in_specs=[vmem] * 9,
        out_specs=vmem,
        compiler_params=pltpu.CompilerParams(vmem_limit_bytes=8 * 2**20),
    )(*arrays)


def coherence_of(mid_ref, first, second, out_ref):
    lane = lax.broadcasted_iota(jnp.int32, (16, 128), 1)
    squares = []
    for at in (128, 256):
        x = mid_ref[:, at : at + 128]
        squares.append(x * x + pltpu.roll(x * x, 64, 1))
    magnitude = jnp.sqrt(jnp.where(lane < 64, squares[0], squares[1]))
    coherence = magnitude / jnp.sqrt((first + 1e-06) * (second + 1e-06))
    for p in range(PAIRS_DEV):
        left = coherence if p == 0 else pltpu.roll(coherence, 128 - HALF * p, 1)
        right = pltpu.roll(coherence, (HALF + 64 - HALF * p) % 128, 1)
        out_ref[p] = jnp.where(lane < HALF, left, right)[:, :PATCH]


def goldstein_kernel(
    first_swap, mid_ref, second_swap, ns_ref, rf_ref, cf_ref, rb_ref, cb_ref, crossing_ref, first_ref, second_ref, late_ref,
    out_ref, coh_ref,
):
    odd_crossing = (crossing_ref[...] == 1) & (odd_date() == 1)
    coherence_of(mid_ref, first_ref[...], jnp.where(odd_crossing, late_ref[16:], second_ref[...]), coh_ref)
    row = lax.axis_index("row")
    odd_row = row % 2 == 1
    up = jnp.where(odd_row, first_swap[...], second_swap[...])
    down = jnp.where(odd_row, second_swap[...], first_swap[...])
    up = jnp.where(row == 0, 0.0, up)
    down = jnp.where(row == lax.axis_size("row") - 1, 0.0, down)
    x = jnp.concatenate([up, mid_ref[...], down], axis=0)
    lane = lax.broadcasted_iota(jnp.int32, (48, 128), 1)
    sign = jnp.where(lane < 64, -1.0, 1.0)
    turned = [pltpu.roll(x[:, 128 * b : 128 * b + 128], 64, 1) * sign for b in range(4)]
    xx = jnp.concatenate([x, jnp.concatenate(turned, axis=1)], axis=0)
    xh, xl = split(xx)
    rh, rl = rf_ref[0], rf_ref[1]
    y = mm(jnp.concatenate([rh, rh], axis=1), jnp.concatenate([xh, xl], axis=0)) + mm(rl, xh)
    ys = jnp.concatenate([y[:, 128 * j : 128 * j + 256] for j in range(3)], axis=0)
    yh, yl = split(ys)
    ch, cl = cf_ref[0], cf_ref[1]
    z = mm(yh, ch) + (mm(yl, ch) + mm(yh, cl))
    zr, zi = z[:, :128], z[:, 128:]
    magnitude = jnp.sqrt(zr * zr + zi * zi)
    mh, ml = split(magnitude)
    across = mm(jnp.concatenate([mh, ml], axis=1), jnp.concatenate([ns_ref[...], ns_ref[...]], axis=0))
    grouped = across.reshape(6, PATCH, 128)
    down_one = jnp.concatenate([grouped[:, PATCH - 1 :], grouped[:, : PATCH - 1]], axis=1)
    up_one = jnp.concatenate([grouped[:, 1:], grouped[:, :1]], axis=1)
    smooth = (grouped + (down_one + up_one)).reshape(192, 128)
    response = jnp.sqrt(smooth * (1.0 / 9.0)) * (1.0 / PATCH)
    fr, fi = zr * response, zi * response
    w = jnp.concatenate(
        [
            jnp.concatenate([fr[64 * j : 64 * j + 64] for j in range(3)], axis=1),
            jnp.concatenate([fi[64 * j : 64 * j + 64] for j in range(3)], axis=1),
        ],
        axis=0,
    )
    wh, wl = split(w)
    bh, bl = rb_ref[0], rb_ref[1]
    t = mm(jnp.concatenate([bh, bh], axis=1), jnp.concatenate([wh, wl], axis=0)) + mm(bl, wh)
    th, tl = split(t)
    gh, gl = cb_ref[0], cb_ref[1]
    oo = mm(jnp.concatenate([th, tl], axis=0), gh)
    o = oo[:32] + (oo[32:] + mm(th, gl))
    real = o[:16, :128] - o[16:, 128:]
    imag = o[16:, :128] + o[:16, 128:]
    for p in range(PAIRS_DEV):
        out_ref[p, 0] = real[:, PATCH * p : PATCH * p + PATCH]
        out_ref[p, 1] = imag[:, PATCH * p : PATCH * p + PATCH]


def goldstein(*arrays):
    vmem = pl.BlockSpec(memory_space=pltpu.VMEM)
    return pl.pallas_call(
        goldstein_kernel,
        out_shape=(
            jax.ShapeDtypeStruct((PAIRS_DEV, 2, 16, 32), F32), jax.ShapeDtypeStruct((PAIRS_DEV, 16, 32), F32),
        ),
        in_specs=[vmem] * 12,
        out_specs=(vmem, vmem),
        compiler_params=pltpu.CompilerParams(vmem_limit_bytes=24 * 2**20),
    )(*arrays)


def neighbour(i, n, first):
    if first:
        return i ^ 1
    return ((i - 1) ^ 1) + 1 if 0 < i < n - 1 else i


def shards(stack, pair_list):
    names = ("date", "row", "col")
    dates, rows, cols = (lax.axis_size(name) for name in names)

    def send(x, target):
        pairs = []
        for d in range(dates):
            for r in range(rows):
                for c in range(cols):
                    a, b, e = target(d, r, c)
                    pairs.append(((d * rows + r) * cols + c, (a * rows + b) * cols + e))
        return lax.ppermute(x, names, pairs)

    def swap_cols(first):
        def target(d, r, c):
            e = neighbour(c, cols, first)
            return (d, r, e) if e != c else (d, r ^ 1, c)

        return target

    def swap_rows(first):
        def target(d, r, c):
            b = neighbour(r, rows, first)
            return (d, b, c) if b != r else (d, r, c ^ 1)

        return target

    def between_dates(odd_target, even_target):
        def target(d, r, c):
            if d in (0, dates - 1):
                return d, r, c ^ 1
            if d % 2:
                up, e = odd_target(c)
                return d + up, r, e
            down, e = even_target(c)
            return d - down, r, e

        return target

    end = cols - 1
    straight = between_dates(lambda c: (1, c), lambda c: (1, c))
    def ring(d, r, c):
        if d % 2:
            return (d, r, c - 1) if c > 0 else (d - 1, r, c)
        return (d, r, c + 1) if c < end else (d + 1, r, c)

    from_left = between_dates(
        lambda c: (1, 0) if c == 0 else (0, 0) if c == 1 else (1, c - 1) if c < end else (1, end),
        lambda c: (1, c + 1) if c < end else (0, end - 1),
    )

    listed = pair_list.T
    other = send(pack(stack), straight)
    chip = send(stack, lambda d, r, c: (d ^ 1, r, c))
    left, right, first, second, back, crossing, index, keep, look = early(listed, stack)
    left, right, second, one, two = within_chip(listed, chip, keep, look, crossing, left, right, second)
    one = send(one, swap_cols(True))
    two = send(two, swap_cols(False))
    tables = filter_tables(right)
    other, one, two = lax.optimization_barrier((other, one, two))
    new, with_powers = late(index, other, keep, look, back)
    after = send(new, ring)
    before = send(with_powers, from_left)
    right_late = send(with_powers, straight)
    mid = merge(crossing, before, right_late, after, new, one, two, left, right)
    one = send(mid, swap_rows(True))
    two = send(mid, swap_rows(False))
    return goldstein(one, mid, two, *tables, crossing, first, second, right_late)


def solution(mesh):
    in_specs = (P("date", None, "row", "col"), P())
    out_specs = (P("date", None, "row", "col"), P("date", "row", "col"))
    return jax.shard_map(shards, mesh=mesh, in_specs=in_specs, out_specs=out_specs, check_vma=False)
```

```python
import functools
import math

import jax
import jax.numpy as jnp
import numpy as np
from jax import lax
from jax.experimental import pallas as pl
from jax.experimental.pallas import tpu as pltpu
from jax.sharding import PartitionSpec as P

SPAN = 3
LOOK_R = 5
LOOK_C = 20
PATCH = 32
HALF = PATCH // 2
PAIRS_DEV = 4
F32 = jnp.float32
BF16 = jnp.bfloat16
HBM = pltpu.MemorySpace.HBM


def taper(v):
    return np.where(v < HALF, (v + 0.5) / HALF, (PATCH - 0.5 - v) / HALF)


def whole_part(x, divisor):
    return (x.astype(F32) * (1.0 / divisor) + 0.5 / divisor).astype(jnp.int32)


def look_table():
    lane = lax.broadcasted_iota(jnp.int32, (384, 256), 0)
    n = lax.broadcasted_iota(jnp.int32, (384, 256), 1)
    left = jnp.where(lane < 256, lane, 256 + lane % 64)
    right = jnp.where(lane < 256, 64 + lane, lane % 64)
    cell = whole_part(jnp.where(n < 128, left, right), LOOK_C)
    return (cell == n % HALF).astype(F32).astype(BF16)


def row_forward():
    i, k, q, row = np.meshgrid(np.arange(2), np.arange(PATCH), np.arange(2), np.arange(48), indexing="ij")
    u = row - HALF * i
    angle = 2 * np.pi * k * u / PATCH
    value = np.where(q == 0, np.cos(angle), -np.sin(angle)) * ((u >= 0) & (u < PATCH))
    return value.reshape(64, 96)


def col_forward():
    h, c, p, v, c2, p2, l = np.meshgrid(
        np.arange(2), np.arange(2), np.arange(4), np.arange(HALF), np.arange(2), np.arange(4), np.arange(PATCH),
        indexing="ij",
    )
    angle = 2 * np.pi * l * (HALF * h + v) / PATCH
    value = np.where(c == c2, np.cos(angle), np.where(c == 1, np.sin(angle), -np.sin(angle)))
    return (value * (p == p2)).reshape(256, 256)


def neighbour_sum():
    a = lax.broadcasted_iota(jnp.int32, (128, 128), 0)
    b = lax.broadcasted_iota(jnp.int32, (128, 128), 1)
    d = (a - b) & (PATCH - 1)
    near = (d <= 1) | (d == PATCH - 1)
    return (near & ((a & -PATCH) == (b & -PATCH))).astype(F32).astype(BF16)


def row_back():
    c2, r, c, i, k = np.meshgrid(
        np.arange(2), np.arange(HALF), np.arange(2), np.arange(2), np.arange(PATCH), indexing="ij"
    )
    u = r + HALF * (1 - i)
    angle = 2 * np.pi * k * u / PATCH
    value = np.where(c == c2, np.cos(angle), np.where(c2 == 0, -np.sin(angle), np.sin(angle))) * taper(u)
    return value.reshape(32, 128)


def col_back():
    j, p, l, q, p2, c = np.meshgrid(
        np.arange(3), np.arange(4), np.arange(PATCH), np.arange(2), np.arange(4), np.arange(PATCH), indexing="ij"
    )
    v = c + HALF - HALF * j
    angle = 2 * np.pi * l * v / PATCH
    value = np.where(q == 0, np.cos(angle), np.sin(angle)) * taper(v) * ((v >= 0) & (v < PATCH)) * (p == p2)
    return (value / (PATCH * PATCH)).reshape(384, 256)


def split(x):
    hi = x.astype(BF16)
    return hi, (x - hi.astype(F32)).astype(BF16)


def mm(a, b):
    return jnp.dot(a, b, preferred_element_type=F32)


def half_copies(stack_ref, first, out_ref, tile, sem, slot):
    count = out_ref.shape[0]
    return [
        pltpu.make_async_copy(
            stack_ref.at[first : first + count, comp, :, pl.ds(128 * (tile + t), 128)],
            out_ref.at[:, 2 * comp + t],
            sem.at[slot, 2 * comp + t],
        )
        for comp in range(2)
        for t in range(2)
    ]


def lower_lanes(shape):
    return lax.broadcasted_iota(jnp.int32, shape, len(shape) - 1) % 128 < 64


def mixed_tile(real, imag, right):
    turned = pltpu.roll(jnp.where(right, real, imag), 64, 1)
    return jnp.where(lower_lanes(real.shape) == right, turned, jnp.where(right, imag, real))


def half_pair(stack_ref, count, left_ref, right_ref, middle, sem):
    lanes = pl.ds(256, 128)
    copies = [pltpu.make_async_copy(stack_ref.at[:count, :, :, lanes], middle, sem.at[2, 0])]
    copies += half_copies(stack_ref, 0, left_ref, 0, sem, 0)
    copies += half_copies(stack_ref, 0, right_ref, 3, sem, 1)
    for copy in copies:
        copy.start()
    return copies


def half_pair_end(copies, count, left_ref, right_ref, middle):
    copies[0].wait()
    for acq in range(count):
        left_ref[acq, 4] = mixed_tile(middle[acq, 0], middle[acq, 1], False)
        right_ref[acq, 4] = mixed_tile(middle[acq, 0], middle[acq, 1], True)
    for copy in copies[1:]:
        copy.wait()


def odd_date():
    return lax.axis_index("date") % 2


def pack_kernel(stack_ref, out_ref, middle, sem):
    odd = odd_date()
    acqs = pl.ds(odd, SPAN)
    copies = [pltpu.make_async_copy(stack_ref.at[acqs, :, :, pl.ds(256, 128)], middle, sem.at[4])]
    for comp in range(2):
        for t in range(2):
            lanes = pl.ds(pl.multiple_of(128 * (3 * odd + t), 128), 128)
            at = 2 * comp + t
            copies.append(pltpu.make_async_copy(stack_ref.at[acqs, comp, :, lanes], out_ref.at[:, at], sem.at[at]))
    for copy in copies:
        copy.start()
    copies[0].wait()
    for acq in range(SPAN):
        out_ref[acq, 4] = mixed_tile(middle[acq, 0], middle[acq, 1], odd == 1)
    for copy in copies[1:]:
        copy.wait()


def pack(stack):
    return pl.pallas_call(
        pack_kernel,
        out_shape=pltpu.VMEM((SPAN, 5, 80, 128), F32),
        in_specs=[pl.BlockSpec(memory_space=pl.ANY)],
        out_specs=pl.BlockSpec(memory_space=pltpu.VMEM),
        scratch_shapes=[pltpu.VMEM((SPAN, 2, 80, 128), F32), pltpu.SemaphoreType.DMA((5,))],
        compiler_params=pltpu.CompilerParams(vmem_limit_bytes=60000000),
    )(stack)


def cross(a_ref, a, b_ref, b):
    real, imag = [0.0] * 3, [0.0] * 3
    for k in range(LOOK_R):
        rows = pl.ds(k, 16, stride=LOOK_R)
        x = [a_ref[a, t, rows, :] for t in range(5)]
        y = [b_ref[b, t, rows, :] for t in range(5)]
        for t in range(2):
            real[t] += x[t] * y[t] + x[t + 2] * y[t + 2]
            imag[t] += x[t + 2] * y[t] - x[t] * y[t + 2]
        real[2] += x[4] * y[4]
        imag[2] += x[4] * pltpu.roll(y[4], 64, 1)
    imag[2] = jnp.where(lower_lanes((16, 128)), -imag[2], imag[2])
    return jnp.concatenate(real, axis=1), jnp.concatenate(imag, axis=1)


def power(a_ref, a):
    total = [0.0] * 3
    for k in range(LOOK_R):
        x = [a_ref[a, t, pl.ds(k, 16, stride=LOOK_R), :] for t in range(5)]
        for t in range(2):
            total[t] += x[t] * x[t] + x[t + 2] * x[t + 2]
        total[2] += x[4] * x[4]
    return jnp.concatenate(total, axis=1)


def pooled(planes, table):
    high, low = split(jnp.concatenate(planes, axis=0))
    cells = (mm(high, table) + mm(low, table)) * (1.0 / (LOOK_R * LOOK_C))
    return cells.reshape(len(planes), 16, 256)


def pair_lanes():
    return lax.broadcasted_iota(jnp.int32, (16, 128), 1) // HALF


def message(cells, offset):
    group = pair_lanes()
    out = jnp.zeros((16, 128), F32)
    for p in range(PAIRS_DEV):
        for comp in range(2):
            value = cells[2 * p + comp, :, offset : offset + 128]
            out = jnp.where(group == comp * PAIRS_DEV + p, value, out)
    return out


def power_cells(left_cells, right_cells):
    return jnp.where(lower_lanes((16, 128)), left_cells[:, :128], right_cells[:, 128:])


def by_pair(values):
    group = pair_lanes() % PAIRS_DEV
    out = values[0]
    for p in range(1, PAIRS_DEV):
        out = jnp.where(group == p, values[p], out)
    return out


def pair_of(list_ref, group, p):
    return tuple(list_ref[i, PAIRS_DEV * group + p] - 4 * group for i in range(2))


def early_kernel(
    list_ref, stack_ref, left_ref, right_ref, first_ref, second_ref, back_ref, crossing_ref, index_ref, keep, look_out,
    powers, middle, sem,
):
    keep_l, keep_r = keep.at[0], keep.at[1]
    copies = half_pair(stack_ref, 4, keep_l, keep_r, middle, sem)
    table = look_table()
    look_out[...] = table
    date = lax.axis_index("date")
    odd = odd_date() == 1
    before = jnp.maximum(date - 1, 0)
    own = [pair_of(list_ref, date, p) for p in range(PAIRS_DEV)]
    others = [pair_of(list_ref, before, p) for p in range(PAIRS_DEV)]
    crossing_ref[...] = by_pair([jnp.full((16, 128), (b >= 4).astype(jnp.int32)) for a, b in own])
    lane = lax.broadcasted_iota(jnp.int32, (8, 128), 1)
    index = jnp.zeros((8, 128), jnp.int32)
    for p in range(PAIRS_DEV):
        mine = jnp.where(odd, own[p][0], jnp.clip(others[p][1] - 4, 0, 3))
        theirs = jnp.where(odd, jnp.clip(own[p][1] - 4, 0, 2), jnp.clip(others[p][0] - 1, 0, 2))
        index = jnp.where(lane == p, mine, jnp.where(lane == PAIRS_DEV + p, theirs, index))
    index_ref[...] = index
    half_pair_end(copies, 4, keep_l, keep_r, middle)
    planes_l, planes_r = [], []
    for a, b in own:
        planes_l += cross(keep_l, a, keep_l, jnp.minimum(b, 3))
        planes_r += cross(keep_r, a, keep_r, jnp.minimum(b, 3))
    for acq in range(4):
        planes_l.append(power(keep_l, acq))
        planes_r.append(power(keep_r, acq))
    cells_l = pooled(planes_l, table)
    cells_r = pooled(planes_r, table)
    left_ref[...] = message(cells_l, 0)
    right_ref[...] = message(cells_r, 128)
    for acq in range(4):
        powers[acq] = power_cells(cells_l[8 + acq], cells_r[8 + acq])
    first_ref[...] = by_pair([powers[a] for a, b in own])
    second_ref[...] = by_pair([powers[jnp.minimum(b, 3)] for a, b in own])
    back_ref[...] = by_pair([powers[jnp.clip(b - 4, 0, 3)] for a, b in others])


def early(listed, stack):
    vmem = pl.BlockSpec(memory_space=pltpu.VMEM)
    smem = pl.BlockSpec(memory_space=pltpu.SMEM)
    out_shape = [jax.ShapeDtypeStruct((16, 128), F32)] * 5 + [
        jax.ShapeDtypeStruct((16, 128), jnp.int32),
        jax.ShapeDtypeStruct((8, 128), jnp.int32),
        jax.ShapeDtypeStruct((2, 4, 5, 80, 128), F32),
        jax.ShapeDtypeStruct((384, 256), BF16),
    ]
    return pl.pallas_call(
        early_kernel,
        out_shape=out_shape,
        in_specs=[smem, pl.BlockSpec(memory_space=HBM)],
        out_specs=[vmem] * len(out_shape),
        scratch_shapes=[
            pltpu.VMEM((4, 16, 128), F32), pltpu.VMEM((4, 2, 80, 128), F32), pltpu.SemaphoreType.DMA((3, 4)),
        ],
        compiler_params=pltpu.CompilerParams(vmem_limit_bytes=24 * 2**20),
        cost_estimate=pl.CostEstimate(flops=10**9, bytes_accessed=10**7, transcendentals=0),
    )(listed, stack)


def chip_kernel(
    list_ref, other_ref, keep, table_ref, crossing_ref, left_in, right_in, second_in, left_ref, right_ref, second_ref,
    first_swap, second_swap, *scratch,
):
    left_ref[...] = left_in[...]
    right_ref[...] = right_in[...]
    second_ref[...] = second_in[...]

    @pl.when(odd_date() == 0)
    def _():
        other_l, other_r, powers, middle, sem = scratch
        copies = half_pair(other_ref, SPAN, other_l, other_r, middle, sem)
        half_pair_end(copies, SPAN, other_l, other_r, middle)
        date = lax.axis_index("date")
        planes_l, planes_r, seconds = [], [], []
        for p in range(PAIRS_DEV):
            a, b = pair_of(list_ref, date, p)
            seconds.append(jnp.maximum(b - 4, 0))
            planes_l += cross(keep.at[0], a, other_l, seconds[p])
            planes_r += cross(keep.at[1], a, other_r, seconds[p])
        for acq in range(SPAN):
            planes_l.append(power(other_l, acq))
            planes_r.append(power(other_r, acq))
        cells_l = pooled(planes_l, table_ref[...])
        cells_r = pooled(planes_r, table_ref[...])
        crossing = crossing_ref[...] == 1
        left_ref[...] = jnp.where(crossing, message(cells_l, 0), left_in[...])
        right_ref[...] = jnp.where(crossing, message(cells_r, 128), right_in[...])
        for acq in range(SPAN):
            powers[acq] = power_cells(cells_l[8 + acq], cells_r[8 + acq])
        second_ref[...] = jnp.where(crossing, by_pair([powers[b] for b in seconds]), second_in[...])

    odd_col = lax.axis_index("col") % 2 == 1
    left, right = left_ref[...], right_ref[...]
    first_swap[...] = jnp.where(odd_col, left, right)
    second_swap[...] = jnp.where(odd_col, right, left)


def within_chip(listed, other, *arrays):
    vmem = pl.BlockSpec(memory_space=pltpu.VMEM)
    half = pltpu.VMEM((SPAN, 5, 80, 128), F32)
    return pl.pallas_call(
        chip_kernel,
        out_shape=[jax.ShapeDtypeStruct((16, 128), F32)] * 5,
        in_specs=[pl.BlockSpec(memory_space=pltpu.SMEM), pl.BlockSpec(memory_space=HBM)] + [vmem] * 6,
        out_specs=[vmem] * 5,
        scratch_shapes=[
            half, half, pltpu.VMEM((SPAN, 16, 128), F32), pltpu.VMEM((SPAN, 2, 80, 128), F32),
            pltpu.SemaphoreType.DMA((3, 4)),
        ],
        compiler_params=pltpu.CompilerParams(vmem_limit_bytes=24 * 2**20),
        cost_estimate=pl.CostEstimate(flops=10**9, bytes_accessed=10**7, transcendentals=0),
    )(listed, other, *arrays)


def table_kernel(after_ref, trig_ref, ns_out, rf_out, cf_out, rb_out, cb_out):
    ns_out[...] = neighbour_sum()
    for source, target in (
        (trig_ref[:256], cf_out),
        (trig_ref[256:640], cb_out),
        (trig_ref[640:704, :96], rf_out),
        (trig_ref[640:672, 128:], rb_out),
    ):
        high, low = split(source)
        target[0] = high
        target[1] = low


def filter_tables(after):
    vmem = pl.BlockSpec(memory_space=pltpu.VMEM)
    trig = np.zeros((704, 256))
    trig[:256] = col_forward()
    trig[256:640] = col_back()
    trig[640:704, :96] = row_forward()
    trig[640:672, 128:] = row_back()
    out_shape = [jax.ShapeDtypeStruct((128, 128), BF16)] + [
        jax.ShapeDtypeStruct((2,) + shape, BF16) for shape in ((64, 96), (256, 256), (32, 128), (384, 256))
    ]
    return pl.pallas_call(
        table_kernel,
        out_shape=out_shape,
        in_specs=[vmem] * 2,
        out_specs=[vmem] * 5,
        compiler_params=pltpu.CompilerParams(vmem_limit_bytes=16 * 2**20),
        cost_estimate=pl.CostEstimate(flops=10**8, bytes_accessed=10**6, transcendentals=0),
    )(after, jnp.asarray(trig, F32))


def late_kernel(index_ref, other_ref, keep, table_ref, back_in, new_ref, out_ref):
    odd = odd_date() == 1
    side = jnp.where(odd, 0, 1)
    index = index_ref[...]
    planes = []
    for p in range(PAIRS_DEV):
        planes += cross(keep.at[side], index[0, p], other_ref, index[0, PAIRS_DEV + p])
    table = table_ref[:, pl.ds(pl.multiple_of(128 * side, 128), 128)]
    high, low = split(jnp.concatenate(planes, axis=0))
    cells = mm(high, table) + mm(low, table)
    new = message(cells.reshape(len(planes), 16, 128), 0) * (1.0 / (LOOK_R * LOOK_C))
    new = jnp.where(odd | lower_lanes((16, 128)), new, -new)
    new_ref[...] = new
    out_ref[:16] = new
    out_ref[16:] = back_in[...]


def late(*arrays):
    vmem = pl.BlockSpec(memory_space=pltpu.VMEM)
    return pl.pallas_call(
        late_kernel,
        out_shape=(jax.ShapeDtypeStruct((16, 128), F32), jax.ShapeDtypeStruct((32, 128), F32)),
        in_specs=[vmem] * 5,
        out_specs=(vmem, vmem),
        compiler_params=pltpu.CompilerParams(vmem_limit_bytes=24 * 2**20),
    )(*arrays)


def merge_kernel(
    crossing_ref, before_late, right_late, after_late, left_late, first_ref, second_ref, left_early, right_early, mid_ref
):
    crossing = (crossing_ref[...] == 1) & (odd_date() == 1)
    col = lax.axis_index("col")
    odd_col = col % 2 == 1
    before = jnp.where(crossing, before_late[:16], jnp.where(odd_col, first_ref[...], second_ref[...]))
    after = jnp.where(crossing, after_late[...], jnp.where(odd_col, second_ref[...], first_ref[...]))
    mid_ref[:, :128] = jnp.where(col == 0, 0.0, before)
    mid_ref[:, 128:256] = jnp.where(crossing, left_late[...], left_early[...])
    mid_ref[:, 256:384] = jnp.where(crossing, right_late[:16], right_early[...])
    mid_ref[:, 384:] = jnp.where(col == lax.axis_size("col") - 1, 0.0, after)


def merge(*arrays):
    vmem = pl.BlockSpec(memory_space=pltpu.VMEM)
    return pl.pallas_call(
        merge_kernel,
        out_shape=jax.ShapeDtypeStruct((16, 512), F32),
        in_specs=[vmem] * 9,
        out_specs=vmem,
        compiler_params=pltpu.CompilerParams(vmem_limit_bytes=8 * 2**20),
    )(*arrays)


def coherence_of(mid_ref, first, second, out_ref):
    lane = lax.broadcasted_iota(jnp.int32, (16, 128), 1)
    squares = []
    for at in (128, 256):
        x = mid_ref[:, at : at + 128]
        squares.append(x * x + pltpu.roll(x * x, 64, 1))
    magnitude = jnp.sqrt(jnp.where(lane < 64, squares[0], squares[1]))
    coherence = magnitude / jnp.sqrt((first + 1e-06) * (second + 1e-06))
    for p in range(PAIRS_DEV):
        left = coherence if p == 0 else pltpu.roll(coherence, 128 - HALF * p, 1)
        right = pltpu.roll(coherence, (HALF + 64 - HALF * p) % 128, 1)
        out_ref[p] = jnp.where(lane < HALF, left, right)[:, :PATCH]


def goldstein_kernel(
    first_swap, mid_ref, second_swap, ns_ref, rf_ref, cf_ref, rb_ref, cb_ref, crossing_ref, first_ref, second_ref, late_ref,
    out_ref, coh_ref,
):
    odd_crossing = (crossing_ref[...] == 1) & (odd_date() == 1)
    coherence_of(mid_ref, first_ref[...], jnp.where(odd_crossing, late_ref[16:], second_ref[...]), coh_ref)
    row = lax.axis_index("row")
    odd_row = row % 2 == 1
    up = jnp.where(odd_row, first_swap[...], second_swap[...])
    down = jnp.where(odd_row, second_swap[...], first_swap[...])
    up = jnp.where(row == 0, 0.0, up)
    down = jnp.where(row == lax.axis_size("row") - 1, 0.0, down)
    x = jnp.concatenate([up, mid_ref[...], down], axis=0)
    lane = lax.broadcasted_iota(jnp.int32, (48, 128), 1)
    sign = jnp.where(lane < 64, -1.0, 1.0)
    turned = [pltpu.roll(x[:, 128 * b : 128 * b + 128], 64, 1) * sign for b in range(4)]
    xx = jnp.concatenate([x, jnp.concatenate(turned, axis=1)], axis=0)
    xh, xl = split(xx)
    rh, rl = rf_ref[0], rf_ref[1]
    y = mm(jnp.concatenate([rh, rh], axis=1), jnp.concatenate([xh, xl], axis=0)) + mm(rl, xh)
    ys = jnp.concatenate([y[:, 128 * j : 128 * j + 256] for j in range(3)], axis=0)
    yh, yl = split(ys)
    ch, cl = cf_ref[0], cf_ref[1]
    z = mm(yh, ch) + (mm(yl, ch) + mm(yh, cl))
    zr, zi = z[:, :128], z[:, 128:]
    magnitude = jnp.sqrt(zr * zr + zi * zi)
    mh, ml = split(magnitude)
    across = mm(jnp.concatenate([mh, ml], axis=1), jnp.concatenate([ns_ref[...], ns_ref[...]], axis=0))
    grouped = across.reshape(6, PATCH, 128)
    down_one = jnp.concatenate([grouped[:, PATCH - 1 :], grouped[:, : PATCH - 1]], axis=1)
    up_one = jnp.concatenate([grouped[:, 1:], grouped[:, :1]], axis=1)
    smooth = (grouped + (down_one + up_one)).reshape(192, 128)
    response = jnp.sqrt(smooth * (1.0 / 9.0)) * (1.0 / PATCH)
    fr, fi = zr * response, zi * response
    w = jnp.concatenate(
        [
            jnp.concatenate([fr[64 * j : 64 * j + 64] for j in range(3)], axis=1),
            jnp.concatenate([fi[64 * j : 64 * j + 64] for j in range(3)], axis=1),
        ],
        axis=0,
    )
    wh, wl = split(w)
    bh, bl = rb_ref[0], rb_ref[1]
    t = mm(jnp.concatenate([bh, bh], axis=1), jnp.concatenate([wh, wl], axis=0)) + mm(bl, wh)
    th, tl = split(t)
    gh, gl = cb_ref[0], cb_ref[1]
    oo = mm(jnp.concatenate([th, tl], axis=0), gh)
    o = oo[:32] + (oo[32:] + mm(th, gl))
    real = o[:16, :128] - o[16:, 128:]
    imag = o[16:, :128] + o[:16, 128:]
    for p in range(PAIRS_DEV):
        out_ref[p, 0] = real[:, PATCH * p : PATCH * p + PATCH]
        out_ref[p, 1] = imag[:, PATCH * p : PATCH * p + PATCH]


def goldstein(*arrays):
    vmem = pl.BlockSpec(memory_space=pltpu.VMEM)
    return pl.pallas_call(
        goldstein_kernel,
        out_shape=(
            jax.ShapeDtypeStruct((PAIRS_DEV, 2, 16, 32), F32), jax.ShapeDtypeStruct((PAIRS_DEV, 16, 32), F32),
        ),
        in_specs=[vmem] * 12,
        out_specs=(vmem, vmem),
        compiler_params=pltpu.CompilerParams(vmem_limit_bytes=24 * 2**20),
    )(*arrays)


def neighbour(i, n, first):
    if first:
        return i ^ 1
    return ((i - 1) ^ 1) + 1 if 0 < i < n - 1 else i


def shards(stack, pair_list):
    names = ("date", "row", "col")
    dates, rows, cols = (lax.axis_size(name) for name in names)

    def send(x, target):
        pairs = []
        for d in range(dates):
            for r in range(rows):
                for c in range(cols):
                    a, b, e = target(d, r, c)
                    pairs.append(((d * rows + r) * cols + c, (a * rows + b) * cols + e))
        return lax.ppermute(x, names, pairs)

    def swap_cols(first):
        def target(d, r, c):
            e = neighbour(c, cols, first)
            return (d, r, e) if e != c else (d, r ^ 1, c)

        return target

    def swap_rows(first):
        def target(d, r, c):
            b = neighbour(r, rows, first)
            return (d, b, c) if b != r else (d ^ 1, r, c)

        return target

    def between_dates(odd_target, even_target):
        def target(d, r, c):
            if d in (0, dates - 1):
                return d, r, c ^ 1
            if d % 2:
                up, e = odd_target(c)
                return d + up, r, e
            down, e = even_target(c)
            return d - down, r, e

        return target

    end = cols - 1
    straight = between_dates(lambda c: (1, c), lambda c: (1, c))
    def ring(d, r, c):
        if d % 2:
            return (d, r, c - 1) if c > 0 else (d - 1, r, c)
        return (d, r, c + 1) if c < end else (d + 1, r, c)

    from_left = between_dates(
        lambda c: (1, 0) if c == 0 else (0, 0) if c == 1 else (1, c - 1) if c < end else (1, end),
        lambda c: (1, c + 1) if c < end else (0, end - 1),
    )

    listed = pair_list.T
    other = send(pack(stack), straight)
    chip = send(stack, lambda d, r, c: (d ^ 1, r, c))
    left, right, first, second, back, crossing, index, keep, look = early(listed, stack)
    left, right, second, one, two = within_chip(listed, chip, keep, look, crossing, left, right, second)
    one = send(one, swap_cols(True))
    two = send(two, swap_cols(False))
    tables = filter_tables(right)
    other, one, two = lax.optimization_barrier((other, one, two))
    new, with_powers = late(index, other, keep, look, back)
    after = send(new, ring)
    before = send(with_powers, from_left)
    right_late = send(with_powers, straight)
    mid = merge(crossing, before, right_late, after, new, one, two, left, right)
    one = send(mid, swap_rows(True))
    two = send(mid, swap_rows(False))
    return goldstein(one, mid, two, *tables, crossing, first, second, right_late)


def solution(mesh):
    in_specs = (P("date", None, "row", "col"), P())
    out_specs = (P("date", None, "row", "col"), P("date", "row", "col"))
    return jax.shard_map(shards, mesh=mesh, in_specs=in_specs, out_specs=out_specs, check_vma=False)
```

```python
import functools
import math

import jax
import jax.numpy as jnp
import numpy as np
from jax import lax
from jax.experimental import pallas as pl
from jax.experimental.pallas import tpu as pltpu
from jax.sharding import PartitionSpec as P

SPAN = 3
LOOK_R = 5
LOOK_C = 20
PATCH = 32
HALF = PATCH // 2
PAIRS_DEV = 4
F32 = jnp.float32
BF16 = jnp.bfloat16
HBM = pltpu.MemorySpace.HBM


def taper(v):
    return np.where(v < HALF, (v + 0.5) / HALF, (PATCH - 0.5 - v) / HALF)


def whole_part(x, divisor):
    return (x.astype(F32) * (1.0 / divisor) + 0.5 / divisor).astype(jnp.int32)


def look_table():
    lane = lax.broadcasted_iota(jnp.int32, (384, 256), 0)
    n = lax.broadcasted_iota(jnp.int32, (384, 256), 1)
    left = jnp.where(lane < 256, lane, 256 + lane % 64)
    right = jnp.where(lane < 256, 64 + lane, lane % 64)
    cell = whole_part(jnp.where(n < 128, left, right), LOOK_C)
    return (cell == n % HALF).astype(F32).astype(BF16)


def row_forward():
    i, k, q, row = np.meshgrid(np.arange(2), np.arange(PATCH), np.arange(2), np.arange(48), indexing="ij")
    u = row - HALF * i
    angle = 2 * np.pi * k * u / PATCH
    value = np.where(q == 0, np.cos(angle), -np.sin(angle)) * ((u >= 0) & (u < PATCH))
    return value.reshape(64, 96)


def col_forward():
    h, c, p, v, c2, p2, l = np.meshgrid(
        np.arange(2), np.arange(2), np.arange(4), np.arange(HALF), np.arange(2), np.arange(4), np.arange(PATCH),
        indexing="ij",
    )
    angle = 2 * np.pi * l * (HALF * h + v) / PATCH
    value = np.where(c == c2, np.cos(angle), np.where(c == 1, np.sin(angle), -np.sin(angle)))
    return (value * (p == p2)).reshape(256, 256)


def neighbour_sum():
    a = lax.broadcasted_iota(jnp.int32, (128, 128), 0)
    b = lax.broadcasted_iota(jnp.int32, (128, 128), 1)
    d = (a - b) & (PATCH - 1)
    near = (d <= 1) | (d == PATCH - 1)
    return (near & ((a & -PATCH) == (b & -PATCH))).astype(F32).astype(BF16)


def row_back():
    c2, r, c, i, k = np.meshgrid(
        np.arange(2), np.arange(HALF), np.arange(2), np.arange(2), np.arange(PATCH), indexing="ij"
    )
    u = r + HALF * (1 - i)
    angle = 2 * np.pi * k * u / PATCH
    value = np.where(c == c2, np.cos(angle), np.where(c2 == 0, -np.sin(angle), np.sin(angle))) * taper(u)
    return value.reshape(32, 128)


def col_back():
    j, p, l, q, p2, c = np.meshgrid(
        np.arange(3), np.arange(4), np.arange(PATCH), np.arange(2), np.arange(4), np.arange(PATCH), indexing="ij"
    )
    v = c + HALF - HALF * j
    angle = 2 * np.pi * l * v / PATCH
    value = np.where(q == 0, np.cos(angle), np.sin(angle)) * taper(v) * ((v >= 0) & (v < PATCH)) * (p == p2)
    return (value / (PATCH * PATCH)).reshape(384, 256)


def split(x):
    hi = x.astype(BF16)
    return hi, (x - hi.astype(F32)).astype(BF16)


def mm(a, b):
    return jnp.dot(a, b, preferred_element_type=F32)


def half_copies(stack_ref, first, out_ref, tile, sem, slot):
    count = out_ref.shape[0]
    return [
        pltpu.make_async_copy(
            stack_ref.at[first : first + count, comp, :, pl.ds(128 * (tile + t), 128)],
            out_ref.at[:, 2 * comp + t],
            sem.at[slot, 2 * comp + t],
        )
        for comp in range(2)
        for t in range(2)
    ]


def lower_lanes(shape):
    return lax.broadcasted_iota(jnp.int32, shape, len(shape) - 1) % 128 < 64


def mixed_tile(real, imag, right):
    turned = pltpu.roll(jnp.where(right, real, imag), 64, 1)
    return jnp.where(lower_lanes(real.shape) == right, turned, jnp.where(right, imag, real))


def half_pair(stack_ref, count, left_ref, right_ref, middle, sem):
    lanes = pl.ds(256, 128)
    copies = [pltpu.make_async_copy(stack_ref.at[:count, :, :, lanes], middle, sem.at[2, 0])]
    copies += half_copies(stack_ref, 0, left_ref, 0, sem, 0)
    copies += half_copies(stack_ref, 0, right_ref, 3, sem, 1)
    for copy in copies:
        copy.start()
    return copies


def half_pair_end(copies, count, left_ref, right_ref, middle):
    copies[0].wait()
    for acq in range(count):
        left_ref[acq, 4] = mixed_tile(middle[acq, 0], middle[acq, 1], False)
        right_ref[acq, 4] = mixed_tile(middle[acq, 0], middle[acq, 1], True)
    for copy in copies[1:]:
        copy.wait()


def odd_date():
    return lax.axis_index("date") % 2


def pack_kernel(stack_ref, out_ref, middle, sem):
    odd = odd_date()
    acqs = pl.ds(odd, SPAN)
    copies = [pltpu.make_async_copy(stack_ref.at[acqs, :, :, pl.ds(256, 128)], middle, sem.at[4])]
    for comp in range(2):
        for t in range(2):
            lanes = pl.ds(pl.multiple_of(128 * (3 * odd + t), 128), 128)
            at = 2 * comp + t
            copies.append(pltpu.make_async_copy(stack_ref.at[acqs, comp, :, lanes], out_ref.at[:, at], sem.at[at]))
    for copy in copies:
        copy.start()
    copies[0].wait()
    for acq in range(SPAN):
        out_ref[acq, 4] = mixed_tile(middle[acq, 0], middle[acq, 1], odd == 1)
    for copy in copies[1:]:
        copy.wait()


def pack(stack):
    return pl.pallas_call(
        pack_kernel,
        out_shape=pltpu.VMEM((SPAN, 5, 80, 128), F32),
        in_specs=[pl.BlockSpec(memory_space=pl.ANY)],
        out_specs=pl.BlockSpec(memory_space=pltpu.VMEM),
        scratch_shapes=[pltpu.VMEM((SPAN, 2, 80, 128), F32), pltpu.SemaphoreType.DMA((5,))],
        compiler_params=pltpu.CompilerParams(vmem_limit_bytes=60000000),
    )(stack)


def cross(a_ref, a, b_ref, b):
    real, imag = [0.0] * 3, [0.0] * 3
    for k in range(LOOK_R):
        rows = pl.ds(k, 16, stride=LOOK_R)
        x = [a_ref[a, t, rows, :] for t in range(5)]
        y = [b_ref[b, t, rows, :] for t in range(5)]
        for t in range(2):
            real[t] += x[t] * y[t] + x[t + 2] * y[t + 2]
            imag[t] += x[t + 2] * y[t] - x[t] * y[t + 2]
        real[2] += x[4] * y[4]
        imag[2] += x[4] * pltpu.roll(y[4], 64, 1)
    imag[2] = jnp.where(lower_lanes((16, 128)), -imag[2], imag[2])
    return jnp.concatenate(real, axis=1), jnp.concatenate(imag, axis=1)


def power(a_ref, a):
    total = [0.0] * 3
    for k in range(LOOK_R):
        x = [a_ref[a, t, pl.ds(k, 16, stride=LOOK_R), :] for t in range(5)]
        for t in range(2):
            total[t] += x[t] * x[t] + x[t + 2] * x[t + 2]
        total[2] += x[4] * x[4]
    return jnp.concatenate(total, axis=1)


def pooled(planes, table):
    high, low = split(jnp.concatenate(planes, axis=0))
    cells = (mm(high, table) + mm(low, table)) * (1.0 / (LOOK_R * LOOK_C))
    return cells.reshape(len(planes), 16, 256)


def pair_lanes():
    return lax.broadcasted_iota(jnp.int32, (16, 128), 1) // HALF


def message(cells, offset):
    group = pair_lanes()
    out = jnp.zeros((16, 128), F32)
    for p in range(PAIRS_DEV):
        for comp in range(2):
            value = cells[2 * p + comp, :, offset : offset + 128]
            out = jnp.where(group == comp * PAIRS_DEV + p, value, out)
    return out


def power_cells(left_cells, right_cells):
    return jnp.where(lower_lanes((16, 128)), left_cells[:, :128], right_cells[:, 128:])


def by_pair(values):
    group = pair_lanes() % PAIRS_DEV
    out = values[0]
    for p in range(1, PAIRS_DEV):
        out = jnp.where(group == p, values[p], out)
    return out


def pair_of(list_ref, group, p):
    return tuple(list_ref[i, PAIRS_DEV * group + p] - 4 * group for i in range(2))


def early_kernel(
    list_ref, stack_ref, left_ref, right_ref, first_ref, second_ref, back_ref, crossing_ref, index_ref, keep, look_out,
    mine_ref, powers, middle, sem,
):
    keep_l, keep_r = keep.at[0], keep.at[1]
    copies = half_pair(stack_ref, 4, keep_l, keep_r, middle, sem)
    table = look_table()
    look_out[...] = table
    date = lax.axis_index("date")
    odd = odd_date() == 1
    before = jnp.maximum(date - 1, 0)
    own = [pair_of(list_ref, date, p) for p in range(PAIRS_DEV)]
    others = [pair_of(list_ref, before, p) for p in range(PAIRS_DEV)]
    crossing_ref[...] = by_pair([jnp.full((16, 128), (b >= 4).astype(jnp.int32)) for a, b in own])
    lane = lax.broadcasted_iota(jnp.int32, (8, 128), 1)
    index = jnp.zeros((8, 128), jnp.int32)
    mines = []
    for p in range(PAIRS_DEV):
        mines.append(jnp.where(odd, own[p][0], jnp.clip(others[p][1] - 4, 0, 3)))
        theirs = jnp.where(odd, jnp.clip(own[p][1] - 4, 0, 2), jnp.clip(others[p][0] - 1, 0, 2))
        index = jnp.where(lane == p, theirs, index)
    index_ref[...] = index
    half_pair_end(copies, 4, keep_l, keep_r, middle)
    for p in range(PAIRS_DEV):
        mine_ref[p] = keep[jnp.where(odd, 0, 1), mines[p]]
    planes_l, planes_r = [], []
    for a, b in own:
        planes_l += cross(keep_l, a, keep_l, jnp.minimum(b, 3))
        planes_r += cross(keep_r, a, keep_r, jnp.minimum(b, 3))
    for acq in range(4):
        planes_l.append(power(keep_l, acq))
        planes_r.append(power(keep_r, acq))
    cells_l = pooled(planes_l, table)
    cells_r = pooled(planes_r, table)
    left_ref[...] = message(cells_l, 0)
    right_ref[...] = message(cells_r, 128)
    for acq in range(4):
        powers[acq] = power_cells(cells_l[8 + acq], cells_r[8 + acq])
    first_ref[...] = by_pair([powers[a] for a, b in own])
    second_ref[...] = by_pair([powers[jnp.minimum(b, 3)] for a, b in own])
    back_ref[...] = by_pair([powers[jnp.clip(b - 4, 0, 3)] for a, b in others])


def early(listed, stack):
    vmem = pl.BlockSpec(memory_space=pltpu.VMEM)
    smem = pl.BlockSpec(memory_space=pltpu.SMEM)
    out_shape = [jax.ShapeDtypeStruct((16, 128), F32)] * 5 + [
        jax.ShapeDtypeStruct((16, 128), jnp.int32),
        jax.ShapeDtypeStruct((8, 128), jnp.int32),
        jax.ShapeDtypeStruct((2, 4, 5, 80, 128), F32),
        jax.ShapeDtypeStruct((384, 256), BF16),
        jax.ShapeDtypeStruct((PAIRS_DEV, 5, 80, 128), F32),
    ]
    return pl.pallas_call(
        early_kernel,
        out_shape=out_shape,
        in_specs=[smem, pl.BlockSpec(memory_space=HBM)],
        out_specs=[vmem] * len(out_shape),
        scratch_shapes=[
            pltpu.VMEM((4, 16, 128), F32), pltpu.VMEM((4, 2, 80, 128), F32), pltpu.SemaphoreType.DMA((3, 4)),
        ],
        compiler_params=pltpu.CompilerParams(vmem_limit_bytes=24 * 2**20),
        cost_estimate=pl.CostEstimate(flops=10**9, bytes_accessed=10**7, transcendentals=0),
    )(listed, stack)


def chip_kernel(
    list_ref, other_ref, keep, table_ref, crossing_ref, left_in, right_in, second_in, left_ref, right_ref, second_ref,
    first_swap, second_swap, *scratch,
):
    left_ref[...] = left_in[...]
    right_ref[...] = right_in[...]
    second_ref[...] = second_in[...]

    @pl.when(odd_date() == 0)
    def _():
        other_l, other_r, powers, middle, sem = scratch
        copies = half_pair(other_ref, SPAN, other_l, other_r, middle, sem)
        half_pair_end(copies, SPAN, other_l, other_r, middle)
        date = lax.axis_index("date")
        planes_l, planes_r, seconds = [], [], []
        for p in range(PAIRS_DEV):
            a, b = pair_of(list_ref, date, p)
            seconds.append(jnp.maximum(b - 4, 0))
            planes_l += cross(keep.at[0], a, other_l, seconds[p])
            planes_r += cross(keep.at[1], a, other_r, seconds[p])
        for acq in range(SPAN):
            planes_l.append(power(other_l, acq))
            planes_r.append(power(other_r, acq))
        cells_l = pooled(planes_l, table_ref[...])
        cells_r = pooled(planes_r, table_ref[...])
        crossing = crossing_ref[...] == 1
        left_ref[...] = jnp.where(crossing, message(cells_l, 0), left_in[...])
        right_ref[...] = jnp.where(crossing, message(cells_r, 128), right_in[...])
        for acq in range(SPAN):
            powers[acq] = power_cells(cells_l[8 + acq], cells_r[8 + acq])
        second_ref[...] = jnp.where(crossing, by_pair([powers[b] for b in seconds]), second_in[...])

    odd_col = lax.axis_index("col") % 2 == 1
    left, right = left_ref[...], right_ref[...]
    first_swap[...] = jnp.where(odd_col, left, right)
    second_swap[...] = jnp.where(odd_col, right, left)


def within_chip(listed, other, *arrays):
    vmem = pl.BlockSpec(memory_space=pltpu.VMEM)
    half = pltpu.VMEM((SPAN, 5, 80, 128), F32)
    return pl.pallas_call(
        chip_kernel,
        out_shape=[jax.ShapeDtypeStruct((16, 128), F32)] * 5,
        in_specs=[pl.BlockSpec(memory_space=pltpu.SMEM), pl.BlockSpec(memory_space=HBM)] + [vmem] * 6,
        out_specs=[vmem] * 5,
        scratch_shapes=[
            half, half, pltpu.VMEM((SPAN, 16, 128), F32), pltpu.VMEM((SPAN, 2, 80, 128), F32),
            pltpu.SemaphoreType.DMA((3, 4)),
        ],
        compiler_params=pltpu.CompilerParams(vmem_limit_bytes=24 * 2**20),
        cost_estimate=pl.CostEstimate(flops=10**9, bytes_accessed=10**7, transcendentals=0),
    )(listed, other, *arrays)


def table_kernel(after_ref, trig_ref, ns_out, rf_out, cf_out, rb_out, cb_out):
    ns_out[...] = neighbour_sum()
    for source, target in (
        (trig_ref[:256], cf_out),
        (trig_ref[256:640], cb_out),
        (trig_ref[640:704, :96], rf_out),
        (trig_ref[640:672, 128:], rb_out),
    ):
        high, low = split(source)
        target[0] = high
        target[1] = low


def filter_tables(after):
    vmem = pl.BlockSpec(memory_space=pltpu.VMEM)
    trig = np.zeros((704, 256))
    trig[:256] = col_forward()
    trig[256:640] = col_back()
    trig[640:704, :96] = row_forward()
    trig[640:672, 128:] = row_back()
    out_shape = [jax.ShapeDtypeStruct((128, 128), BF16)] + [
        jax.ShapeDtypeStruct((2,) + shape, BF16) for shape in ((64, 96), (256, 256), (32, 128), (384, 256))
    ]
    return pl.pallas_call(
        table_kernel,
        out_shape=out_shape,
        in_specs=[vmem] * 2,
        out_specs=[vmem] * 5,
        compiler_params=pltpu.CompilerParams(vmem_limit_bytes=16 * 2**20),
        cost_estimate=pl.CostEstimate(flops=10**8, bytes_accessed=10**6, transcendentals=0),
    )(after, jnp.asarray(trig, F32))


def late_kernel(index_ref, other_ref, mine_ref, table_ref, back_in, new_ref, out_ref):
    odd = odd_date() == 1
    side = jnp.where(odd, 0, 1)
    index = index_ref[...]
    planes = []
    for p in range(PAIRS_DEV):
        planes += cross(mine_ref, p, other_ref, index[0, p])
    table = table_ref[:, pl.ds(pl.multiple_of(128 * side, 128), 128)]
    high, low = split(jnp.concatenate(planes, axis=0))
    cells = mm(high, table) + mm(low, table)
    new = message(cells.reshape(len(planes), 16, 128), 0) * (1.0 / (LOOK_R * LOOK_C))
    new = jnp.where(odd | lower_lanes((16, 128)), new, -new)
    new_ref[...] = new
    out_ref[:16] = new
    out_ref[16:] = back_in[...]


def late(*arrays):
    vmem = pl.BlockSpec(memory_space=pltpu.VMEM)
    return pl.pallas_call(
        late_kernel,
        out_shape=(jax.ShapeDtypeStruct((16, 128), F32), jax.ShapeDtypeStruct((32, 128), F32)),
        in_specs=[vmem] * 5,
        out_specs=(vmem, vmem),
        compiler_params=pltpu.CompilerParams(vmem_limit_bytes=24 * 2**20),
    )(*arrays)


def merge_kernel(
    crossing_ref, before_late, right_late, after_late, left_late, first_ref, second_ref, left_early, right_early, mid_ref
):
    crossing = (crossing_ref[...] == 1) & (odd_date() == 1)
    col = lax.axis_index("col")
    odd_col = col % 2 == 1
    before = jnp.where(crossing, before_late[:16], jnp.where(odd_col, first_ref[...], second_ref[...]))
    after = jnp.where(crossing, after_late[...], jnp.where(odd_col, second_ref[...], first_ref[...]))
    mid_ref[:, :128] = jnp.where(col == 0, 0.0, before)
    mid_ref[:, 128:256] = jnp.where(crossing, left_late[...], left_early[...])
    mid_ref[:, 256:384] = jnp.where(crossing, right_late[:16], right_early[...])
    mid_ref[:, 384:] = jnp.where(col == lax.axis_size("col") - 1, 0.0, after)


def merge(*arrays):
    vmem = pl.BlockSpec(memory_space=pltpu.VMEM)
    return pl.pallas_call(
        merge_kernel,
        out_shape=jax.ShapeDtypeStruct((16, 512), F32),
        in_specs=[vmem] * 9,
        out_specs=vmem,
        compiler_params=pltpu.CompilerParams(vmem_limit_bytes=8 * 2**20),
    )(*arrays)


def coherence_of(mid_ref, first, second, out_ref):
    lane = lax.broadcasted_iota(jnp.int32, (16, 128), 1)
    squares = []
    for at in (128, 256):
        x = mid_ref[:, at : at + 128]
        squares.append(x * x + pltpu.roll(x * x, 64, 1))
    magnitude = jnp.sqrt(jnp.where(lane < 64, squares[0], squares[1]))
    coherence = magnitude / jnp.sqrt((first + 1e-06) * (second + 1e-06))
    for p in range(PAIRS_DEV):
        left = coherence if p == 0 else pltpu.roll(coherence, 128 - HALF * p, 1)
        right = pltpu.roll(coherence, (HALF + 64 - HALF * p) % 128, 1)
        out_ref[p] = jnp.where(lane < HALF, left, right)[:, :PATCH]


def goldstein_kernel(
    first_swap, mid_ref, second_swap, ns_ref, rf_ref, cf_ref, rb_ref, cb_ref, crossing_ref, first_ref, second_ref, late_ref,
    out_ref, coh_ref,
):
    odd_crossing = (crossing_ref[...] == 1) & (odd_date() == 1)
    coherence_of(mid_ref, first_ref[...], jnp.where(odd_crossing, late_ref[16:], second_ref[...]), coh_ref)
    row = lax.axis_index("row")
    odd_row = row % 2 == 1
    up = jnp.where(odd_row, first_swap[...], second_swap[...])
    down = jnp.where(odd_row, second_swap[...], first_swap[...])
    up = jnp.where(row == 0, 0.0, up)
    down = jnp.where(row == lax.axis_size("row") - 1, 0.0, down)
    x = jnp.concatenate([up, mid_ref[...], down], axis=0)
    lane = lax.broadcasted_iota(jnp.int32, (48, 128), 1)
    sign = jnp.where(lane < 64, -1.0, 1.0)
    turned = [pltpu.roll(x[:, 128 * b : 128 * b + 128], 64, 1) * sign for b in range(4)]
    xx = jnp.concatenate([x, jnp.concatenate(turned, axis=1)], axis=0)
    xh, xl = split(xx)
    rh, rl = rf_ref[0], rf_ref[1]
    y = mm(jnp.concatenate([rh, rh], axis=1), jnp.concatenate([xh, xl], axis=0)) + mm(rl, xh)
    ys = jnp.concatenate([y[:, 128 * j : 128 * j + 256] for j in range(3)], axis=0)
    yh, yl = split(ys)
    ch, cl = cf_ref[0], cf_ref[1]
    z = mm(yh, ch) + (mm(yl, ch) + mm(yh, cl))
    zr, zi = z[:, :128], z[:, 128:]
    magnitude = jnp.sqrt(zr * zr + zi * zi)
    mh, ml = split(magnitude)
    across = mm(jnp.concatenate([mh, ml], axis=1), jnp.concatenate([ns_ref[...], ns_ref[...]], axis=0))
    grouped = across.reshape(6, PATCH, 128)
    down_one = jnp.concatenate([grouped[:, PATCH - 1 :], grouped[:, : PATCH - 1]], axis=1)
    up_one = jnp.concatenate([grouped[:, 1:], grouped[:, :1]], axis=1)
    smooth = (grouped + (down_one + up_one)).reshape(192, 128)
    response = jnp.sqrt(smooth * (1.0 / 9.0)) * (1.0 / PATCH)
    fr, fi = zr * response, zi * response
    w = jnp.concatenate(
        [
            jnp.concatenate([fr[64 * j : 64 * j + 64] for j in range(3)], axis=1),
            jnp.concatenate([fi[64 * j : 64 * j + 64] for j in range(3)], axis=1),
        ],
        axis=0,
    )
    wh, wl = split(w)
    bh, bl = rb_ref[0], rb_ref[1]
    t = mm(jnp.concatenate([bh, bh], axis=1), jnp.concatenate([wh, wl], axis=0)) + mm(bl, wh)
    th, tl = split(t)
    gh, gl = cb_ref[0], cb_ref[1]
    oo = mm(jnp.concatenate([th, tl], axis=0), gh)
    o = oo[:32] + (oo[32:] + mm(th, gl))
    real = o[:16, :128] - o[16:, 128:]
    imag = o[16:, :128] + o[:16, 128:]
    for p in range(PAIRS_DEV):
        out_ref[p, 0] = real[:, PATCH * p : PATCH * p + PATCH]
        out_ref[p, 1] = imag[:, PATCH * p : PATCH * p + PATCH]


def goldstein(*arrays):
    vmem = pl.BlockSpec(memory_space=pltpu.VMEM)
    return pl.pallas_call(
        goldstein_kernel,
        out_shape=(
            jax.ShapeDtypeStruct((PAIRS_DEV, 2, 16, 32), F32), jax.ShapeDtypeStruct((PAIRS_DEV, 16, 32), F32),
        ),
        in_specs=[vmem] * 12,
        out_specs=(vmem, vmem),
        compiler_params=pltpu.CompilerParams(vmem_limit_bytes=24 * 2**20),
    )(*arrays)


def neighbour(i, n, first):
    if first:
        return i ^ 1
    return ((i - 1) ^ 1) + 1 if 0 < i < n - 1 else i


def shards(stack, pair_list):
    names = ("date", "row", "col")
    dates, rows, cols = (lax.axis_size(name) for name in names)

    def send(x, target):
        pairs = []
        for d in range(dates):
            for r in range(rows):
                for c in range(cols):
                    a, b, e = target(d, r, c)
                    pairs.append(((d * rows + r) * cols + c, (a * rows + b) * cols + e))
        return lax.ppermute(x, names, pairs)

    def swap_cols(first):
        def target(d, r, c):
            e = neighbour(c, cols, first)
            return (d, r, e) if e != c else (d, r ^ 1, c)

        return target

    def swap_rows(first):
        def target(d, r, c):
            b = neighbour(r, rows, first)
            return (d, b, c) if b != r else (d ^ 1, r, c)

        return target

    def between_dates(odd_target, even_target):
        def target(d, r, c):
            if d in (0, dates - 1):
                return d, r, c ^ 1
            if d % 2:
                up, e = odd_target(c)
                return d + up, r, e
            down, e = even_target(c)
            return d - down, r, e

        return target

    end = cols - 1
    straight = between_dates(lambda c: (1, c), lambda c: (1, c))
    def ring(d, r, c):
        if d % 2:
            return (d, r, c - 1) if c > 0 else (d - 1, r, c)
        return (d, r, c + 1) if c < end else (d + 1, r, c)

    from_left = between_dates(
        lambda c: (1, 0) if c == 0 else (0, 0) if c == 1 else (1, c - 1) if c < end else (1, end),
        lambda c: (1, c + 1) if c < end else (0, end - 1),
    )

    listed = pair_list.T
    other = send(pack(stack), straight)
    chip = send(stack, lambda d, r, c: (d ^ 1, r, c))
    left, right, first, second, back, crossing, index, keep, look, mine = early(listed, stack)
    left, right, second, one, two = within_chip(listed, chip, keep, look, crossing, left, right, second)
    one = send(one, swap_cols(True))
    two = send(two, swap_cols(False))
    tables = filter_tables(right)
    other, one, two = lax.optimization_barrier((other, one, two))
    new, with_powers = late(index, other, mine, look, back)
    after = send(new, ring)
    before = send(with_powers, from_left)
    right_late = send(with_powers, straight)
    mid = merge(crossing, before, right_late, after, new, one, two, left, right)
    one = send(mid, swap_rows(True))
    two = send(mid, swap_rows(False))
    return goldstein(one, mid, two, *tables, crossing, first, second, right_late)


def solution(mesh):
    in_specs = (P("date", None, "row", "col"), P())
    out_specs = (P("date", None, "row", "col"), P("date", "row", "col"))
    return jax.shard_map(shards, mesh=mesh, in_specs=in_specs, out_specs=out_specs, check_vma=False)
```

```python
import functools
import math

import jax
import jax.numpy as jnp
import numpy as np
from jax import lax
from jax.experimental import pallas as pl
from jax.experimental.pallas import tpu as pltpu
from jax.sharding import PartitionSpec as P

SPAN = 3
LOOK_R = 5
LOOK_C = 20
PATCH = 32
HALF = PATCH // 2
PAIRS_DEV = 4
F32 = jnp.float32
BF16 = jnp.bfloat16
HBM = pltpu.MemorySpace.HBM


def taper(v):
    return np.where(v < HALF, (v + 0.5) / HALF, (PATCH - 0.5 - v) / HALF)


def whole_part(x, divisor):
    return (x.astype(F32) * (1.0 / divisor) + 0.5 / divisor).astype(jnp.int32)


def look_table():
    lane = lax.broadcasted_iota(jnp.int32, (384, 256), 0)
    n = lax.broadcasted_iota(jnp.int32, (384, 256), 1)
    left = jnp.where(lane < 256, lane, 256 + lane % 64)
    right = jnp.where(lane < 256, 64 + lane, lane % 64)
    cell = whole_part(jnp.where(n < 128, left, right), LOOK_C)
    return (cell == n % HALF).astype(F32).astype(BF16)


def row_forward():
    i, k, q, row = np.meshgrid(np.arange(2), np.arange(PATCH), np.arange(2), np.arange(48), indexing="ij")
    u = row - HALF * i
    angle = 2 * np.pi * k * u / PATCH
    value = np.where(q == 0, np.cos(angle), -np.sin(angle)) * ((u >= 0) & (u < PATCH))
    return value.reshape(64, 96)


def col_forward():
    h, c, p, v, c2, p2, l = np.meshgrid(
        np.arange(2), np.arange(2), np.arange(4), np.arange(HALF), np.arange(2), np.arange(4), np.arange(PATCH),
        indexing="ij",
    )
    angle = 2 * np.pi * l * (HALF * h + v) / PATCH
    value = np.where(c == c2, np.cos(angle), np.where(c == 1, np.sin(angle), -np.sin(angle)))
    return (value * (p == p2)).reshape(256, 256)


def neighbour_sum():
    a = lax.broadcasted_iota(jnp.int32, (128, 128), 0)
    b = lax.broadcasted_iota(jnp.int32, (128, 128), 1)
    d = (a - b) & (PATCH - 1)
    near = (d <= 1) | (d == PATCH - 1)
    return (near & ((a & -PATCH) == (b & -PATCH))).astype(F32).astype(BF16)


def row_back():
    c2, r, c, i, k = np.meshgrid(
        np.arange(2), np.arange(HALF), np.arange(2), np.arange(2), np.arange(PATCH), indexing="ij"
    )
    u = r + HALF * (1 - i)
    angle = 2 * np.pi * k * u / PATCH
    value = np.where(c == c2, np.cos(angle), np.where(c2 == 0, -np.sin(angle), np.sin(angle))) * taper(u)
    return value.reshape(32, 128)


def col_back():
    j, p, l, q, p2, c = np.meshgrid(
        np.arange(3), np.arange(4), np.arange(PATCH), np.arange(2), np.arange(4), np.arange(PATCH), indexing="ij"
    )
    v = c + HALF - HALF * j
    angle = 2 * np.pi * l * v / PATCH
    value = np.where(q == 0, np.cos(angle), np.sin(angle)) * taper(v) * ((v >= 0) & (v < PATCH)) * (p == p2)
    return (value / (PATCH * PATCH)).reshape(384, 256)


def split(x):
    hi = x.astype(BF16)
    return hi, (x - hi.astype(F32)).astype(BF16)


def mm(a, b):
    return jnp.dot(a, b, preferred_element_type=F32)


def half_copies(stack_ref, first, out_ref, tile, sem, slot):
    count = out_ref.shape[0]
    return [
        pltpu.make_async_copy(
            stack_ref.at[first : first + count, comp, :, pl.ds(128 * (tile + t), 128)],
            out_ref.at[:, 2 * comp + t],
            sem.at[slot, 2 * comp + t],
        )
        for comp in range(2)
        for t in range(2)
    ]


def lower_lanes(shape):
    return lax.broadcasted_iota(jnp.int32, shape, len(shape) - 1) % 128 < 64


def mixed_tile(real, imag, right):
    turned = pltpu.roll(jnp.where(right, real, imag), 64, 1)
    return jnp.where(lower_lanes(real.shape) == right, turned, jnp.where(right, imag, real))


def half_pair(stack_ref, count, left_ref, right_ref, middle, sem):
    lanes = pl.ds(256, 128)
    copies = [pltpu.make_async_copy(stack_ref.at[:count, :, :, lanes], middle, sem.at[2, 0])]
    copies += half_copies(stack_ref, 0, left_ref, 0, sem, 0)
    copies += half_copies(stack_ref, 0, right_ref, 3, sem, 1)
    for copy in copies:
        copy.start()
    return copies


def half_pair_end(copies, count, left_ref, right_ref, middle):
    copies[0].wait()
    for acq in range(count):
        left_ref[acq, 4] = mixed_tile(middle[acq, 0], middle[acq, 1], False)
        right_ref[acq, 4] = mixed_tile(middle[acq, 0], middle[acq, 1], True)
    for copy in copies[1:]:
        copy.wait()


def odd_date():
    return lax.axis_index("date") % 2


def pack_kernel(stack_ref, out_ref, middle, sem):
    odd = odd_date()
    acqs = pl.ds(odd, SPAN)
    copies = [pltpu.make_async_copy(stack_ref.at[acqs, :, :, pl.ds(256, 128)], middle, sem.at[4])]
    for comp in range(2):
        for t in range(2):
            lanes = pl.ds(pl.multiple_of(128 * (3 * odd + t), 128), 128)
            at = 2 * comp + t
            copies.append(pltpu.make_async_copy(stack_ref.at[acqs, comp, :, lanes], out_ref.at[:, at], sem.at[at]))
    for copy in copies:
        copy.start()
    copies[0].wait()
    for acq in range(SPAN):
        out_ref[acq, 4] = mixed_tile(middle[acq, 0], middle[acq, 1], odd == 1)
    for copy in copies[1:]:
        copy.wait()


def pack(stack):
    return pl.pallas_call(
        pack_kernel,
        out_shape=pltpu.VMEM((SPAN, 5, 80, 128), F32),
        in_specs=[pl.BlockSpec(memory_space=pl.ANY)],
        out_specs=pl.BlockSpec(memory_space=pltpu.VMEM),
        scratch_shapes=[pltpu.VMEM((SPAN, 2, 80, 128), F32), pltpu.SemaphoreType.DMA((5,))],
        compiler_params=pltpu.CompilerParams(vmem_limit_bytes=60000000),
    )(stack)


def cross(a_ref, a, b_ref, b):
    real, imag = [0.0] * 3, [0.0] * 3
    for k in range(LOOK_R):
        rows = pl.ds(k, 16, stride=LOOK_R)
        x = [a_ref[a, t, rows, :] for t in range(5)]
        y = [b_ref[b, t, rows, :] for t in range(5)]
        for t in range(2):
            real[t] += x[t] * y[t] + x[t + 2] * y[t + 2]
            imag[t] += x[t + 2] * y[t] - x[t] * y[t + 2]
        real[2] += x[4] * y[4]
        imag[2] += x[4] * pltpu.roll(y[4], 64, 1)
    imag[2] = jnp.where(lower_lanes((16, 128)), -imag[2], imag[2])
    return jnp.concatenate(real, axis=1), jnp.concatenate(imag, axis=1)


def power(a_ref, a):
    total = [0.0] * 3
    for k in range(LOOK_R):
        x = [a_ref[a, t, pl.ds(k, 16, stride=LOOK_R), :] for t in range(5)]
        for t in range(2):
            total[t] += x[t] * x[t] + x[t + 2] * x[t + 2]
        total[2] += x[4] * x[4]
    return jnp.concatenate(total, axis=1)


def pooled(planes, table):
    high, low = split(jnp.concatenate(planes, axis=0))
    cells = (mm(high, table) + mm(low, table)) * (1.0 / (LOOK_R * LOOK_C))
    return cells.reshape(len(planes), 16, 256)


def pair_lanes():
    return lax.broadcasted_iota(jnp.int32, (16, 128), 1) // HALF


def message(cells, offset):
    group = pair_lanes()
    out = jnp.zeros((16, 128), F32)
    for p in range(PAIRS_DEV):
        for comp in range(2):
            value = cells[2 * p + comp, :, offset : offset + 128]
            out = jnp.where(group == comp * PAIRS_DEV + p, value, out)
    return out


def power_cells(left_cells, right_cells):
    return jnp.where(lower_lanes((16, 128)), left_cells[:, :128], right_cells[:, 128:])


def by_pair(values):
    group = pair_lanes() % PAIRS_DEV
    out = values[0]
    for p in range(1, PAIRS_DEV):
        out = jnp.where(group == p, values[p], out)
    return out


def pair_of(list_ref, group, p):
    return tuple(list_ref[i, PAIRS_DEV * group + p] - 4 * group for i in range(2))


def early_kernel(
    list_ref, stack_ref, left_ref, right_ref, first_ref, second_ref, back_ref, crossing_ref, index_ref, keep, look_out,
    powers, middle, sem,
):
    keep_l, keep_r = keep.at[0], keep.at[1]
    copies = half_pair(stack_ref, 4, keep_l, keep_r, middle, sem)
    table = look_table()
    look_out[...] = table
    date = lax.axis_index("date")
    odd = odd_date() == 1
    before = jnp.maximum(date - 1, 0)
    own = [pair_of(list_ref, date, p) for p in range(PAIRS_DEV)]
    others = [pair_of(list_ref, before, p) for p in range(PAIRS_DEV)]
    crossing_ref[...] = by_pair([jnp.full((16, 128), (b >= 4).astype(jnp.int32)) for a, b in own])
    lane = lax.broadcasted_iota(jnp.int32, (8, 128), 1)
    index = jnp.zeros((8, 128), jnp.int32)
    for p in range(PAIRS_DEV):
        mine = jnp.where(odd, own[p][0], jnp.clip(others[p][1] - 4, 0, 3))
        theirs = jnp.where(odd, jnp.clip(own[p][1] - 4, 0, 2), jnp.clip(others[p][0] - 1, 0, 2))
        index = jnp.where(lane == p, mine, jnp.where(lane == PAIRS_DEV + p, theirs, index))
    index_ref[...] = index
    half_pair_end(copies, 4, keep_l, keep_r, middle)
    planes_l, planes_r = [], []
    for a, b in own:
        planes_l += cross(keep_l, a, keep_l, jnp.minimum(b, 3))
        planes_r += cross(keep_r, a, keep_r, jnp.minimum(b, 3))
    for acq in range(4):
        planes_l.append(power(keep_l, acq))
        planes_r.append(power(keep_r, acq))
    cells_l = pooled(planes_l, table)
    cells_r = pooled(planes_r, table)
    left_ref[...] = message(cells_l, 0)
    right_ref[...] = message(cells_r, 128)
    for acq in range(4):
        powers[acq] = power_cells(cells_l[8 + acq], cells_r[8 + acq])
    first_ref[...] = by_pair([powers[a] for a, b in own])
    second_ref[...] = by_pair([powers[jnp.minimum(b, 3)] for a, b in own])
    back_ref[...] = by_pair([powers[jnp.clip(b - 4, 0, 3)] for a, b in others])


def early(listed, stack):
    vmem = pl.BlockSpec(memory_space=pltpu.VMEM)
    smem = pl.BlockSpec(memory_space=pltpu.SMEM)
    out_shape = [jax.ShapeDtypeStruct((16, 128), F32)] * 5 + [
        jax.ShapeDtypeStruct((16, 128), jnp.int32),
        jax.ShapeDtypeStruct((8, 128), jnp.int32),
        jax.ShapeDtypeStruct((2, 4, 5, 80, 128), F32),
        jax.ShapeDtypeStruct((384, 256), BF16),
    ]
    return pl.pallas_call(
        early_kernel,
        out_shape=out_shape,
        in_specs=[smem, pl.BlockSpec(memory_space=HBM)],
        out_specs=[vmem] * len(out_shape),
        scratch_shapes=[
            pltpu.VMEM((4, 16, 128), F32), pltpu.VMEM((4, 2, 80, 128), F32), pltpu.SemaphoreType.DMA((3, 4)),
        ],
        compiler_params=pltpu.CompilerParams(vmem_limit_bytes=24 * 2**20),
        cost_estimate=pl.CostEstimate(flops=10**9, bytes_accessed=10**7, transcendentals=0),
    )(listed, stack)


def chip_kernel(
    list_ref, other_ref, keep, table_ref, crossing_ref, left_in, right_in, second_in, left_ref, right_ref, second_ref,
    first_swap, second_swap, *scratch,
):
    left_ref[...] = left_in[...]
    right_ref[...] = right_in[...]
    second_ref[...] = second_in[...]

    @pl.when(odd_date() == 0)
    def _():
        other_l, other_r, powers, middle, sem = scratch
        copies = half_pair(other_ref, SPAN, other_l, other_r, middle, sem)
        half_pair_end(copies, SPAN, other_l, other_r, middle)
        date = lax.axis_index("date")
        planes_l, planes_r, seconds = [], [], []
        for p in range(PAIRS_DEV):
            a, b = pair_of(list_ref, date, p)
            seconds.append(jnp.maximum(b - 4, 0))
            planes_l += cross(keep.at[0], a, other_l, seconds[p])
            planes_r += cross(keep.at[1], a, other_r, seconds[p])
        for acq in range(SPAN):
            planes_l.append(power(other_l, acq))
            planes_r.append(power(other_r, acq))
        cells_l = pooled(planes_l, table_ref[...])
        cells_r = pooled(planes_r, table_ref[...])
        crossing = crossing_ref[...] == 1
        left_ref[...] = jnp.where(crossing, message(cells_l, 0), left_in[...])
        right_ref[...] = jnp.where(crossing, message(cells_r, 128), right_in[...])
        for acq in range(SPAN):
            powers[acq] = power_cells(cells_l[8 + acq], cells_r[8 + acq])
        second_ref[...] = jnp.where(crossing, by_pair([powers[b] for b in seconds]), second_in[...])

    odd_col = lax.axis_index("col") % 2 == 1
    left, right = left_ref[...], right_ref[...]
    first_swap[...] = jnp.where(odd_col, left, right)
    second_swap[...] = jnp.where(odd_col, right, left)


def within_chip(listed, other, *arrays):
    vmem = pl.BlockSpec(memory_space=pltpu.VMEM)
    half = pltpu.VMEM((SPAN, 5, 80, 128), F32)
    return pl.pallas_call(
        chip_kernel,
        out_shape=[jax.ShapeDtypeStruct((16, 128), F32)] * 5,
        in_specs=[pl.BlockSpec(memory_space=pltpu.SMEM), pl.BlockSpec(memory_space=HBM)] + [vmem] * 6,
        out_specs=[vmem] * 5,
        scratch_shapes=[
            half, half, pltpu.VMEM((SPAN, 16, 128), F32), pltpu.VMEM((SPAN, 2, 80, 128), F32),
            pltpu.SemaphoreType.DMA((3, 4)),
        ],
        compiler_params=pltpu.CompilerParams(vmem_limit_bytes=24 * 2**20),
        cost_estimate=pl.CostEstimate(flops=10**9, bytes_accessed=10**7, transcendentals=0),
    )(listed, other, *arrays)


def table_kernel(after_ref, trig_ref, ns_out, rf_out, cf_out, rb_out, cb_out):
    ns_out[...] = neighbour_sum()
    for source, target in (
        (trig_ref[:256], cf_out),
        (trig_ref[256:640], cb_out),
        (trig_ref[640:704, :96], rf_out),
        (trig_ref[640:672, 128:], rb_out),
    ):
        high, low = split(source)
        target[0] = high
        target[1] = low


def filter_tables(after):
    vmem = pl.BlockSpec(memory_space=pltpu.VMEM)
    trig = np.zeros((704, 256))
    trig[:256] = col_forward()
    trig[256:640] = col_back()
    trig[640:704, :96] = row_forward()
    trig[640:672, 128:] = row_back()
    out_shape = [jax.ShapeDtypeStruct((128, 128), BF16)] + [
        jax.ShapeDtypeStruct((2,) + shape, BF16) for shape in ((64, 96), (256, 256), (32, 128), (384, 256))
    ]
    return pl.pallas_call(
        table_kernel,
        out_shape=out_shape,
        in_specs=[vmem] * 2,
        out_specs=[vmem] * 5,
        compiler_params=pltpu.CompilerParams(vmem_limit_bytes=16 * 2**20),
        cost_estimate=pl.CostEstimate(flops=10**8, bytes_accessed=10**6, transcendentals=0),
    )(after, jnp.asarray(trig, F32))


def late_kernel(index_ref, other_ref, keep, table_ref, back_in, new_ref, out_ref):
    odd = odd_date() == 1
    side = jnp.where(odd, 0, 1)
    index = index_ref[...]
    planes = []
    for p in range(PAIRS_DEV):
        planes += cross(keep.at[side], index[0, p], other_ref, index[0, PAIRS_DEV + p])
    table = table_ref[:, pl.ds(pl.multiple_of(128 * side, 128), 128)]
    high, low = split(jnp.concatenate(planes, axis=0))
    cells = mm(high, table) + mm(low, table)
    new = message(cells.reshape(len(planes), 16, 128), 0) * (1.0 / (LOOK_R * LOOK_C))
    new = jnp.where(odd | lower_lanes((16, 128)), new, -new)
    new_ref[...] = new
    out_ref[:16] = new
    out_ref[16:] = back_in[...]


def late(*arrays):
    vmem = pl.BlockSpec(memory_space=pltpu.VMEM)
    return pl.pallas_call(
        late_kernel,
        out_shape=(jax.ShapeDtypeStruct((16, 128), F32), jax.ShapeDtypeStruct((32, 128), F32)),
        in_specs=[vmem] * 5,
        out_specs=(vmem, vmem),
        compiler_params=pltpu.CompilerParams(vmem_limit_bytes=24 * 2**20),
    )(*arrays)


def merge_kernel(
    crossing_ref, before_late, right_late, after_late, left_late, first_ref, second_ref, left_early, right_early, mid_ref
):
    crossing = (crossing_ref[...] == 1) & (odd_date() == 1)
    col = lax.axis_index("col")
    odd_col = col % 2 == 1
    before = jnp.where(crossing, before_late[:16], jnp.where(odd_col, first_ref[...], second_ref[...]))
    after = jnp.where(crossing, after_late[...], jnp.where(odd_col, second_ref[...], first_ref[...]))
    mid_ref[:, :128] = jnp.where(col == 0, 0.0, before)
    mid_ref[:, 128:256] = jnp.where(crossing, left_late[...], left_early[...])
    mid_ref[:, 256:384] = jnp.where(crossing, right_late[:16], right_early[...])
    mid_ref[:, 384:] = jnp.where(col == lax.axis_size("col") - 1, 0.0, after)


def merge(*arrays):
    vmem = pl.BlockSpec(memory_space=pltpu.VMEM)
    return pl.pallas_call(
        merge_kernel,
        out_shape=jax.ShapeDtypeStruct((16, 512), F32),
        in_specs=[vmem] * 9,
        out_specs=vmem,
        compiler_params=pltpu.CompilerParams(vmem_limit_bytes=8 * 2**20),
    )(*arrays)


def coherence_of(mid_ref, first, second, out_ref):
    lane = lax.broadcasted_iota(jnp.int32, (16, 128), 1)
    squares = []
    for at in (128, 256):
        x = mid_ref[:, at : at + 128]
        squares.append(x * x + pltpu.roll(x * x, 64, 1))
    magnitude = jnp.sqrt(jnp.where(lane < 64, squares[0], squares[1]))
    coherence = magnitude / jnp.sqrt((first + 1e-06) * (second + 1e-06))
    for p in range(PAIRS_DEV):
        left = coherence if p == 0 else pltpu.roll(coherence, 128 - HALF * p, 1)
        right = pltpu.roll(coherence, (HALF + 64 - HALF * p) % 128, 1)
        out_ref[p] = jnp.where(lane < HALF, left, right)[:, :PATCH]


def goldstein_kernel(
    first_swap, mid_ref, second_swap, ns_ref, rf_ref, cf_ref, rb_ref, cb_ref, crossing_ref, first_ref, second_ref, late_ref,
    out_ref, coh_ref,
):
    odd_crossing = (crossing_ref[...] == 1) & (odd_date() == 1)
    coherence_of(mid_ref, first_ref[...], jnp.where(odd_crossing, late_ref[16:], second_ref[...]), coh_ref)
    row = lax.axis_index("row")
    odd_row = row % 2 == 1
    up = jnp.where(odd_row, first_swap[...], second_swap[...])
    down = jnp.where(odd_row, second_swap[...], first_swap[...])
    up = jnp.where(row == 0, 0.0, up)
    down = jnp.where(row == lax.axis_size("row") - 1, 0.0, down)
    x = jnp.concatenate([up, mid_ref[...], down], axis=0)
    lane = lax.broadcasted_iota(jnp.int32, (48, 128), 1)
    sign = jnp.where(lane < 64, -1.0, 1.0)
    turned = [pltpu.roll(x[:, 128 * b : 128 * b + 128], 64, 1) * sign for b in range(4)]
    xx = jnp.concatenate([x, jnp.concatenate(turned, axis=1)], axis=0)
    xh, xl = split(xx)
    rh, rl = rf_ref[0], rf_ref[1]
    y = mm(jnp.concatenate([rh, rh], axis=1), jnp.concatenate([xh, xl], axis=0)) + mm(rl, xh)
    ys = jnp.concatenate([y[:, 128 * j : 128 * j + 256] for j in range(3)], axis=0)
    yh, yl = split(ys)
    ch, cl = cf_ref[0], cf_ref[1]
    z = mm(yh, ch) + (mm(yl, ch) + mm(yh, cl))
    zr, zi = z[:, :128], z[:, 128:]
    magnitude = jnp.sqrt(zr * zr + zi * zi)
    mh, ml = split(magnitude)
    across = mm(jnp.concatenate([mh, ml], axis=1), jnp.concatenate([ns_ref[...], ns_ref[...]], axis=0))
    grouped = across.reshape(6, PATCH, 128)
    down_one = jnp.concatenate([grouped[:, PATCH - 1 :], grouped[:, : PATCH - 1]], axis=1)
    up_one = jnp.concatenate([grouped[:, 1:], grouped[:, :1]], axis=1)
    smooth = (grouped + (down_one + up_one)).reshape(192, 128)
    response = jnp.sqrt(smooth * (1.0 / 9.0)) * (1.0 / PATCH)
    fr, fi = zr * response, zi * response
    w = jnp.concatenate(
        [
            jnp.concatenate([fr[64 * j : 64 * j + 64] for j in range(3)], axis=1),
            jnp.concatenate([fi[64 * j : 64 * j + 64] for j in range(3)], axis=1),
        ],
        axis=0,
    )
    wh, wl = split(w)
    bh, bl = rb_ref[0], rb_ref[1]
    t = mm(jnp.concatenate([bh, bh], axis=1), jnp.concatenate([wh, wl], axis=0)) + mm(bl, wh)
    th, tl = split(t)
    gh, gl = cb_ref[0], cb_ref[1]
    oo = mm(jnp.concatenate([th, tl], axis=0), gh)
    o = oo[:32] + (oo[32:] + mm(th, gl))
    real = o[:16, :128] - o[16:, 128:]
    imag = o[16:, :128] + o[:16, 128:]
    for p in range(PAIRS_DEV):
        out_ref[p, 0] = real[:, PATCH * p : PATCH * p + PATCH]
        out_ref[p, 1] = imag[:, PATCH * p : PATCH * p + PATCH]


def goldstein(*arrays):
    vmem = pl.BlockSpec(memory_space=pltpu.VMEM)
    return pl.pallas_call(
        goldstein_kernel,
        out_shape=(
            jax.ShapeDtypeStruct((PAIRS_DEV, 2, 16, 32), F32), jax.ShapeDtypeStruct((PAIRS_DEV, 16, 32), F32),
        ),
        in_specs=[vmem] * 12,
        out_specs=(vmem, vmem),
        compiler_params=pltpu.CompilerParams(vmem_limit_bytes=24 * 2**20),
    )(*arrays)


def neighbour(i, n, first):
    if first:
        return i ^ 1
    return ((i - 1) ^ 1) + 1 if 0 < i < n - 1 else i


def shards(stack, pair_list):
    names = ("date", "row", "col")
    dates, rows, cols = (lax.axis_size(name) for name in names)

    def send(x, target):
        pairs = []
        for d in range(dates):
            for r in range(rows):
                for c in range(cols):
                    a, b, e = target(d, r, c)
                    pairs.append(((d * rows + r) * cols + c, (a * rows + b) * cols + e))
        return lax.ppermute(x, names, pairs)

    def swap_cols(first):
        def target(d, r, c):
            e = neighbour(c, cols, first)
            return (d, r, e) if e != c else (d ^ 1, r, c)

        return target

    def swap_rows(first):
        def target(d, r, c):
            b = neighbour(r, rows, first)
            return (d, b, c) if b != r else (d ^ 1, r, c)

        return target

    def between_dates(odd_target, even_target):
        def target(d, r, c):
            if d in (0, dates - 1):
                return d, r, c ^ 1
            if d % 2:
                up, e = odd_target(c)
                return d + up, r, e
            down, e = even_target(c)
            return d - down, r, e

        return target

    end = cols - 1
    straight = between_dates(lambda c: (1, c), lambda c: (1, c))
    def ring(d, r, c):
        if d % 2:
            return (d, r, c - 1) if c > 0 else (d - 1, r, c)
        return (d, r, c + 1) if c < end else (d + 1, r, c)

    from_left = between_dates(
        lambda c: (0, 0) if c == 1 else (1, c),
        lambda c: (1, c + 1) if c < end else (0, 1),
    )

    listed = pair_list.T
    other = send(pack(stack), straight)
    chip = send(stack, lambda d, r, c: (d ^ 1, r, c))
    left, right, first, second, back, crossing, index, keep, look = early(listed, stack)
    left, right, second, one, two = within_chip(listed, chip, keep, look, crossing, left, right, second)
    one = send(one, swap_cols(True))
    two = send(two, swap_cols(False))
    tables = filter_tables(right)
    other, one, two = lax.optimization_barrier((other, one, two))
    new, with_powers = late(index, other, keep, look, back)
    after = send(new, ring)
    before = send(with_powers, from_left)
    right_late = send(with_powers, straight)
    mid = merge(crossing, before, right_late, after, new, one, two, left, right)
    one = send(mid, swap_rows(True))
    two = send(mid, swap_rows(False))
    return goldstein(one, mid, two, *tables, crossing, first, second, right_late)


def solution(mesh):
    in_specs = (P("date", None, "row", "col"), P())
    out_specs = (P("date", None, "row", "col"), P("date", "row", "col"))
    return jax.shard_map(shards, mesh=mesh, in_specs=in_specs, out_specs=out_specs, check_vma=False)
```

```python
import functools
import math

import jax
import jax.numpy as jnp
import numpy as np
from jax import lax
from jax.experimental import pallas as pl
from jax.experimental.pallas import tpu as pltpu
from jax.sharding import PartitionSpec as P

SPAN = 3
LOOK_R = 5
LOOK_C = 20
PATCH = 32
HALF = PATCH // 2
PAIRS_DEV = 4
F32 = jnp.float32
BF16 = jnp.bfloat16
HBM = pltpu.MemorySpace.HBM


def taper(v):
    return np.where(v < HALF, (v + 0.5) / HALF, (PATCH - 0.5 - v) / HALF)


def whole_part(x, divisor):
    return (x.astype(F32) * (1.0 / divisor) + 0.5 / divisor).astype(jnp.int32)


def look_table():
    lane = lax.broadcasted_iota(jnp.int32, (384, 256), 0)
    n = lax.broadcasted_iota(jnp.int32, (384, 256), 1)
    left = jnp.where(lane < 256, lane, 256 + lane % 64)
    right = jnp.where(lane < 256, 64 + lane, lane % 64)
    cell = whole_part(jnp.where(n < 128, left, right), LOOK_C)
    return (cell == n % HALF).astype(F32).astype(BF16)


def row_forward():
    i, k, q, row = np.meshgrid(np.arange(2), np.arange(PATCH), np.arange(2), np.arange(48), indexing="ij")
    u = row - HALF * i
    angle = 2 * np.pi * k * u / PATCH
    value = np.where(q == 0, np.cos(angle), -np.sin(angle)) * ((u >= 0) & (u < PATCH))
    return value.reshape(64, 96)


def col_forward():
    h, c, p, v, c2, p2, l = np.meshgrid(
        np.arange(2), np.arange(2), np.arange(4), np.arange(HALF), np.arange(2), np.arange(4), np.arange(PATCH),
        indexing="ij",
    )
    angle = 2 * np.pi * l * (HALF * h + v) / PATCH
    value = np.where(c == c2, np.cos(angle), np.where(c == 1, np.sin(angle), -np.sin(angle)))
    return (value * (p == p2)).reshape(256, 256)


def neighbour_sum():
    a = lax.broadcasted_iota(jnp.int32, (128, 128), 0)
    b = lax.broadcasted_iota(jnp.int32, (128, 128), 1)
    d = (a - b) & (PATCH - 1)
    near = (d <= 1) | (d == PATCH - 1)
    return (near & ((a & -PATCH) == (b & -PATCH))).astype(F32).astype(BF16)


def row_back():
    c2, r, c, i, k = np.meshgrid(
        np.arange(2), np.arange(HALF), np.arange(2), np.arange(2), np.arange(PATCH), indexing="ij"
    )
    u = r + HALF * (1 - i)
    angle = 2 * np.pi * k * u / PATCH
    value = np.where(c == c2, np.cos(angle), np.where(c2 == 0, -np.sin(angle), np.sin(angle))) * taper(u)
    return value.reshape(32, 128)


def col_back():
    j, p, l, q, p2, c = np.meshgrid(
        np.arange(3), np.arange(4), np.arange(PATCH), np.arange(2), np.arange(4), np.arange(PATCH), indexing="ij"
    )
    v = c + HALF - HALF * j
    angle = 2 * np.pi * l * v / PATCH
    value = np.where(q == 0, np.cos(angle), np.sin(angle)) * taper(v) * ((v >= 0) & (v < PATCH)) * (p == p2)
    return (value / (PATCH * PATCH)).reshape(384, 256)


def split(x):
    hi = x.astype(BF16)
    return hi, (x - hi.astype(F32)).astype(BF16)


def mm(a, b):
    return jnp.dot(a, b, preferred_element_type=F32)


def half_copies(stack_ref, first, out_ref, tile, sem, slot):
    count = out_ref.shape[0]
    return [
        pltpu.make_async_copy(
            stack_ref.at[first : first + count, comp, :, pl.ds(128 * (tile + t), 128)],
            out_ref.at[:, 2 * comp + t],
            sem.at[slot, 2 * comp + t],
        )
        for comp in range(2)
        for t in range(2)
    ]


def lower_lanes(shape):
    return lax.broadcasted_iota(jnp.int32, shape, len(shape) - 1) % 128 < 64


def mixed_tile(real, imag, right):
    turned = pltpu.roll(jnp.where(right, real, imag), 64, 1)
    return jnp.where(lower_lanes(real.shape) == right, turned, jnp.where(right, imag, real))


def half_pair(stack_ref, count, left_ref, right_ref, middle, sem):
    lanes = pl.ds(256, 128)
    copies = [pltpu.make_async_copy(stack_ref.at[:count, :, :, lanes], middle, sem.at[2, 0])]
    copies += half_copies(stack_ref, 0, left_ref, 0, sem, 0)
    copies += half_copies(stack_ref, 0, right_ref, 3, sem, 1)
    for copy in copies:
        copy.start()
    return copies


def half_pair_end(copies, count, left_ref, right_ref, middle):
    copies[0].wait()
    for acq in range(count):
        left_ref[acq, 4] = mixed_tile(middle[acq, 0], middle[acq, 1], False)
        right_ref[acq, 4] = mixed_tile(middle[acq, 0], middle[acq, 1], True)
    for copy in copies[1:]:
        copy.wait()


def odd_date():
    return lax.axis_index("date") % 2


def pack_kernel(stack_ref, out_ref, middle, sem):
    odd = odd_date()
    acqs = pl.ds(odd, SPAN)
    copies = [pltpu.make_async_copy(stack_ref.at[acqs, :, :, pl.ds(256, 128)], middle, sem.at[4])]
    for comp in range(2):
        for t in range(2):
            lanes = pl.ds(pl.multiple_of(128 * (3 * odd + t), 128), 128)
            at = 2 * comp + t
            copies.append(pltpu.make_async_copy(stack_ref.at[acqs, comp, :, lanes], out_ref.at[:, at], sem.at[at]))
    for copy in copies:
        copy.start()
    copies[0].wait()
    for acq in range(SPAN):
        out_ref[acq, 4] = mixed_tile(middle[acq, 0], middle[acq, 1], odd == 1)
    for copy in copies[1:]:
        copy.wait()


def pack(stack):
    return pl.pallas_call(
        pack_kernel,
        out_shape=pltpu.VMEM((SPAN, 5, 80, 128), F32),
        in_specs=[pl.BlockSpec(memory_space=pl.ANY)],
        out_specs=pl.BlockSpec(memory_space=pltpu.VMEM),
        scratch_shapes=[pltpu.VMEM((SPAN, 2, 80, 128), F32), pltpu.SemaphoreType.DMA((5,))],
        compiler_params=pltpu.CompilerParams(vmem_limit_bytes=60000000),
    )(stack)


def cross(a_ref, a, b_ref, b):
    real, imag = [0.0] * 3, [0.0] * 3
    for k in range(LOOK_R):
        rows = pl.ds(k, 16, stride=LOOK_R)
        x = [a_ref[a, t, rows, :] for t in range(5)]
        y = [b_ref[b, t, rows, :] for t in range(5)]
        for t in range(2):
            real[t] += x[t] * y[t] + x[t + 2] * y[t + 2]
            imag[t] += x[t + 2] * y[t] - x[t] * y[t + 2]
        real[2] += x[4] * y[4]
        imag[2] += x[4] * pltpu.roll(y[4], 64, 1)
    imag[2] = jnp.where(lower_lanes((16, 128)), -imag[2], imag[2])
    return jnp.concatenate(real, axis=1), jnp.concatenate(imag, axis=1)


def power(a_ref, a):
    total = [0.0] * 3
    for k in range(LOOK_R):
        x = [a_ref[a, t, pl.ds(k, 16, stride=LOOK_R), :] for t in range(5)]
        for t in range(2):
            total[t] += x[t] * x[t] + x[t + 2] * x[t + 2]
        total[2] += x[4] * x[4]
    return jnp.concatenate(total, axis=1)


def pooled(planes, table):
    high, low = split(jnp.concatenate(planes, axis=0))
    cells = (mm(high, table) + mm(low, table)) * (1.0 / (LOOK_R * LOOK_C))
    return cells.reshape(len(planes), 16, 256)


def pair_lanes():
    return lax.broadcasted_iota(jnp.int32, (16, 128), 1) // HALF


def message(cells, offset):
    group = pair_lanes()
    out = jnp.zeros((16, 128), F32)
    for p in range(PAIRS_DEV):
        for comp in range(2):
            value = cells[2 * p + comp, :, offset : offset + 128]
            out = jnp.where(group == comp * PAIRS_DEV + p, value, out)
    return out


def power_cells(left_cells, right_cells):
    return jnp.where(lower_lanes((16, 128)), left_cells[:, :128], right_cells[:, 128:])


def by_pair(values):
    group = pair_lanes() % PAIRS_DEV
    out = values[0]
    for p in range(1, PAIRS_DEV):
        out = jnp.where(group == p, values[p], out)
    return out


def pair_of(list_ref, group, p):
    return tuple(list_ref[i, PAIRS_DEV * group + p] - 4 * group for i in range(2))


def early_kernel(
    list_ref, stack_ref, left_ref, right_ref, first_ref, second_ref, back_ref, crossing_ref, index_ref, keep, look_out,
    mine_ref, powers, middle, sem,
):
    keep_l, keep_r = keep.at[0], keep.at[1]
    copies = half_pair(stack_ref, 4, keep_l, keep_r, middle, sem)
    table = look_table()
    look_out[...] = table
    date = lax.axis_index("date")
    odd = odd_date() == 1
    before = jnp.maximum(date - 1, 0)
    own = [pair_of(list_ref, date, p) for p in range(PAIRS_DEV)]
    others = [pair_of(list_ref, before, p) for p in range(PAIRS_DEV)]
    crossing_ref[...] = by_pair([jnp.full((16, 128), (b >= 4).astype(jnp.int32)) for a, b in own])
    lane = lax.broadcasted_iota(jnp.int32, (8, 128), 1)
    index = jnp.zeros((8, 128), jnp.int32)
    mines = []
    for p in range(PAIRS_DEV):
        mines.append(jnp.where(odd, own[p][0], jnp.clip(others[p][1] - 4, 0, 3)))
        theirs = jnp.where(odd, jnp.clip(own[p][1] - 4, 0, 2), jnp.clip(others[p][0] - 1, 0, 2))
        index = jnp.where(lane == p, theirs, index)
    index_ref[...] = index
    half_pair_end(copies, 4, keep_l, keep_r, middle)
    for p in range(PAIRS_DEV):
        mine_ref[p] = keep[jnp.where(odd, 0, 1), mines[p]]
    planes_l, planes_r = [], []
    for a, b in own:
        planes_l += cross(keep_l, a, keep_l, jnp.minimum(b, 3))
        planes_r += cross(keep_r, a, keep_r, jnp.minimum(b, 3))
    for acq in range(4):
        planes_l.append(power(keep_l, acq))
        planes_r.append(power(keep_r, acq))
    cells_l = pooled(planes_l, table)
    cells_r = pooled(planes_r, table)
    left_ref[...] = message(cells_l, 0)
    right_ref[...] = message(cells_r, 128)
    for acq in range(4):
        powers[acq] = power_cells(cells_l[8 + acq], cells_r[8 + acq])
    first_ref[...] = by_pair([powers[a] for a, b in own])
    second_ref[...] = by_pair([powers[jnp.minimum(b, 3)] for a, b in own])
    back_ref[...] = by_pair([powers[jnp.clip(b - 4, 0, 3)] for a, b in others])


def early(listed, stack):
    vmem = pl.BlockSpec(memory_space=pltpu.VMEM)
    smem = pl.BlockSpec(memory_space=pltpu.SMEM)
    out_shape = [jax.ShapeDtypeStruct((16, 128), F32)] * 5 + [
        jax.ShapeDtypeStruct((16, 128), jnp.int32),
        jax.ShapeDtypeStruct((8, 128), jnp.int32),
        jax.ShapeDtypeStruct((2, 4, 5, 80, 128), F32),
        jax.ShapeDtypeStruct((384, 256), BF16),
        jax.ShapeDtypeStruct((PAIRS_DEV, 5, 80, 128), F32),
    ]
    return pl.pallas_call(
        early_kernel,
        out_shape=out_shape,
        in_specs=[smem, pl.BlockSpec(memory_space=HBM)],
        out_specs=[vmem] * len(out_shape),
        scratch_shapes=[
            pltpu.VMEM((4, 16, 128), F32), pltpu.VMEM((4, 2, 80, 128), F32), pltpu.SemaphoreType.DMA((3, 4)),
        ],
        compiler_params=pltpu.CompilerParams(vmem_limit_bytes=24 * 2**20),
        cost_estimate=pl.CostEstimate(flops=10**9, bytes_accessed=10**7, transcendentals=0),
    )(listed, stack)


def chip_kernel(
    list_ref, other_ref, keep, table_ref, crossing_ref, left_in, right_in, second_in, left_ref, right_ref, second_ref,
    first_swap, second_swap, *scratch,
):
    left_ref[...] = left_in[...]
    right_ref[...] = right_in[...]
    second_ref[...] = second_in[...]

    @pl.when(odd_date() == 0)
    def _():
        other_l, other_r, powers, middle, sem = scratch
        copies = half_pair(other_ref, SPAN, other_l, other_r, middle, sem)
        half_pair_end(copies, SPAN, other_l, other_r, middle)
        date = lax.axis_index("date")
        planes_l, planes_r, seconds = [], [], []
        for p in range(PAIRS_DEV):
            a, b = pair_of(list_ref, date, p)
            seconds.append(jnp.maximum(b - 4, 0))
            planes_l += cross(keep.at[0], a, other_l, seconds[p])
            planes_r += cross(keep.at[1], a, other_r, seconds[p])
        for acq in range(SPAN):
            planes_l.append(power(other_l, acq))
            planes_r.append(power(other_r, acq))
        cells_l = pooled(planes_l, table_ref[...])
        cells_r = pooled(planes_r, table_ref[...])
        crossing = crossing_ref[...] == 1
        left_ref[...] = jnp.where(crossing, message(cells_l, 0), left_in[...])
        right_ref[...] = jnp.where(crossing, message(cells_r, 128), right_in[...])
        for acq in range(SPAN):
            powers[acq] = power_cells(cells_l[8 + acq], cells_r[8 + acq])
        second_ref[...] = jnp.where(crossing, by_pair([powers[b] for b in seconds]), second_in[...])

    odd_col = lax.axis_index("col") % 2 == 1
    left, right = left_ref[...], right_ref[...]
    first_swap[...] = jnp.where(odd_col, left, right)
    second_swap[...] = jnp.where(odd_col, right, left)


def within_chip(listed, other, *arrays):
    vmem = pl.BlockSpec(memory_space=pltpu.VMEM)
    half = pltpu.VMEM((SPAN, 5, 80, 128), F32)
    return pl.pallas_call(
        chip_kernel,
        out_shape=[jax.ShapeDtypeStruct((16, 128), F32)] * 5,
        in_specs=[pl.BlockSpec(memory_space=pltpu.SMEM), pl.BlockSpec(memory_space=HBM)] + [vmem] * 6,
        out_specs=[vmem] * 5,
        scratch_shapes=[
            half, half, pltpu.VMEM((SPAN, 16, 128), F32), pltpu.VMEM((SPAN, 2, 80, 128), F32),
            pltpu.SemaphoreType.DMA((3, 4)),
        ],
        compiler_params=pltpu.CompilerParams(vmem_limit_bytes=24 * 2**20),
        cost_estimate=pl.CostEstimate(flops=10**9, bytes_accessed=10**7, transcendentals=0),
    )(listed, other, *arrays)


def table_kernel(after_ref, trig_ref, ns_out, rf_out, cf_out, rb_out, cb_out):
    ns_out[...] = neighbour_sum()
    for source, target in (
        (trig_ref[:256], cf_out),
        (trig_ref[256:640], cb_out),
        (trig_ref[640:704, :96], rf_out),
        (trig_ref[640:672, 128:], rb_out),
    ):
        high, low = split(source)
        target[0] = high
        target[1] = low


def filter_tables(after):
    vmem = pl.BlockSpec(memory_space=pltpu.VMEM)
    trig = np.zeros((704, 256))
    trig[:256] = col_forward()
    trig[256:640] = col_back()
    trig[640:704, :96] = row_forward()
    trig[640:672, 128:] = row_back()
    out_shape = [jax.ShapeDtypeStruct((128, 128), BF16)] + [
        jax.ShapeDtypeStruct((2,) + shape, BF16) for shape in ((64, 96), (256, 256), (32, 128), (384, 256))
    ]
    return pl.pallas_call(
        table_kernel,
        out_shape=out_shape,
        in_specs=[vmem] * 2,
        out_specs=[vmem] * 5,
        compiler_params=pltpu.CompilerParams(vmem_limit_bytes=16 * 2**20),
        cost_estimate=pl.CostEstimate(flops=10**8, bytes_accessed=10**6, transcendentals=0),
    )(after, jnp.asarray(trig, F32))


def late_kernel(index_ref, other_ref, mine_ref, table_ref, back_in, new_ref, out_ref):
    odd = odd_date() == 1
    side = jnp.where(odd, 0, 1)
    index = index_ref[...]
    planes = []
    for p in range(PAIRS_DEV):
        planes += cross(mine_ref, p, other_ref, index[0, p])
    table = table_ref[:, pl.ds(pl.multiple_of(128 * side, 128), 128)]
    high, low = split(jnp.concatenate(planes, axis=0))
    cells = mm(high, table) + mm(low, table)
    new = message(cells.reshape(len(planes), 16, 128), 0) * (1.0 / (LOOK_R * LOOK_C))
    new = jnp.where(odd | lower_lanes((16, 128)), new, -new)
    new_ref[...] = new
    out_ref[:16] = new
    out_ref[16:] = back_in[...]


def late(*arrays):
    vmem = pl.BlockSpec(memory_space=pltpu.VMEM)
    return pl.pallas_call(
        late_kernel,
        out_shape=(jax.ShapeDtypeStruct((16, 128), F32), jax.ShapeDtypeStruct((32, 128), F32)),
        in_specs=[vmem] * 5,
        out_specs=(vmem, vmem),
        compiler_params=pltpu.CompilerParams(vmem_limit_bytes=24 * 2**20),
    )(*arrays)


def merge_kernel(
    crossing_ref, before_late, right_late, after_late, left_late, first_ref, second_ref, left_early, right_early, mid_ref
):
    crossing = (crossing_ref[...] == 1) & (odd_date() == 1)
    col = lax.axis_index("col")
    odd_col = col % 2 == 1
    before = jnp.where(crossing, before_late[:16], jnp.where(odd_col, first_ref[...], second_ref[...]))
    after = jnp.where(crossing, after_late[...], jnp.where(odd_col, second_ref[...], first_ref[...]))
    mid_ref[:, :128] = jnp.where(col == 0, 0.0, before)
    mid_ref[:, 128:256] = jnp.where(crossing, left_late[...], left_early[...])
    mid_ref[:, 256:384] = jnp.where(crossing, right_late[:16], right_early[...])
    mid_ref[:, 384:] = jnp.where(col == lax.axis_size("col") - 1, 0.0, after)


def merge(*arrays):
    vmem = pl.BlockSpec(memory_space=pltpu.VMEM)
    return pl.pallas_call(
        merge_kernel,
        out_shape=jax.ShapeDtypeStruct((16, 512), F32),
        in_specs=[vmem] * 9,
        out_specs=vmem,
        compiler_params=pltpu.CompilerParams(vmem_limit_bytes=8 * 2**20),
    )(*arrays)


def coherence_of(mid_ref, first, second, out_ref):
    lane = lax.broadcasted_iota(jnp.int32, (16, 128), 1)
    squares = []
    for at in (128, 256):
        x = mid_ref[:, at : at + 128]
        squares.append(x * x + pltpu.roll(x * x, 64, 1))
    magnitude = jnp.sqrt(jnp.where(lane < 64, squares[0], squares[1]))
    coherence = magnitude / jnp.sqrt((first + 1e-06) * (second + 1e-06))
    for p in range(PAIRS_DEV):
        left = coherence if p == 0 else pltpu.roll(coherence, 128 - HALF * p, 1)
        right = pltpu.roll(coherence, (HALF + 64 - HALF * p) % 128, 1)
        out_ref[p] = jnp.where(lane < HALF, left, right)[:, :PATCH]


def goldstein_kernel(
    first_swap, mid_ref, second_swap, ns_ref, rf_ref, cf_ref, rb_ref, cb_ref, crossing_ref, first_ref, second_ref, late_ref,
    out_ref, coh_ref,
):
    odd_crossing = (crossing_ref[...] == 1) & (odd_date() == 1)
    coherence_of(mid_ref, first_ref[...], jnp.where(odd_crossing, late_ref[16:], second_ref[...]), coh_ref)
    row = lax.axis_index("row")
    odd_row = row % 2 == 1
    up = jnp.where(odd_row, first_swap[...], second_swap[...])
    down = jnp.where(odd_row, second_swap[...], first_swap[...])
    up = jnp.where(row == 0, 0.0, up)
    down = jnp.where(row == lax.axis_size("row") - 1, 0.0, down)
    x = jnp.concatenate([up, mid_ref[...], down], axis=0)
    lane = lax.broadcasted_iota(jnp.int32, (48, 128), 1)
    sign = jnp.where(lane < 64, -1.0, 1.0)
    turned = [pltpu.roll(x[:, 128 * b : 128 * b + 128], 64, 1) * sign for b in range(4)]
    xx = jnp.concatenate([x, jnp.concatenate(turned, axis=1)], axis=0)
    xh, xl = split(xx)
    rh, rl = rf_ref[0], rf_ref[1]
    y = mm(jnp.concatenate([rh, rh], axis=1), jnp.concatenate([xh, xl], axis=0)) + mm(rl, xh)
    ys = jnp.concatenate([y[:, 128 * j : 128 * j + 256] for j in range(3)], axis=0)
    yh, yl = split(ys)
    ch, cl = cf_ref[0], cf_ref[1]
    z = mm(yh, ch) + (mm(yl, ch) + mm(yh, cl))
    zr, zi = z[:, :128], z[:, 128:]
    magnitude = jnp.sqrt(zr * zr + zi * zi)
    mh, ml = split(magnitude)
    across = mm(jnp.concatenate([mh, ml], axis=1), jnp.concatenate([ns_ref[...], ns_ref[...]], axis=0))
    grouped = across.reshape(6, PATCH, 128)
    down_one = jnp.concatenate([grouped[:, PATCH - 1 :], grouped[:, : PATCH - 1]], axis=1)
    up_one = jnp.concatenate([grouped[:, 1:], grouped[:, :1]], axis=1)
    smooth = (grouped + (down_one + up_one)).reshape(192, 128)
    response = jnp.sqrt(smooth * (1.0 / 9.0)) * (1.0 / PATCH)
    fr, fi = zr * response, zi * response
    w = jnp.concatenate(
        [
            jnp.concatenate([fr[64 * j : 64 * j + 64] for j in range(3)], axis=1),
            jnp.concatenate([fi[64 * j : 64 * j + 64] for j in range(3)], axis=1),
        ],
        axis=0,
    )
    wh, wl = split(w)
    bh, bl = rb_ref[0], rb_ref[1]
    t = mm(jnp.concatenate([bh, bh], axis=1), jnp.concatenate([wh, wl], axis=0)) + mm(bl, wh)
    th, tl = split(t)
    gh, gl = cb_ref[0], cb_ref[1]
    oo = mm(jnp.concatenate([th, tl], axis=0), gh)
    o = oo[:32] + (oo[32:] + mm(th, gl))
    real = o[:16, :128] - o[16:, 128:]
    imag = o[16:, :128] + o[:16, 128:]
    for p in range(PAIRS_DEV):
        out_ref[p, 0] = real[:, PATCH * p : PATCH * p + PATCH]
        out_ref[p, 1] = imag[:, PATCH * p : PATCH * p + PATCH]


def goldstein(*arrays):
    vmem = pl.BlockSpec(memory_space=pltpu.VMEM)
    return pl.pallas_call(
        goldstein_kernel,
        out_shape=(
            jax.ShapeDtypeStruct((PAIRS_DEV, 2, 16, 32), F32), jax.ShapeDtypeStruct((PAIRS_DEV, 16, 32), F32),
        ),
        in_specs=[vmem] * 12,
        out_specs=(vmem, vmem),
        compiler_params=pltpu.CompilerParams(vmem_limit_bytes=24 * 2**20),
    )(*arrays)


def neighbour(i, n, first):
    if first:
        return i ^ 1
    return ((i - 1) ^ 1) + 1 if 0 < i < n - 1 else i


def shards(stack, pair_list):
    names = ("date", "row", "col")
    dates, rows, cols = (lax.axis_size(name) for name in names)

    def send(x, target):
        pairs = []
        for d in range(dates):
            for r in range(rows):
                for c in range(cols):
                    a, b, e = target(d, r, c)
                    pairs.append(((d * rows + r) * cols + c, (a * rows + b) * cols + e))
        return lax.ppermute(x, names, pairs)

    def swap_cols(first):
        def target(d, r, c):
            e = neighbour(c, cols, first)
            return (d, r, e) if e != c else (d ^ 1, r, c)

        return target

    def swap_rows(first):
        def target(d, r, c):
            b = neighbour(r, rows, first)
            return (d, b, c) if b != r else (d ^ 1, r, c)

        return target

    def between_dates(odd_target, even_target):
        def target(d, r, c):
            if d in (0, dates - 1):
                return d, r, c ^ 1
            if d % 2:
                up, e = odd_target(c)
                return d + up, r, e
            down, e = even_target(c)
            return d - down, r, e

        return target

    end = cols - 1
    straight = between_dates(lambda c: (1, c), lambda c: (1, c))
    def ring(d, r, c):
        if d % 2:
            return (d, r, c - 1) if c > 0 else (d - 1, r, c)
        return (d, r, c + 1) if c < end else (d + 1, r, c)

    from_left = between_dates(
        lambda c: (0, 0) if c == 1 else (1, c),
        lambda c: (1, c + 1) if c < end else (0, 1),
    )

    listed = pair_list.T
    other = send(pack(stack), straight)
    chip = send(stack, lambda d, r, c: (d ^ 1, r, c))
    left, right, first, second, back, crossing, index, keep, look, mine = early(listed, stack)
    left, right, second, one, two = within_chip(listed, chip, keep, look, crossing, left, right, second)
    one = send(one, swap_cols(True))
    two = send(two, swap_cols(False))
    tables = filter_tables(right)
    other, one, two = lax.optimization_barrier((other, one, two))
    new, with_powers = late(index, other, mine, look, back)
    after = send(new, ring)
    before = send(with_powers, from_left)
    right_late = send(with_powers, straight)
    mid = merge(crossing, before, right_late, after, new, one, two, left, right)
    one = send(mid, swap_rows(True))
    two = send(mid, swap_rows(False))
    return goldstein(one, mid, two, *tables, crossing, first, second, right_late)


def solution(mesh):
    in_specs = (P("date", None, "row", "col"), P())
    out_specs = (P("date", None, "row", "col"), P("date", "row", "col"))
    return jax.shard_map(shards, mesh=mesh, in_specs=in_specs, out_specs=out_specs, check_vma=False)
```
